32 devices in a mesh: tile: 8 (over z, y), sub: 4 (over x, core).
Axes of the slice: x: 2, y: 2, z: 4, core: 2. Of those that a mesh axis runs over, the one named last changes fastest.
Arguments:
- offsets: float32 [3, 32, 16, 1024], P(None, None, 'tile', 'sub'), may hold values from 0 to 1
- velocity: float32 [3, 32, 16, 1024], P(None, None, 'tile', 'sub'), may hold values from -1.5 to 1.5
- mass: float32 [32, 16, 1024], P(None, 'tile', 'sub'), may hold values from 0.015625 to 0.0625
- entropy: float32 [32, 16, 1024], P(None, 'tile', 'sub'), may hold values from 0.5 to 2
- active_counts: int32 [3, 16, 1024], P(None, 'tile', 'sub'), may hold values from 0 to 32, as said below
- targets: int32 [32, 16, 1024], P(None, 'tile', 'sub'), may hold values from 0 to 3, as said below
Outputs:
- arrived: float32 [8, 786432], P(None, ('tile', 'sub'))
The draws below stay inside these ranges and needn't reach their ends.
Inputs may be any that keep to these rules, and one draw needn't show every extreme that they name: active_counts[0] is a cell's number of occupied slots, from 16 to 32; counts never rise from one level to the next; active_counts[1] is at most 16 and active_counts[2] at most 8, and these bounds and 32 are each reached in some cell. Active particles of a substep are the cell's first slots. `targets`: among one device's 16384 particles, no destination is named by more than 6144 of them, and one destination is named by exactly 6144.
All inputs are finite; a program needn't handle non-finite values.
Results may differ from the reference program's by a relative error of at most 0.0001.
Values sent between devices are 32-bit elements; how exact they have to be, the bound alone decides.
No kernel may reach another device: no remote copies, remote signals or barrier semaphores. Data moves between devices by JAX's collectives and lax.ppermute only.
A program may use at most 128 MiB of HBM per device.

```python
import math
import jax
import jax.numpy as jnp
from jax import lax

S = 32
LEVELS = 3
TX = 2
SY = 256
GX = 16
GY = 1024
CAP = 6144


def draw_active_counts(key, part):
    tile_count = GX // TX
    subkeys = jax.random.split(jax.random.fold_in(key, 11), 3)
    occupied = jax.random.randint(subkeys[0], (GX, GY), S // 2, S + 1)
    level_draw = jax.random.randint(subkeys[1], (tile_count,), 0, 4)
    tile_weight = jnp.where(level_draw == 3, 8, 1)
    row_weight = jnp.repeat(tile_weight, TX)[:, None]
    middle = jnp.minimum(occupied * row_weight // 16, S // 2)
    finest = jnp.minimum(middle * row_weight // 16, S // 4)
    chosen_cell = jax.random.randint(subkeys[2], (), 0, GX * GY)
    cell_ids = jnp.arange(GX * GY).reshape(GX, GY)
    picked = cell_ids == chosen_cell
    occupied = jnp.where(picked, S, occupied)
    middle = jnp.where(picked, S // 2, middle)
    finest = jnp.where(picked, S // 4, finest)
    return jnp.stack([occupied, middle, finest]).astype(jnp.int32)


def draw_targets(key, part):
    tile_count = GX // TX
    sub_count = GY // SY
    per_device = S * TX * SY
    capacity = 3 * per_device // 8

    def device_labels(device):
        device_key = jax.random.fold_in(jax.random.fold_in(key, 7), device)
        subkeys = jax.random.split(device_key, 4)
        ordering = jax.random.permutation(subkeys[0], sub_count)
        second_load = jax.random.randint(subkeys[1], (), per_device // 4, capacity + 1)
        coin_flip = jax.random.randint(subkeys[2], (per_device,), 0, 2)
        position = jnp.arange(per_device)
        labels = jnp.where(position < capacity, ordering[0], jnp.where(position < capacity + second_load, ordering[1], jnp.where(coin_flip == 0, ordering[2], ordering[3])))
        return jax.random.permutation(subkeys[3], labels)
    blocks = jax.vmap(device_labels)(jnp.arange(tile_count * sub_count))
    blocks = blocks.reshape(tile_count, sub_count, S, TX, SY)
    return jnp.transpose(blocks, (2, 0, 3, 1, 4)).reshape(S, GX, GY).astype(jnp.int32)


def levels(own_key, shape, cuts, least, top_value):
    factor_of, own = 1.0, jax.random.fold_in(own_key, 6)
    for axis_at, blocks in cuts:
        draws = jnp.exp(jax.random.uniform(jax.random.fold_in(own, axis_at), (blocks,), jnp.float32, least / len(cuts), top_value / len(cuts)))
        factor_of = factor_of * jnp.repeat(draws, shape[axis_at] // blocks).reshape([-1 if axis == axis_at else 1 for axis in range(len(shape))])
    return factor_of


def normal_values(stream_key, shape, deviation, reach, cuts=(), kind=jnp.bfloat16):
    factor_of = levels(stream_key, shape, cuts, -0.22, 0.18) if cuts else 1.0
    entries = jax.random.normal(stream_key, shape, jnp.float32) * deviation * factor_of
    return jnp.minimum(jnp.maximum(entries, -reach), reach).astype(kind)


def setup_inputs(seed: int = 0) -> dict:
    key_of = jax.random.split(jax.random.key(seed), 7)
    return {
        "offsets": jnp.clip(1.0 * jax.random.uniform(key_of[0], (3, S, GX, GY), jnp.float32) ** levels(key_of[0], (3, S, GX, GY), ((2, 8), (3, 4)), -0.2, 0.2), 0.0, 1.0),
        "velocity": normal_values(key_of[1], (3, S, GX, GY), 0.3, 1.5, ((2, 8), (3, 4)), jnp.float32),
        "mass": jnp.clip(jnp.exp(math.log(0.0625) - 1.3862944 * jax.random.uniform(key_of[2], (S, GX, GY), jnp.float32) ** levels(key_of[2], (S, GX, GY), ((1, 8), (2, 4)), -0.2, 0.2)), 0.015625, 0.0625),
        "entropy": jnp.clip(jnp.exp(math.log(2.0) - 1.3862944 * jax.random.uniform(key_of[3], (S, GX, GY), jnp.float32) ** levels(key_of[3], (S, GX, GY), ((1, 8), (2, 4)), -0.2, 0.2)), 0.5, 2.0),
        "active_counts": draw_active_counts(jax.random.fold_in(key_of[6], 71), 0),
        "targets": draw_targets(jax.random.fold_in(key_of[6], 71), 0),
    }


KERNEL_NORM = 21.0 / (2.0 * math.pi)
GAMMA = 5.0 / 3.0
VISC_ALPHA = 1.0
VISC_BETA = 2.0
TIME_STEP = 0.05
SOFTEN = 0.01

def separation(local_part, theirs, shift_x, shift_y):
    delta_x = local_part[0][:, None] - theirs[0][None, :] - shift_x
    delta_y = local_part[1][:, None] - theirs[1][None, :] - shift_y
    delta_z = local_part[2][:, None] - theirs[2][None, :]
    return (delta_x, delta_y, delta_z)

def density_pair(local_part, theirs, shift_x, shift_y):
    delta_x, delta_y, delta_z = separation(local_part, theirs, shift_x, shift_y)
    squared = delta_x * delta_x + delta_y * delta_y + delta_z * delta_z
    radius = jnp.sqrt(squared)
    remain = jnp.maximum(1.0 - radius, 0.0)
    weight = KERNEL_NORM * remain ** 4 * (1.0 + 4.0 * radius)
    return lax.optimization_barrier(jnp.sum(theirs[6][None, :] * weight, axis=1))

def force_pair(local_part, theirs, own_pressure, their_pressure, shift_x, shift_y):
    delta_x, delta_y, delta_z = separation(local_part, theirs, shift_x, shift_y)
    squared = delta_x * delta_x + delta_y * delta_y + delta_z * delta_z
    radius = jnp.sqrt(squared)
    remain = jnp.maximum(1.0 - radius, 0.0)
    relative_x = local_part[3][:, None] - theirs[3][None, :]
    relative_y = local_part[4][:, None] - theirs[4][None, :]
    relative_z = local_part[5][:, None] - theirs[5][None, :]
    approach = delta_x * relative_x + delta_y * relative_y + delta_z * relative_z
    closing = jnp.minimum(approach, 0.0) / (squared + SOFTEN)
    sound_mean = 0.5 * (own_pressure[1][:, None] + their_pressure[1][None, :])
    mean_density = 0.5 * (own_pressure[2][:, None] + their_pressure[2][None, :])
    viscous = (-VISC_ALPHA * sound_mean * closing + VISC_BETA * closing * closing) / mean_density
    strength = theirs[6][None, :] * (own_pressure[0][:, None] + their_pressure[0][None, :] + viscous)
    strength = strength * (20.0 * KERNEL_NORM) * remain ** 3
    return jnp.stack([lax.optimization_barrier(jnp.sum(strength * delta_x, axis=1)), lax.optimization_barrier(jnp.sum(strength * delta_y, axis=1)), lax.optimization_barrier(jnp.sum(strength * delta_z, axis=1))])

def pressure_terms(density, entropy, occupied):
    density_used = jnp.where(occupied, density, 1.0)
    return jnp.stack([entropy * density_used ** (GAMMA - 2.0), jnp.sqrt(GAMMA * entropy * density_used ** (GAMMA - 1.0)), density_used])

def wrap_rows(field):
    return jnp.concatenate([field[:, :, -1:], field, field[:, :, :1]], axis=2)

def density_all(motion):
    padded = wrap_rows(motion)

    def one_row(row_index):
        window = lax.dynamic_slice_in_dim(padded, row_index, 3, 2)
        local_part = window[:, :, 1]
        summed = jnp.zeros(local_part.shape[1:], jnp.float32)
        for shift_x in (-1, 0, 1):
            for shift_y in (-1, 0, 1):
                theirs = jnp.roll(window[:, :, 1 + shift_x], -shift_y, axis=2)
                summed = summed + density_pair(local_part, theirs, float(shift_x), float(shift_y))
        return summed
    rows = lax.map(one_row, jnp.arange(GX, dtype=jnp.int32))
    return jnp.transpose(rows, (1, 0, 2))

def force_all(motion, pressure):
    padded = wrap_rows(motion)
    padded_pressure = wrap_rows(pressure)

    def one_row(row_index):
        window = lax.dynamic_slice_in_dim(padded, row_index, 3, 2)
        window_pressure = lax.dynamic_slice_in_dim(padded_pressure, row_index, 3, 2)
        local_part = window[:, :, 1]
        own_pressure = window_pressure[:, :, 1]
        summed = jnp.zeros((3,) + local_part.shape[1:], jnp.float32)
        for shift_x in (-1, 0, 1):
            for shift_y in (-1, 0, 1):
                theirs = jnp.roll(window[:, :, 1 + shift_x], -shift_y, axis=2)
                their_pressure = jnp.roll(window_pressure[:, :, 1 + shift_x], -shift_y, axis=2)
                summed = summed + force_pair(local_part, theirs, own_pressure, their_pressure, float(shift_x), float(shift_y))
        return summed
    rows = lax.map(one_row, jnp.arange(GX, dtype=jnp.int32))
    return jnp.transpose(rows, (1, 2, 0, 3))

def reference(offsets, velocity, mass, entropy, active_counts, targets):
    slot_index = lax.broadcasted_iota(jnp.int32, (S, GX, GY), 0)
    occupied = slot_index < active_counts[0][None]
    mass_live = jnp.where(occupied, mass, 0.0)
    places = offsets
    speeds = velocity
    density = jnp.ones((S, GX, GY), jnp.float32)
    for substep in range(LEVELS):
        active = slot_index < active_counts[substep][None]
        motion = jnp.concatenate([places, speeds, mass_live[None]], axis=0)
        fresh_density = density_all(motion)
        density = jnp.where(active, fresh_density, density)
        pressure = pressure_terms(density, entropy, occupied)
        acceleration = force_all(motion, pressure)
        speeds = jnp.where(active[None], speeds + TIME_STEP * acceleration, speeds)
        places = jnp.where(active[None], places + TIME_STEP * speeds, places)
    particle_state = jnp.concatenate([places, speeds, density[None], mass_live[None]], axis=0)
    tile_count = GX // TX
    sub_count = GY // SY
    per_device = S * TX * SY
    particle_state = particle_state.reshape(8, S, tile_count, TX, sub_count, SY)
    particle_state = jnp.transpose(particle_state, (0, 2, 4, 1, 3, 5)).reshape(8, tile_count, sub_count, per_device)
    destination = targets.reshape(S, tile_count, TX, sub_count, SY)
    destination = jnp.transpose(destination, (1, 3, 0, 2, 4)).reshape(tile_count, sub_count, per_device)
    choices_of = jnp.arange(sub_count, dtype=jnp.int32)
    onehot = (destination[:, :, None, :] == choices_of[None, None, :, None]).astype(jnp.int32)
    rank_in = lax.optimization_barrier(jnp.sum((jnp.cumsum(onehot, axis=3) - 1) * onehot, axis=2))
    tile_ids = jnp.arange(tile_count, dtype=jnp.int32)[:, None, None]
    source_ids = jnp.arange(sub_count, dtype=jnp.int32)[None, :, None]
    flat_slot = ((tile_ids * sub_count + destination) * sub_count + source_ids) * CAP + rank_in
    arrived = jnp.zeros((8, tile_count * sub_count * sub_count * CAP), jnp.float32)
    arrived = arrived.at[:, flat_slot.reshape(-1)].set(particle_state.reshape(8, -1))
    return arrived
```

```python
import functools
import math

import jax
import jax.numpy as jnp
from jax import lax
from jax.experimental import pallas as pl
from jax.experimental.pallas import tpu as pltpu
from jax.sharding import PartitionSpec as P

KERNEL_NORM = 21.0 / (2.0 * math.pi)
GAMMA = 5.0 / 3.0
TIME_STEP = 0.05
SOFTEN = 0.01
LANES = 128
ROWS = 8
VMEM = pl.BlockSpec(memory_space=pltpu.VMEM)
SMEM = pl.BlockSpec(memory_space=pltpu.SMEM)
PARAMS = pltpu.CompilerParams(vmem_limit_bytes=40 << 20)
MOTION, PRESSURE = 7, 3
SHIFTS = (-1, 0, 1)


def lane_of(shape):
    return lax.broadcasted_iota(jnp.int32, shape, 1)


def cost(pairs, ops):
    return pl.CostEstimate(flops=int(pairs * ops), bytes_accessed=1 << 20, transcendentals=0)


def pair_force(own, their, total):
    xi, yi, zi, ui, vi, wi, qi, ci, ri = own
    xj, yj, zj, uj, vj, wj, qj, cj, rj, mj = their
    dx, dy, dz = xi - xj, yi - yj, zi - zj
    squared = dx * dx + dy * dy + dz * dz
    radius = squared * lax.rsqrt(jnp.maximum(squared, 1e-30))
    remain = jnp.maximum(1.0 - radius, 0.0)
    approach = dx * (ui - uj) + dy * (vi - vj) + dz * (wi - wj)
    closing = jnp.minimum(approach, 0.0) * pl.reciprocal(squared + SOFTEN, approx=True)
    viscous = closing * (closing - (ci + cj)) * pl.reciprocal(ri + rj, approx=True)
    strength = (qi + qj + viscous) * ((remain * remain) * (remain * mj))
    return (total[0] + strength * dx, total[1] + strength * dy, total[2] + strength * dz)


def pair_density(own, their, total):
    xi, yi, zi = own
    xj, yj, zj, mj = their
    dx, dy, dz = xi - xj, yi - yj, zi - zj
    squared = dx * dx + dy * dy + dz * dz
    radius = squared * lax.rsqrt(jnp.maximum(squared, 1e-30))
    remain = jnp.maximum(1.0 - radius, 0.0)
    square = remain * remain
    return (total[0] + (square * square) * ((5.0 - 4.0 * remain) * mj),)


DENSITY = ((0, 1.0), (1, 1.0), (2, 1.0)), (), ((6, KERNEL_NORM),), pair_density, 1
FORCE = (
    tuple((c, 1.0) for c in range(3)) + tuple((c, 4.0) for c in range(3, 6)),
    ((0, 1.0), (1, 1.0), (2, 4.0)),
    ((6, 20.0 * KERNEL_NORM),),
    pair_force,
    3,
)


def store_shifted(shifted, col, row, lo, hi, blocks, left, right, is_y):
    lane = lane_of(blocks[0].shape)
    up = [pltpu.roll(v, 1, 1) for v in [left] + blocks]
    down = [pltpu.roll(v, LANES - 1, 1) for v in blocks + [right]]
    for b, block in enumerate(blocks):
        before = jnp.where(lane == 0, up[b], up[b + 1])
        after = jnp.where(lane == LANES - 1, down[b + 1], down[b])
        for s, value in zip(SHIFTS, (before, block, after)):
            if is_y and s:
                value = value + float(s)
            shifted[col, s + 1, b, row, lo:hi, :] = value


def fill_shifted(shifted, col, row, pieces, field, scale, group):
    for cells, left, right, lo, hi in pieces:
        count = cells.shape[-1] // LANES
        blocks = [cells[field, lo:hi, b * LANES : (b + 1) * LANES] for b in range(count)]
        left_end = pltpu.roll(left[lo:hi, :], LANES - 1 - group, 1)
        right_end = right[lo:hi, :]
        if group:
            right_end = pltpu.roll(right_end, LANES - group, 1)
        if scale != 1.0:
            blocks = [v * scale for v in blocks]
            left_end, right_end = left_end * scale, right_end * scale
        store_shifted(shifted, col, row, lo, hi, blocks, left_end, right_end, field == 1 and scale == 1.0 and row == 1)


def fill_column(shifted, col, kind, motion, pressure, group_of):
    moved, pressed, massed, _, _ = kind
    row = 0
    for pieces, fields, width in ((motion, moved, MOTION), (pressure, pressed, PRESSURE), (motion, massed, MOTION)):
        for field, scale in fields:
            fill_shifted(shifted, col, row, pieces(field), field, scale, group_of(field))
            row += 1


def add_pairs(kind, motion_ref, pressure_ref, shifted, x, sources, limit, first, last, fold):
    moved, pressed, _, pair, width = kind
    slots = shifted.shape[-2]
    blocks = shifted.shape[2]
    rows = shifted.shape[3]
    group = min(limit // ROWS, 2 if width == 3 else 4)
    unroll = 4 if group > 1 else 8
    low_col, low_shift = sources[0]

    def lane_block(b, carry):
        lanes = pl.ds(pl.multiple_of(b * LANES, LANES), LANES)
        for part in range(limit // (ROWS * group)):
            spans = [slice((part * group + v) * ROWS, (part * group + v + 1) * ROWS) for v in range(group)]
            own = []
            for span in spans:
                values = [motion_ref[x, f, span, lanes] * s if s != 1.0 else motion_ref[x, f, span, lanes] for f, s in moved]
                values += [pressure_ref[x, f, span, lanes] * s if s != 1.0 else pressure_ref[x, f, span, lanes] for f, s in pressed]
                own.append(values)

            def source(at, totals):
                col = at // 3
                shift = at - 3 * col
                offset = (col + low_shift).astype(jnp.float32)
                mine = [[v[0] - offset] + v[1:] for v in own]

                def step(outer, totals):
                    totals = list(totals)
                    for inner in range(unroll):
                        slot = outer * unroll + inner
                        their = [
                            jnp.broadcast_to(shifted[col + low_col, shift, b, r, pl.ds(slot, 1), :], (ROWS, LANES))
                            for r in range(rows)
                        ]
                        for v in range(group):
                            totals[v] = pair(mine[v], their, totals[v])
                    return tuple(totals)

                return lax.fori_loop(0, slots // unroll, step, totals)

            totals = tuple(first(x, span, lanes) for span in spans)
            totals = lax.fori_loop(0, 3 * len(sources), source, totals)
            for span, total in zip(spans, totals):
                last(x, span, lanes, total)
        return carry

    lax.fori_loop(0, blocks, lane_block, 0)


def own_sources(x, columns):
    return [(c, c - x) for c in range(columns) if abs(c - x) <= 1]


def pack_ends(field_of, fields, columns, left_ref, right_ref):
    for ref, at_last in ((left_ref, False), (right_ref, True)):
        lane = None
        packed = None
        for group in range(fields * columns):
            block = field_of(group // columns, group % columns, at_last)
            if lane is None:
                lane = lane_of(block.shape)
                packed = jnp.zeros(block.shape, jnp.float32)
            turn = (group + 1) % LANES if at_last else group
            packed = jnp.where(lane == group, pltpu.roll(block, turn, 1) if turn else block, packed)
        ref[...] = packed


def end_block(ref, column, field, at_last, limit):
    width = ref.shape[-1]
    lanes = slice(width - LANES, width) if at_last else slice(0, LANES)
    return ref[column, field, :limit, lanes]


def first_ends(motion):
    columns, _, slots, _ = motion.shape

    def kernel(motion_ref, left_ref, right_ref):
        pack_ends(
            lambda f, c, last: end_block(motion_ref, c, f, last, slots), MOTION, columns, left_ref, right_ref
        )

    ends = jax.ShapeDtypeStruct((slots, LANES), jnp.float32)
    return pl.pallas_call(kernel, out_shape=(ends, ends), in_specs=[VMEM], out_specs=(VMEM, VMEM), compiler_params=PARAMS)(motion)


def bounds_of(arrays, axis):
    spans, lo = [], 0
    for index, array in enumerate(arrays):
        hi = array.shape[axis]
        if hi > lo:
            spans.append((index, lo, hi))
            lo = hi
    return spans


def own_part(kind, motion, pressure, ends_m, ends_p, limit):
    columns, _, slots, width = motion.shape
    moved, pressed, massed, _, outs = kind
    flat_m = [e for pair in ends_m for e in pair]
    flat_p = [e for pair in ends_p for e in pair]
    spans_m = bounds_of([e[0] for e in ends_m], 0)
    spans_p = bounds_of([e[0] for e in ends_p], 0)
    inputs = [motion] + ([pressure] if pressed else []) + flat_m + flat_p
    rows = len(moved) + len(pressed) + len(massed)

    def kernel(*refs):
        refs = list(refs)
        motion_ref = refs.pop(0)
        pressure_ref = refs.pop(0) if pressed else None
        m_refs = refs[: len(flat_m)]
        p_refs = refs[len(flat_m) : len(flat_m) + len(flat_p)]
        out_ref, shifted = refs[-2:]
        for c in range(columns):

            def motion_pieces(field):
                spans = spans_m if field < 6 else [(len(ends_m) - 1, 0, slots)]
                return [(motion_ref.at[c], m_refs[2 * i], m_refs[2 * i + 1], lo, hi) for i, lo, hi in spans]

            def pressure_pieces(field):
                return [(pressure_ref.at[c], p_refs[2 * i], p_refs[2 * i + 1], lo, hi) for i, lo, hi in spans_p]

            fill_column(shifted, c, kind, motion_pieces, pressure_pieces, lambda f: f * columns + c)
        zero = jnp.zeros((ROWS, LANES), jnp.float32)

        def last(x, span, lanes, total):
            for k in range(outs):
                out_ref[x, k, span, lanes] = total[k]

        for x in range(columns):
            add_pairs(kind, motion_ref, pressure_ref, shifted, x, own_sources(x, columns), limit, lambda *_: (zero,) * outs, last, None)

    return pl.pallas_call(
        kernel,
        out_shape=jax.ShapeDtypeStruct((columns, outs, limit, width), jnp.float32),
        in_specs=[VMEM] * len(inputs),
        out_specs=VMEM,
        scratch_shapes=[pltpu.VMEM((columns, 3, width // LANES, rows, slots, LANES), jnp.float32)],
        compiler_params=PARAMS,
        cost_estimate=cost(limit * slots * 3 * (3 * columns - 2) * width, 60 if outs == 3 else 30),
    )(*inputs)


def halo_sums(kind, refs, columns, slots, counts, limit, out_first, out_last, motion_ref, pressure_ref, shifted):
    moved, pressed, massed, _, outs = kind
    for side in range(2):
        m_refs, p_refs = refs[side]
        column = columns - 1 if side == 0 else 0
        spans_m = bounds_of(m_refs, 1)
        spans_p = bounds_of(p_refs, 1)

        def pieces(history, spans):
            out = []
            for i, lo, hi in spans:
                ref = history[i]
                plane = ref.shape[0] - 1
                out.append((ref, ref.at[plane, :, 0:LANES], ref.at[plane, :, LANES : 2 * LANES], lo, hi))
            return out

        def motion_pieces(field):
            return pieces(m_refs, spans_m if field < 6 else [(len(m_refs) - 1, 0, slots)])

        fill_column(shifted, side, kind, motion_pieces, lambda f: pieces(p_refs, spans_p), lambda f: f * columns + column)
        x, shift = (0, -1) if side == 0 else (columns - 1, 1)
        add_pairs(kind, motion_ref, pressure_ref, shifted, x, [(side, shift)], limit, out_first[side], out_last[side], None)


def density_rest(motion, partial, messages, density, entropy, counts, level, limit, slots_sent):
    columns, _, slots, width = motion.shape
    (m_left, m_right) = messages
    first = density is None
    inputs = [motion, partial, entropy, counts] + ([] if first else [density]) + m_left + m_right
    n_in, n_m = len(inputs), len(m_left)
    rows = 4

    def kernel(*refs):
        motion_ref, partial_ref, entropy_ref, counts_ref = refs[:4]
        old_ref = None if first else refs[4]
        m_refs = refs[n_in - 2 * n_m : n_in]
        press_ref, left_ref, right_ref, shifted, sums = refs[n_in:]
        sums[...] = partial_ref[...]

        def start(x, span, lanes):
            return (sums[x, 0, span, lanes],)

        def end(x, span, lanes, total):
            sums[x, 0, span, lanes] = total[0]

        halo_sums(
            DENSITY, ((m_refs[:n_m], ()), (m_refs[n_m:], ())), columns, slots, counts_ref, limit,
            (start, start), (end, end), motion_ref, None, shifted,
        )
        for x in range(columns):
            count = counts_ref[level, x : x + 1, :]
            for lo in range(0, slots, ROWS):
                span = slice(lo, lo + ROWS)
                if lo >= limit:
                    if first:
                        value = jnp.ones((ROWS, width), jnp.float32)
                    else:
                        for f in range(3):
                            press_ref[x, f, span, :] = old_ref[x, f, span, :]
                        continue
                else:
                    slot = lax.broadcasted_iota(jnp.int32, (ROWS, width), 0) + lo
                    before = jnp.ones((ROWS, width), jnp.float32) if first else old_ref[x, 2, span, :]
                    value = jnp.where(slot < count, sums[x, 0, span, :], before)
                pressure = entropy_ref[x, span, :] * jnp.exp(jnp.log(value) * (GAMMA - 2.0))
                press_ref[x, 0, span, :] = pressure
                press_ref[x, 1, span, :] = jnp.sqrt(GAMMA * pressure * value)
                press_ref[x, 2, span, :] = value
        pack_ends(lambda f, c, last: end_block(press_ref, c, f, last, slots_sent), PRESSURE, columns, left_ref, right_ref)

    ends = jax.ShapeDtypeStruct((slots_sent, LANES), jnp.float32)
    return pl.pallas_call(
        kernel,
        out_shape=(jax.ShapeDtypeStruct((columns, PRESSURE, slots, width), jnp.float32), ends, ends),
        in_specs=[VMEM] * n_in,
        out_specs=(VMEM,) * 3,
        scratch_shapes=[
            pltpu.VMEM((2, 3, width // LANES, rows, slots, LANES), jnp.float32),
            pltpu.VMEM((columns, 1, limit, width), jnp.float32),
        ],
        compiler_params=PARAMS,
        cost_estimate=cost(limit * slots * 6 * width, 30),
    )(*inputs)


def force_rest(motion, pressure, partial, messages_m, messages_p, counts, level, limit, slots_sent):
    columns, _, slots, width = motion.shape
    n_m, n_p = len(messages_m[0]), len(messages_p[0])
    inputs = [motion, pressure, partial, counts] + messages_m[0] + messages_p[0] + messages_m[1] + messages_p[1]
    n_in = len(inputs)
    rows = 10
    ends = jax.ShapeDtypeStruct((slots_sent, LANES), jnp.float32)
    outs = (jax.ShapeDtypeStruct(motion.shape, jnp.float32),) + ((ends, ends) if slots_sent else ())

    def kernel(*refs):
        motion_ref, pressure_ref, partial_ref, counts_ref = refs[:4]
        sides = []
        for side in range(2):
            at = 4 + side * (n_m + n_p)
            sides.append((refs[at : at + n_m], refs[at + n_m : at + n_m + n_p]))
        new_ref = refs[n_in]
        shifted, sums = refs[-2:]
        sums[...] = partial_ref[...]

        def start(x, span, lanes):
            return tuple(sums[x, k, span, lanes] for k in range(3))

        def end(x, span, lanes, total):
            for k in range(3):
                sums[x, k, span, lanes] = total[k]

        halo_sums(FORCE, sides, columns, slots, counts_ref, limit, (start, start), (end, end), motion_ref, pressure_ref, shifted)
        for x in range(columns):
            count = counts_ref[level, x : x + 1, :]
            new_ref[x, 6, :, :] = motion_ref[x, 6, :, :]
            if limit < slots:
                for f in range(6):
                    new_ref[x, f, limit:, :] = motion_ref[x, f, limit:, :]
            for lo in range(0, limit, ROWS):
                span = slice(lo, lo + ROWS)
                active = lax.broadcasted_iota(jnp.int32, (ROWS, width), 0) + lo < count
                for k in range(3):
                    place, speed = motion_ref[x, k, span, :], motion_ref[x, 3 + k, span, :]
                    faster = speed + TIME_STEP * sums[x, k, span, :]
                    new_ref[x, 3 + k, span, :] = jnp.where(active, faster, speed)
                    new_ref[x, k, span, :] = jnp.where(active, place + TIME_STEP * faster, place)
        if slots_sent:
            left_ref, right_ref = refs[n_in + 1 : n_in + 3]
            pack_ends(lambda f, c, last: end_block(new_ref, c, f, last, slots_sent), 6, columns, left_ref, right_ref)

    made = pl.pallas_call(
        kernel,
        out_shape=outs,
        in_specs=[VMEM] * n_in,
        out_specs=(VMEM,) * len(outs),
        scratch_shapes=[
            pltpu.VMEM((2, 3, width // LANES, rows, slots, LANES), jnp.float32),
            pltpu.VMEM((columns, 3, limit, width), jnp.float32),
        ],
        compiler_params=PARAMS,
        cost_estimate=cost(limit * slots * 6 * width, 60),
    )(*inputs)
    return made if slots_sent else (made[0], None, None)


def ranks(destination, parts):
    rows, width = destination.shape

    def kernel(dest_ref, place_ref, meta_ref):
        dest = dest_ref[...]
        low = lax.broadcasted_iota(jnp.int32, (width, width), 0)
        upto = jnp.where(low <= lane_of((width, width)), 1.0, 0.0).astype(jnp.bfloat16)
        above = lax.broadcasted_iota(jnp.int32, (rows, rows), 0) > lane_of((rows, rows))
        above = jnp.where(above, 1.0, 0.0).astype(jnp.bfloat16)
        lane = lane_of((rows, LANES))
        meta = jnp.zeros((rows, LANES), jnp.float32)
        place = jnp.zeros((rows, width), jnp.float32)
        start = jnp.zeros((rows, 1), jnp.float32)
        for d in range(parts):
            mask = jnp.where(dest == d, 1.0, 0.0)
            inside = jnp.dot(mask.astype(jnp.bfloat16), upto, preferred_element_type=jnp.float32)
            count = inside[:, width - 1 : width]
            wide = jnp.broadcast_to(count, (rows, LANES))
            before = jnp.dot(above, wide.astype(jnp.bfloat16), preferred_element_type=jnp.float32)
            place = place + mask * (inside - 1.0 + start)
            meta = jnp.where(lane == d, before, meta)
            meta = jnp.where(lane == parts + d, jnp.broadcast_to(start, (rows, LANES)), meta)
            meta = jnp.where(lane == 2 * parts + d, before + wide, meta)
            start = start + count
        place_ref[...] = place.astype(jnp.int32)
        meta_ref[...] = meta.astype(jnp.int32)

    return pl.pallas_call(
        kernel,
        out_shape=(jax.ShapeDtypeStruct((rows, width), jnp.int32), jax.ShapeDtypeStruct((rows, LANES), jnp.int32)),
        in_specs=[VMEM],
        out_specs=(VMEM, VMEM),
        compiler_params=PARAMS,
    )(destination)


def compact(motion, pressure, place, meta, parts, capacity):
    columns, _, slots, width = motion.shape
    chunks = width // LANES
    total = -(-capacity // LANES)

    def kernel(motion_ref, pressure_ref, place_ref, meta_ref, out_ref, local, lists):
        lane = lane_of((ROWS, LANES))

        def do_group(group, carry):
            span = pl.ds(pl.multiple_of(group * ROWS, ROWS), ROWS)
            fields = [
                [motion_ref[x, f, span, :] for f in range(6)] + [pressure_ref[x, 2, span, :], motion_ref[x, 6, span, :]]
                for x in range(columns)
            ]
            for s in range(ROWS):
                for x in range(columns):
                    state = jnp.concatenate([v[s : s + 1, :] for v in fields[x]], axis=0)
                    high = state.astype(jnp.bfloat16).astype(jnp.float32)
                    rest = state - high
                    middle = rest.astype(jnp.bfloat16).astype(jnp.float32)
                    lowest = rest - middle
                    stacked = jnp.concatenate([high, middle, lowest], axis=0).astype(jnp.bfloat16)
                    row = (group * ROWS + s) * columns + x
                    wanted = place_ref[pl.ds(row, 1), :]
                    hot = jnp.where(lax.broadcasted_iota(jnp.int32, (width, width), 0) == wanted, 1.0, 0.0)
                    moved = lax.dot_general(
                        stacked, hot.astype(jnp.bfloat16), (((1,), (1,)), ((), ())), preferred_element_type=jnp.float32
                    )
                    moved = moved[0:8] + moved[8:16] + moved[16:24]
                    buffer = (s * columns + x) % 4
                    for c in range(chunks):
                        local[buffer, c + 1] = moved[:, c * LANES : (c + 1) * LANES]
                    for d in range(parts):
                        base = meta_ref[row, d]
                        begin = meta_ref[row, parts + d]
                        chunk = lax.shift_right_logical(base, 7)
                        off = lax.bitwise_and(base, LANES - 1)
                        turn = lax.bitwise_and(off - begin, LANES - 1)
                        at = lax.shift_right_logical(begin, 7)
                        at = at + jnp.where(off < lax.bitwise_and(begin, LANES - 1), 1, 0)
                        turned = [pltpu.roll(local[buffer, at + k], turn, 1) for k in range(chunks + 2)]
                        for k in range(chunks + 1):
                            value = jnp.where(lane >= turn, turned[k + 1], turned[k])
                            if k == 0:
                                value = jnp.where(lane >= off, value, lists[d, chunk])
                            lists[d, chunk + k] = value
            return carry

        lax.fori_loop(0, slots // ROWS, do_group, 0)
        for d in range(parts):
            count = meta_ref[slots * columns - 1, 2 * parts + d]
            for c in range(total):
                out_ref[d, :, c * LANES : (c + 1) * LANES] = jnp.where(lane + c * LANES < count, lists[d, c], 0.0)

    return pl.pallas_call(
        kernel,
        out_shape=jax.ShapeDtypeStruct((parts, 8, capacity), jnp.float32),
        in_specs=[VMEM, VMEM, VMEM, SMEM],
        out_specs=VMEM,
        scratch_shapes=[
            pltpu.VMEM((4, 2 * chunks + 4, ROWS, LANES), jnp.float32),
            pltpu.VMEM((parts, total + chunks + 2, ROWS, LANES), jnp.float32),
        ],
        compiler_params=PARAMS,
    )(motion, pressure, place, meta)


def pass_on(value, axis, step):
    count = lax.axis_size(axis)
    return lax.ppermute(value, axis, [(i, (i + step) % count) for i in range(count)])


def swap_ends(left_ends, right_ends):
    return pass_on(right_ends, "sub", 1), pass_on(left_ends, "sub", -1)


def swap_columns(cells, fields, limit, ends):
    width = cells.shape[-1]
    plane = jnp.concatenate(ends, axis=1)
    plane = jnp.pad(plane, ((0, 0), (0, width - plane.shape[1])))[None]
    first = jnp.concatenate([cells[0, :fields, :limit], plane], axis=0)
    final = jnp.concatenate([cells[-1, :fields, :limit], plane], axis=0)
    return pass_on(final, "tile", 1), pass_on(first, "tile", -1)


def shards(offsets, velocity, mass, entropy, active_counts, targets):
    slots, columns, width = mass.shape
    levels = active_counts.shape[0]
    parts = lax.axis_size("sub")
    slot_index = lax.broadcasted_iota(jnp.int32, mass.shape, 0)
    mass_live = jnp.where(slot_index < active_counts[0][None], mass, 0.0)
    motion = jnp.concatenate([offsets, velocity, mass_live[None]], axis=0).transpose(2, 0, 1, 3)
    entropy = entropy.transpose(1, 0, 2)
    limits = (slots, slots // 2, slots // 4)
    pressure = None
    ends_m, ends_p = [], []
    left_m, right_m, left_p, right_p = [], [], [], []
    made = first_ends(motion)
    place, meta = ranks(targets.reshape(slots * columns, width), parts)
    for level in range(levels):
        limit = limits[level]
        sent = limits[max(level - 1, 0)]
        fields = MOTION if level == 0 else 6
        ends_m.insert(0, swap_ends(*made))
        from_left, from_right = swap_columns(motion, fields, sent, ends_m[0])
        left_m.insert(0, from_left)
        right_m.insert(0, from_right)
        partial = own_part(DENSITY, motion, None, ends_m, [], limit)
        pressure, *made = density_rest(motion, partial, (left_m, right_m), pressure, entropy, active_counts, level, limit, limit)
        ends_p.insert(0, swap_ends(*made))
        from_left, from_right = swap_columns(pressure, PRESSURE, limit, ends_p[0])
        left_p.insert(0, from_left)
        right_p.insert(0, from_right)
        partial = own_part(FORCE, motion, pressure, ends_m, ends_p, limit)
        more = limit if level < levels - 1 else 0
        motion, *made = force_rest(
            motion, pressure, partial, (left_m, right_m), (left_p, right_p), active_counts, level, limit, more
        )
    capacity = 3 * slots * columns * width // 8
    lists = compact(motion, pressure, place, meta[:, : 3 * parts], parts, capacity)
    arrived = lax.all_to_all(lists, "sub", split_axis=0, concat_axis=0, tiled=True)
    return arrived.transpose(1, 0, 2).reshape(8, parts * capacity)


def solution(mesh):
    placed = (
        P(None, None, "tile", "sub"),
        P(None, None, "tile", "sub"),
        P(None, "tile", "sub"),
        P(None, "tile", "sub"),
        P(None, "tile", "sub"),
        P(None, "tile", "sub"),
    )
    return jax.shard_map(
        shards, mesh=mesh, in_specs=placed, out_specs=P(None, ("tile", "sub")), check_vma=False
    )
```

```python
import functools
import math

import jax
import jax.numpy as jnp
from jax import lax
from jax.experimental import pallas as pl
from jax.experimental.pallas import tpu as pltpu
from jax.sharding import PartitionSpec as P

KERNEL_NORM = 21.0 / (2.0 * math.pi)
GAMMA = 5.0 / 3.0
TIME_STEP = 0.05
SOFTEN = 0.01
LANES = 128
ROWS = 8
VMEM = pl.BlockSpec(memory_space=pltpu.VMEM)
SMEM = pl.BlockSpec(memory_space=pltpu.SMEM)
PARAMS = pltpu.CompilerParams(vmem_limit_bytes=40 << 20)
MOTION, PRESSURE = 7, 3
SHIFTS = (-1, 0, 1)


def lane_of(shape):
    return lax.broadcasted_iota(jnp.int32, shape, 1)


def cost(pairs, ops):
    return pl.CostEstimate(flops=int(pairs * ops * 140), bytes_accessed=1 << 20, transcendentals=0)


def pair_force(own, their, total):
    xi, yi, zi, ui, vi, wi, qi, ci, ri = own
    xj, yj, zj, uj, vj, wj, qj, cj, rj, mj = their
    dx, dy, dz = xi - xj, yi - yj, zi - zj
    squared = dx * dx + dy * dy + dz * dz
    radius = squared * lax.rsqrt(jnp.maximum(squared, 1e-30))
    remain = jnp.maximum(1.0 - radius, 0.0)
    approach = dx * (ui - uj) + dy * (vi - vj) + dz * (wi - wj)
    closing = jnp.minimum(approach, 0.0) * pl.reciprocal(squared + SOFTEN, approx=True)
    viscous = closing * (closing - (ci + cj)) * pl.reciprocal(ri + rj, approx=True)
    strength = (qi + qj + viscous) * ((remain * remain) * (remain * mj))
    return (total[0] + strength * dx, total[1] + strength * dy, total[2] + strength * dz)


def pair_density(own, their, total):
    xi, yi, zi = own
    xj, yj, zj, mj = their
    dx, dy, dz = xi - xj, yi - yj, zi - zj
    squared = dx * dx + dy * dy + dz * dz
    radius = squared * lax.rsqrt(jnp.maximum(squared, 1e-30))
    remain = jnp.maximum(1.0 - radius, 0.0)
    square = remain * remain
    return (total[0] + (square * square) * ((5.0 - 4.0 * remain) * mj),)


DENSITY = ((0, 1.0), (1, 1.0), (2, 1.0)), (), ((6, KERNEL_NORM),), pair_density, 1
FORCE = (
    tuple((c, 1.0) for c in range(3)) + tuple((c, 4.0) for c in range(3, 6)),
    ((0, 1.0), (1, 1.0), (2, 4.0)),
    ((6, 20.0 * KERNEL_NORM),),
    pair_force,
    3,
)


def fill_shifted(shifted, col, row, pieces, field, scale, group, shifts, is_y):
    for cells, left, right, lo, hi in pieces:
        count = cells.shape[-1] // LANES
        blocks = [cells[field, lo:hi, b * LANES : (b + 1) * LANES] for b in range(count)]
        if scale != 1.0:
            blocks = [v * scale for v in blocks]
        lane = lane_of(blocks[0].shape)
        for at, shift in enumerate(shifts):
            values = blocks
            if shift == -1:
                turned = [pltpu.roll(v, 1, 1) for v in blocks]
                end = pltpu.roll(left[lo:hi, :], (LANES - group) % LANES, 1) if group else left[lo:hi, :]
                turned = [end if scale == 1.0 else end * scale] + turned
                values = [jnp.where(lane == 0, turned[b], turned[b + 1]) for b in range(count)]
            elif shift == 1:
                turned = [pltpu.roll(v, LANES - 1, 1) for v in blocks]
                end = pltpu.roll(right[lo:hi, :], LANES - 1 - group, 1)
                turned.append(end if scale == 1.0 else end * scale)
                values = [jnp.where(lane == LANES - 1, turned[b + 1], turned[b]) for b in range(count)]
            if is_y and shift:
                values = [v + float(shift) for v in values]
            for b in range(count):
                shifted[col, at, b, row, lo:hi, :] = values[b]


def fill_column(shifted, col, kind, motion, pressure, group_of, shifts):
    moved, pressed, massed, _, _ = kind
    row = 0
    for pieces, fields in ((motion, moved), (pressure, pressed), (motion, massed)):
        for field, scale in fields:
            is_y = fields is moved and field == 1
            fill_shifted(shifted, col, row, pieces(field), field, scale, group_of(field), shifts, is_y)
            row += 1


def add_pairs(kind, motion_ref, pressure_ref, shifted, x, sources, limit, first, last):
    moved, pressed, _, pair, width = kind
    slots = shifted.shape[-2]
    blocks = shifted.shape[2]
    rows = shifted.shape[3]
    group = min(limit // ROWS, 2 if width == 3 else 4)
    unroll = min(slots, 16 // group if width == 3 else 32 // group)
    forms = shifted.shape[1]
    low_col, low_shift = sources[0]

    def lane_block(b, carry):
        lanes = pl.ds(pl.multiple_of(b * LANES, LANES), LANES)
        for part in range(limit // (ROWS * group)):
            spans = [slice((part * group + v) * ROWS, (part * group + v + 1) * ROWS) for v in range(group)]
            own = []
            for span in spans:
                values = [motion_ref[x, f, span, lanes] * s if s != 1.0 else motion_ref[x, f, span, lanes] for f, s in moved]
                values += [pressure_ref[x, f, span, lanes] * s if s != 1.0 else pressure_ref[x, f, span, lanes] for f, s in pressed]
                own.append(values)

            def source(at, totals):
                col = at // forms
                shift = at - forms * col
                offset = (col + low_shift).astype(jnp.float32)
                mine = [[v[0] - offset] + v[1:] for v in own]

                def step(outer, totals):
                    totals = list(totals)
                    for inner in range(unroll):
                        slot = outer * unroll + inner
                        their = [
                            jnp.broadcast_to(shifted[col + low_col, shift, b, r, pl.ds(slot, 1), :], (ROWS, LANES))
                            for r in range(rows)
                        ]
                        for v in range(group):
                            totals[v] = pair(mine[v], their, totals[v])
                    return tuple(totals)

                return lax.fori_loop(0, slots // unroll, step, totals)

            totals = tuple(first(x, span, lanes) for span in spans)
            totals = lax.fori_loop(0, forms * len(sources), source, totals)
            for span, total in zip(spans, totals):
                last(x, span, lanes, total)
        return carry

    lax.fori_loop(0, blocks, lane_block, 0)


def own_sources(x, columns):
    return [(c, c - x) for c in range(columns) if abs(c - x) <= 1]


def pack_ends(field_of, fields, columns, left_ref, right_ref):
    for ref, at_last in ((left_ref, False), (right_ref, True)):
        lane = None
        packed = None
        for group in range(fields * columns):
            block = field_of(group // columns, group % columns, at_last)
            if lane is None:
                lane = lane_of(block.shape)
                packed = jnp.zeros(block.shape, jnp.float32)
            turn = (group + 1) % LANES if at_last else group
            packed = jnp.where(lane == group, pltpu.roll(block, turn, 1) if turn else block, packed)
        ref[...] = packed


def end_block(ref, column, field, at_last, limit):
    width = ref.shape[-1]
    lanes = slice(width - LANES, width) if at_last else slice(0, LANES)
    return ref[column, field, :limit, lanes]


def first_ends(motion):
    columns, _, slots, _ = motion.shape

    def kernel(motion_ref, left_ref, right_ref):
        pack_ends(
            lambda f, c, last: end_block(motion_ref, c, f, last, slots), MOTION, columns, left_ref, right_ref
        )

    ends = jax.ShapeDtypeStruct((slots, LANES), jnp.float32)
    return pl.pallas_call(kernel, out_shape=(ends, ends), in_specs=[VMEM], out_specs=(VMEM, VMEM), compiler_params=PARAMS)(motion)


def bounds_of(arrays, axis):
    spans, lo = [], 0
    for index, array in enumerate(arrays):
        hi = array.shape[axis]
        if hi > lo:
            spans.append((index, lo, hi))
            lo = hi
    return spans


def own_part(kind, motion, pressure, ends_m, ends_p, limit, shifts, partial=None):
    columns, _, slots, width = motion.shape
    moved, pressed, massed, _, outs = kind
    inner = shifts == (0,)
    if inner:
        ends_m = ends_p = []
    flat_m = [e for pair in ends_m for e in pair]
    flat_p = [e for pair in ends_p for e in pair]
    whole = [(0, 0, slots)]
    spans_m = whole if inner else bounds_of([e[0] for e in ends_m], 0)
    spans_p = whole if inner else bounds_of([e[0] for e in ends_p], 0)
    inputs = [motion] + ([pressure] if pressed else []) + flat_m + flat_p + ([] if partial is None else [partial])
    rows = len(moved) + len(pressed) + len(massed)

    def kernel(*refs):
        refs = list(refs)
        motion_ref = refs.pop(0)
        pressure_ref = refs.pop(0) if pressed else None
        m_refs = refs[: len(flat_m)]
        p_refs = refs[len(flat_m) : len(flat_m) + len(flat_p)]
        partial_ref = None if partial is None else refs[-3]
        out_ref, shifted = refs[-2:]

        def pieces(cells, ends, spans):
            if inner:
                return [(cells, None, None, 0, slots)]
            return [(cells, ends[2 * i], ends[2 * i + 1], lo, hi) for i, lo, hi in spans]

        for c in range(columns):

            def motion_pieces(field):
                return pieces(motion_ref.at[c], m_refs, spans_m if field < 6 else [(len(ends_m) - 1, 0, slots)])

            def pressure_pieces(field):
                return pieces(pressure_ref.at[c], p_refs, spans_p)

            fill_column(shifted, c, kind, motion_pieces, pressure_pieces, lambda f: f * columns + c, shifts)
        zero = jnp.zeros((ROWS, LANES), jnp.float32)

        def first(x, span, lanes):
            if partial is None:
                return (zero,) * outs
            return tuple(partial_ref[x, k, span, lanes] for k in range(outs))

        def last(x, span, lanes, total):
            for k in range(outs):
                out_ref[x, k, span, lanes] = total[k]

        for x in range(columns):
            add_pairs(kind, motion_ref, pressure_ref, shifted, x, own_sources(x, columns), limit, first, last)

    return pl.pallas_call(
        kernel,
        out_shape=jax.ShapeDtypeStruct((columns, outs, limit, width), jnp.float32),
        in_specs=[VMEM] * len(inputs),
        out_specs=VMEM,
        scratch_shapes=[pltpu.VMEM((columns, len(shifts), width // LANES, rows, slots, LANES), jnp.float32)],
        compiler_params=PARAMS,
        cost_estimate=cost(limit * slots * len(shifts) * (3 * columns - 2) * width, 60 if outs == 3 else 30),
    )(*inputs)


def halo_sums(kind, refs, columns, slots, limit, first, last, motion_ref, pressure_ref, shifted):
    for side in range(2):
        m_refs, p_refs = refs[side]
        column = columns - 1 if side == 0 else 0
        spans_m = bounds_of([ends for _, ends in m_refs], 0)
        spans_p = bounds_of([ends for _, ends in p_refs], 0)

        def pieces(history, spans):
            out = []
            for i, lo, hi in spans:
                cells, ends = history[i]
                out.append((cells, ends.at[:, 0:LANES], ends.at[:, LANES : 2 * LANES], lo, hi))
            return out

        def motion_pieces(field):
            return pieces(m_refs, spans_m if field < 6 else [(len(m_refs) - 1, 0, slots)])

        def pressure_pieces(field):
            return pieces(p_refs, spans_p)

        fill_column(shifted, side, kind, motion_pieces, pressure_pieces, lambda f: f * columns + column, SHIFTS)
        x, shift = (0, -1) if side == 0 else (columns - 1, 1)
        add_pairs(kind, motion_ref, pressure_ref, shifted, x, [(side, shift)], limit, first, last)


def paired(refs):
    return [(refs[i], refs[i + 1]) for i in range(0, len(refs), 2)]


def with_own_ends(refs):
    return [(ref, ref.at[ref.shape[0] - 1]) for ref in refs]


def density_rest(motion, partial, messages, density, entropy, counts, level, limit, slots_sent):
    columns, _, slots, width = motion.shape
    (m_left, m_right) = messages
    first = density is None
    inputs = [motion, partial, entropy, counts] + ([] if first else [density]) + m_left + m_right
    n_in, n_m = len(inputs), len(m_left)
    rows = 4

    def kernel(*refs):
        motion_ref, partial_ref, entropy_ref, counts_ref = refs[:4]
        old_ref = None if first else refs[4]
        m_refs = refs[n_in - 2 * n_m : n_in]
        press_ref, left_ref, right_ref, shifted, sums = refs[n_in:]
        sums[...] = partial_ref[...]

        def start(x, span, lanes):
            return (sums[x, 0, span, lanes],)

        def end(x, span, lanes, total):
            sums[x, 0, span, lanes] = total[0]

        sides = ((paired(m_refs[:n_m]), []), (paired(m_refs[n_m:]), []))
        halo_sums(DENSITY, sides, columns, slots, limit, start, end, motion_ref, None, shifted)
        for x in range(columns):
            count = counts_ref[level, x : x + 1, :]
            for lo in range(0, slots, ROWS):
                span = slice(lo, lo + ROWS)
                if lo >= limit:
                    if first:
                        value = jnp.ones((ROWS, width), jnp.float32)
                    else:
                        for f in range(3):
                            press_ref[x, f, span, :] = old_ref[x, f, span, :]
                        continue
                else:
                    slot = lax.broadcasted_iota(jnp.int32, (ROWS, width), 0) + lo
                    before = jnp.ones((ROWS, width), jnp.float32) if first else old_ref[x, 2, span, :]
                    value = jnp.where(slot < count, sums[x, 0, span, :], before)
                pressure = entropy_ref[x, span, :] * jnp.exp(jnp.log(value) * (GAMMA - 2.0))
                press_ref[x, 0, span, :] = pressure
                press_ref[x, 1, span, :] = jnp.sqrt(GAMMA * pressure * value)
                press_ref[x, 2, span, :] = value
        pack_ends(lambda f, c, last: end_block(press_ref, c, f, last, slots_sent), PRESSURE, columns, left_ref, right_ref)

    ends = jax.ShapeDtypeStruct((slots_sent, LANES), jnp.float32)
    return pl.pallas_call(
        kernel,
        out_shape=(jax.ShapeDtypeStruct((columns, PRESSURE, slots, width), jnp.float32), ends, ends),
        in_specs=[VMEM] * n_in,
        out_specs=(VMEM,) * 3,
        scratch_shapes=[
            pltpu.VMEM((2, 3, width // LANES, rows, slots, LANES), jnp.float32),
            pltpu.VMEM((columns, 1, limit, width), jnp.float32),
        ],
        compiler_params=PARAMS,
        cost_estimate=cost(limit * slots * 6 * width, 30),
    )(*inputs)


def force_rest(motion, pressure, partial, messages_m, messages_p, counts, level, limit, slots_sent):
    columns, _, slots, width = motion.shape
    n_m, n_p = len(messages_m[0]), len(messages_p[0])
    inputs = [motion, pressure, partial, counts] + messages_m[0] + messages_p[0] + messages_m[1] + messages_p[1]
    n_in = len(inputs)
    rows = 10
    ends = jax.ShapeDtypeStruct((slots_sent, LANES), jnp.float32)
    outs = (jax.ShapeDtypeStruct(motion.shape, jnp.float32),) + ((ends, ends) if slots_sent else ())

    def kernel(*refs):
        motion_ref, pressure_ref, partial_ref, counts_ref = refs[:4]
        sides = []
        for side in range(2):
            at = 4 + side * (n_m + n_p)
            sides.append((paired(refs[at : at + n_m]), with_own_ends(refs[at + n_m : at + n_m + n_p])))
        new_ref = refs[n_in]
        shifted, sums = refs[-2:]
        sums[...] = partial_ref[...]

        def start(x, span, lanes):
            return tuple(sums[x, k, span, lanes] for k in range(3))

        def end(x, span, lanes, total):
            for k in range(3):
                sums[x, k, span, lanes] = total[k]

        halo_sums(FORCE, sides, columns, slots, limit, start, end, motion_ref, pressure_ref, shifted)
        for x in range(columns):
            count = counts_ref[level, x : x + 1, :]
            new_ref[x, 6, :, :] = motion_ref[x, 6, :, :]
            if limit < slots:
                for f in range(6):
                    new_ref[x, f, limit:, :] = motion_ref[x, f, limit:, :]
            for lo in range(0, limit, ROWS):
                span = slice(lo, lo + ROWS)
                active = lax.broadcasted_iota(jnp.int32, (ROWS, width), 0) + lo < count
                for k in range(3):
                    place, speed = motion_ref[x, k, span, :], motion_ref[x, 3 + k, span, :]
                    faster = speed + TIME_STEP * sums[x, k, span, :]
                    new_ref[x, 3 + k, span, :] = jnp.where(active, faster, speed)
                    new_ref[x, k, span, :] = jnp.where(active, place + TIME_STEP * faster, place)
        if slots_sent:
            left_ref, right_ref = refs[n_in + 1 : n_in + 3]
            pack_ends(lambda f, c, last: end_block(new_ref, c, f, last, slots_sent), 6, columns, left_ref, right_ref)

    made = pl.pallas_call(
        kernel,
        out_shape=outs,
        in_specs=[VMEM] * n_in,
        out_specs=(VMEM,) * len(outs),
        scratch_shapes=[
            pltpu.VMEM((2, 3, width // LANES, rows, slots, LANES), jnp.float32),
            pltpu.VMEM((columns, 3, limit, width), jnp.float32),
        ],
        compiler_params=PARAMS,
        cost_estimate=cost(limit * slots * 6 * width, 60),
    )(*inputs)
    return made if slots_sent else (made[0], None, None)


def ranks(destination, parts):
    rows, width = destination.shape

    def kernel(dest_ref, place_ref, meta_ref):
        dest = dest_ref[...]
        low = lax.broadcasted_iota(jnp.int32, (width, width), 0)
        upto = jnp.where(low <= lane_of((width, width)), 1.0, 0.0).astype(jnp.bfloat16)
        above = lax.broadcasted_iota(jnp.int32, (rows, rows), 0) > lane_of((rows, rows))
        above = jnp.where(above, 1.0, 0.0).astype(jnp.bfloat16)
        lane = lane_of((rows, LANES))
        meta = jnp.zeros((rows, LANES), jnp.float32)
        place = jnp.zeros((rows, width), jnp.float32)
        start = jnp.zeros((rows, 1), jnp.float32)
        for d in range(parts):
            mask = jnp.where(dest == d, 1.0, 0.0)
            inside = jnp.dot(mask.astype(jnp.bfloat16), upto, preferred_element_type=jnp.float32)
            count = inside[:, width - 1 : width]
            wide = jnp.broadcast_to(count, (rows, LANES))
            before = jnp.dot(above, wide.astype(jnp.bfloat16), preferred_element_type=jnp.float32)
            place = place + mask * (inside - 1.0 + start)
            meta = jnp.where(lane == d, before, meta)
            meta = jnp.where(lane == parts + d, jnp.broadcast_to(start, (rows, LANES)), meta)
            meta = jnp.where(lane == 2 * parts + d, before + wide, meta)
            start = start + count
        place_ref[...] = place.astype(jnp.int32)
        meta_ref[...] = meta.astype(jnp.int32)

    return pl.pallas_call(
        kernel,
        out_shape=(jax.ShapeDtypeStruct((rows, width), jnp.int32), jax.ShapeDtypeStruct((rows, LANES), jnp.int32)),
        in_specs=[VMEM],
        out_specs=(VMEM, VMEM),
        compiler_params=PARAMS,
    )(destination)


def compact(motion, pressure, place, meta, parts, capacity):
    columns, _, slots, width = motion.shape
    chunks = width // LANES
    total = -(-capacity // LANES)

    def kernel(motion_ref, pressure_ref, place_ref, meta_ref, out_ref, local, lists):
        lane = lane_of((ROWS, LANES))

        def do_group(group, carry):
            span = pl.ds(pl.multiple_of(group * ROWS, ROWS), ROWS)
            fields = [
                [motion_ref[x, f, span, :] for f in range(6)] + [pressure_ref[x, 2, span, :], motion_ref[x, 6, span, :]]
                for x in range(columns)
            ]
            for s in range(ROWS):
                for x in range(columns):
                    state = jnp.concatenate([v[s : s + 1, :] for v in fields[x]], axis=0)
                    high = state.astype(jnp.bfloat16).astype(jnp.float32)
                    rest = state - high
                    middle = rest.astype(jnp.bfloat16).astype(jnp.float32)
                    lowest = rest - middle
                    stacked = jnp.concatenate([high, middle, lowest], axis=0).astype(jnp.bfloat16)
                    row = (group * ROWS + s) * columns + x
                    wanted = place_ref[pl.ds(row, 1), :]
                    hot = jnp.where(lax.broadcasted_iota(jnp.int32, (width, width), 0) == wanted, 1.0, 0.0)
                    moved = lax.dot_general(
                        stacked, hot.astype(jnp.bfloat16), (((1,), (1,)), ((), ())), preferred_element_type=jnp.float32
                    )
                    moved = moved[0:8] + moved[8:16] + moved[16:24]
                    buffer = (s * columns + x) % 4
                    for c in range(chunks):
                        local[buffer, c + 1] = moved[:, c * LANES : (c + 1) * LANES]
                    for d in range(parts):
                        base = meta_ref[row, d]
                        begin = meta_ref[row, parts + d]
                        chunk = lax.shift_right_logical(base, 7)
                        off = lax.bitwise_and(base, LANES - 1)
                        turn = lax.bitwise_and(off - begin, LANES - 1)
                        at = lax.shift_right_logical(begin, 7)
                        at = at + jnp.where(off < lax.bitwise_and(begin, LANES - 1), 1, 0)
                        turned = [pltpu.roll(local[buffer, at + k], turn, 1) for k in range(chunks + 2)]
                        for k in range(chunks + 1):
                            value = jnp.where(lane >= turn, turned[k + 1], turned[k])
                            if k == 0:
                                value = jnp.where(lane >= off, value, lists[d, chunk])
                            lists[d, chunk + k] = value
            return carry

        lax.fori_loop(0, slots // ROWS, do_group, 0)
        for d in range(parts):
            count = meta_ref[slots * columns - 1, 2 * parts + d]
            for c in range(total):
                out_ref[d, :, c * LANES : (c + 1) * LANES] = jnp.where(lane + c * LANES < count, lists[d, c], 0.0)

    return pl.pallas_call(
        kernel,
        out_shape=jax.ShapeDtypeStruct((parts, 8, capacity), jnp.float32),
        in_specs=[VMEM, VMEM, VMEM, SMEM],
        out_specs=VMEM,
        scratch_shapes=[
            pltpu.VMEM((4, 2 * chunks + 4, ROWS, LANES), jnp.float32),
            pltpu.VMEM((parts, total + chunks + 2, ROWS, LANES), jnp.float32),
        ],
        compiler_params=PARAMS,
    )(motion, pressure, place, meta)


def pass_on(value, axis, step):
    count = lax.axis_size(axis)
    return lax.ppermute(value, axis, [(i, (i + step) % count) for i in range(count)])


def swap_ends(left_ends, right_ends):
    return pass_on(right_ends, "sub", 1), pass_on(left_ends, "sub", -1)


def swap_columns(first, final):
    return pass_on(final, "tile", 1), pass_on(first, "tile", -1)


def beside(ends, width):
    plane = jnp.concatenate(ends, axis=1)
    return jnp.pad(plane, ((0, 0), (0, width - plane.shape[1])))


def shards(offsets, velocity, mass, entropy, active_counts, targets):
    slots, columns, width = mass.shape
    levels = active_counts.shape[0]
    parts = lax.axis_size("sub")
    slot_index = lax.broadcasted_iota(jnp.int32, mass.shape, 0)
    mass_live = jnp.where(slot_index < active_counts[0][None], mass, 0.0)
    motion = jnp.concatenate([offsets, velocity, mass_live[None]], axis=0).transpose(2, 0, 1, 3)
    entropy = entropy.transpose(1, 0, 2)
    limits = (slots, slots // 2, slots // 4)
    pressure = None
    ends_m, ends_p = [], []
    left_m, right_m, left_p, right_p = [], [], [], []
    made = first_ends(motion)
    place, meta = ranks(targets.reshape(slots * columns, width), parts)
    for level in range(levels):
        limit = limits[level]
        sent = limits[max(level - 1, 0)]
        fields = MOTION if level == 0 else 6
        cells = swap_columns(motion[0, :fields, :sent], motion[-1, :fields, :sent])
        ends_m.insert(0, swap_ends(*made))
        partial = own_part(DENSITY, motion, None, ends_m, [], limit, (0,))
        plane = beside(ends_m[0], width)
        corners = swap_columns(plane, plane)
        partial = own_part(DENSITY, motion, None, ends_m, [], limit, (-1, 1), partial)
        left_m[:0] = [cells[0], corners[0]]
        right_m[:0] = [cells[1], corners[1]]
        pressure, *made = density_rest(motion, partial, (left_m, right_m), pressure, entropy, active_counts, level, limit, limit)
        ends_p.insert(0, swap_ends(*made))
        partial = own_part(FORCE, motion, pressure, ends_m, ends_p, limit, (0,))
        plane = beside(ends_p[0], width)[None]
        first = jnp.concatenate([pressure[0, :, :limit], plane], axis=0)
        final = jnp.concatenate([pressure[-1, :, :limit], plane], axis=0)
        cells = swap_columns(first, final)
        left_p.insert(0, cells[0])
        right_p.insert(0, cells[1])
        partial = own_part(FORCE, motion, pressure, ends_m, ends_p, limit, (-1, 1), partial)
        more = limit if level < levels - 1 else 0
        motion, *made = force_rest(
            motion, pressure, partial, (left_m, right_m), (left_p, right_p), active_counts, level, limit, more
        )
    capacity = 3 * slots * columns * width // 8
    lists = compact(motion, pressure, place, meta[:, : 3 * parts], parts, capacity)
    arrived = lax.all_to_all(lists, "sub", split_axis=0, concat_axis=0, tiled=True)
    return arrived.transpose(1, 0, 2).reshape(8, parts * capacity)


def solution(mesh):
    placed = (
        P(None, None, "tile", "sub"),
        P(None, None, "tile", "sub"),
        P(None, "tile", "sub"),
        P(None, "tile", "sub"),
        P(None, "tile", "sub"),
        P(None, "tile", "sub"),
    )
    return jax.shard_map(
        shards, mesh=mesh, in_specs=placed, out_specs=P(None, ("tile", "sub")), check_vma=False
    )
```

```python
import functools
import math

import jax
import jax.numpy as jnp
from jax import lax
from jax.experimental import pallas as pl
from jax.experimental.pallas import tpu as pltpu
from jax.sharding import PartitionSpec as P

KERNEL_NORM = 21.0 / (2.0 * math.pi)
GAMMA = 5.0 / 3.0
TIME_STEP = 0.05
SOFTEN = 0.01
LANES = 128
ROWS = 8
VMEM = pl.BlockSpec(memory_space=pltpu.VMEM)
SMEM = pl.BlockSpec(memory_space=pltpu.SMEM)
PARAMS = pltpu.CompilerParams(vmem_limit_bytes=40 << 20)
MOTION, PRESSURE = 7, 3
SHIFTS = (-1, 0, 1)


def lane_of(shape):
    return lax.broadcasted_iota(jnp.int32, shape, 1)


def cost(pairs, ops):
    return pl.CostEstimate(flops=int(pairs * ops * 15), bytes_accessed=1 << 20, transcendentals=0)


def pair_force(own, their, total):
    xi, yi, zi, ui, vi, wi, qi, ci, ri = own
    xj, yj, zj, uj, vj, wj, qj, cj, rj, mj = their
    dx, dy, dz = xi - xj, yi - yj, zi - zj
    squared = dx * dx + dy * dy + dz * dz
    radius = squared * lax.rsqrt(jnp.maximum(squared, 1e-30))
    remain = jnp.maximum(1.0 - radius, 0.0)
    approach = dx * (ui - uj) + dy * (vi - vj) + dz * (wi - wj)
    closing = jnp.minimum(approach, 0.0) * pl.reciprocal(squared + SOFTEN, approx=True)
    viscous = closing * (closing - (ci + cj)) * pl.reciprocal(ri + rj, approx=True)
    strength = (qi + qj + viscous) * ((remain * remain) * (remain * mj))
    return (total[0] + strength * dx, total[1] + strength * dy, total[2] + strength * dz)


def pair_density(own, their, total):
    xi, yi, zi = own
    xj, yj, zj, mj = their
    dx, dy, dz = xi - xj, yi - yj, zi - zj
    squared = dx * dx + dy * dy + dz * dz
    radius = squared * lax.rsqrt(jnp.maximum(squared, 1e-30))
    remain = jnp.maximum(1.0 - radius, 0.0)
    square = remain * remain
    return (total[0] + (square * square) * ((5.0 - 4.0 * remain) * mj),)


DENSITY = ((0, 1.0), (1, 1.0), (2, 1.0)), (), ((6, KERNEL_NORM),), pair_density, 1
FORCE = (
    tuple((c, 1.0) for c in range(3)) + tuple((c, 4.0) for c in range(3, 6)),
    ((0, 1.0), (1, 1.0), (2, 4.0)),
    ((6, 20.0 * KERNEL_NORM),),
    pair_force,
    3,
)


def fill_shifted(shifted, col, row, pieces, scale, group, shifts, is_y):
    for cells, left, right, lo, hi in pieces:
        count = cells.shape[-1] // LANES
        blocks = [cells[lo:hi, b * LANES : (b + 1) * LANES] for b in range(count)]
        if scale != 1.0:
            blocks = [v * scale for v in blocks]
        lane = lane_of(blocks[0].shape)
        for at, shift in enumerate(shifts):
            values = blocks
            if shift == -1:
                turned = [pltpu.roll(v, 1, 1) for v in blocks]
                end = pltpu.roll(left[lo:hi, :], (LANES - group) % LANES, 1) if group else left[lo:hi, :]
                turned = [end if scale == 1.0 else end * scale] + turned
                values = [jnp.where(lane == 0, turned[b], turned[b + 1]) for b in range(count)]
            elif shift == 1:
                turned = [pltpu.roll(v, LANES - 1, 1) for v in blocks]
                end = pltpu.roll(right[lo:hi, :], LANES - 1 - group, 1)
                turned.append(end if scale == 1.0 else end * scale)
                values = [jnp.where(lane == LANES - 1, turned[b + 1], turned[b]) for b in range(count)]
            if is_y and shift:
                values = [v + float(shift) for v in values]
            for b in range(count):
                shifted[col, at, b, row, lo:hi, :] = values[b]


def fill_column(shifted, col, kind, motion, pressure, group_of, shifts):
    moved, pressed, massed, _, _ = kind
    row = 0
    for pieces, fields in ((motion, moved), (pressure, pressed), (motion, massed)):
        for field, scale in fields:
            is_y = fields is moved and field == 1
            fill_shifted(shifted, col, row, pieces(field), scale, group_of(field), shifts, is_y)
            row += 1


def add_pairs(kind, motion_ref, pressure_ref, shifted, x, sources, limit, first, last):
    moved, pressed, _, pair, width = kind
    slots = shifted.shape[-2]
    blocks = shifted.shape[2]
    rows = shifted.shape[3]
    group = min(limit // ROWS, 2 if width == 3 else 4)
    unroll = min(slots, 16 // group if width == 3 else 32 // group)
    forms = shifted.shape[1]
    low_col, low_shift = sources[0]

    def lane_block(b, carry):
        lanes = pl.ds(pl.multiple_of(b * LANES, LANES), LANES)
        for part in range(limit // (ROWS * group)):
            spans = [slice((part * group + v) * ROWS, (part * group + v + 1) * ROWS) for v in range(group)]
            own = []
            for span in spans:
                values = [motion_ref[x, f, span, lanes] * s if s != 1.0 else motion_ref[x, f, span, lanes] for f, s in moved]
                values += [pressure_ref[x, f, span, lanes] * s if s != 1.0 else pressure_ref[x, f, span, lanes] for f, s in pressed]
                own.append(values)

            def source(at, totals):
                col = at // forms
                shift = at - forms * col
                offset = (col + low_shift).astype(jnp.float32)
                mine = [[v[0] - offset] + v[1:] for v in own]

                def step(outer, totals):
                    totals = list(totals)
                    for inner in range(unroll):
                        slot = outer * unroll + inner
                        their = [
                            jnp.broadcast_to(shifted[col + low_col, shift, b, r, pl.ds(slot, 1), :], (ROWS, LANES))
                            for r in range(rows)
                        ]
                        for v in range(group):
                            totals[v] = pair(mine[v], their, totals[v])
                    return tuple(totals)

                return lax.fori_loop(0, slots // unroll, step, totals)

            totals = tuple(first(x, span, lanes) for span in spans)
            totals = lax.fori_loop(0, forms * len(sources), source, totals)
            for span, total in zip(spans, totals):
                last(x, span, lanes, total)
        return carry

    lax.fori_loop(0, blocks, lane_block, 0)


def own_sources(x, columns):
    return [(c, c - x) for c in range(columns) if abs(c - x) <= 1]


def pack_ends(field_of, fields, columns, left_ref, right_ref):
    for ref, at_last in ((left_ref, False), (right_ref, True)):
        lane = None
        packed = None
        for group in range(fields * columns):
            block = field_of(group // columns, group % columns, at_last)
            if lane is None:
                lane = lane_of(block.shape)
                packed = jnp.zeros(block.shape, jnp.float32)
            turn = (group + 1) % LANES if at_last else group
            packed = jnp.where(lane == group, pltpu.roll(block, turn, 1) if turn else block, packed)
        ref[...] = packed


def end_block(ref, column, field, at_last, limit):
    width = ref.shape[-1]
    lanes = slice(width - LANES, width) if at_last else slice(0, LANES)
    return ref[column, field, :limit, lanes]


def first_ends(motion):
    columns, _, slots, _ = motion.shape

    def kernel(motion_ref, left_ref, right_ref):
        pack_ends(
            lambda f, c, last: end_block(motion_ref, c, f, last, slots), MOTION, columns, left_ref, right_ref
        )

    ends = jax.ShapeDtypeStruct((slots, LANES), jnp.float32)
    return pl.pallas_call(kernel, out_shape=(ends, ends), in_specs=[VMEM], out_specs=(VMEM, VMEM), compiler_params=PARAMS)(motion)


def bounds_of(sizes):
    spans, lo = [], 0
    for index, hi in enumerate(sizes):
        if hi > lo:
            spans.append((index, lo, hi))
            lo = hi
    return spans


def own_part(kind, motion, pressure, ends_m, ends_p, limit, shifts, partial=None):
    columns, _, slots, width = motion.shape
    moved, pressed, massed, _, outs = kind
    inner = shifts == (0,)
    if inner:
        ends_m = ends_p = []
    flat_m = [e for pair in ends_m for e in pair]
    flat_p = [e for pair in ends_p for e in pair]
    whole = [(0, 0, slots)]
    spans_m = whole if inner else bounds_of([e[0].shape[0] for e in ends_m])
    spans_p = whole if inner else bounds_of([e[0].shape[0] for e in ends_p])
    inputs = [motion] + ([pressure] if pressed else []) + flat_m + flat_p + ([] if partial is None else [partial])
    rows = len(moved) + len(pressed) + len(massed)

    def kernel(*refs):
        refs = list(refs)
        motion_ref = refs.pop(0)
        pressure_ref = refs.pop(0) if pressed else None
        m_refs = refs[: len(flat_m)]
        p_refs = refs[len(flat_m) : len(flat_m) + len(flat_p)]
        partial_ref = None if partial is None else refs[-3]
        out_ref, shifted = refs[-2:]

        def pieces(cells, ends, spans):
            if inner:
                return [(cells, None, None, 0, slots)]
            return [(cells, ends[2 * i], ends[2 * i + 1], lo, hi) for i, lo, hi in spans]

        for c in range(columns):

            def motion_pieces(field):
                return pieces(motion_ref.at[c, field], m_refs, spans_m if field < 6 else [(len(ends_m) - 1, 0, slots)])

            def pressure_pieces(field):
                return pieces(pressure_ref.at[c, field], p_refs, spans_p)

            fill_column(shifted, c, kind, motion_pieces, pressure_pieces, lambda f: f * columns + c, shifts)
        zero = jnp.zeros((ROWS, LANES), jnp.float32)

        def first(x, span, lanes):
            if partial is None:
                return (zero,) * outs
            return tuple(partial_ref[x, k, span, lanes] for k in range(outs))

        def last(x, span, lanes, total):
            for k in range(outs):
                out_ref[x, k, span, lanes] = total[k]

        for x in range(columns):
            add_pairs(kind, motion_ref, pressure_ref, shifted, x, own_sources(x, columns), limit, first, last)

    return pl.pallas_call(
        kernel,
        out_shape=jax.ShapeDtypeStruct((columns, outs, limit, width), jnp.float32),
        in_specs=[VMEM] * len(inputs),
        out_specs=VMEM,
        scratch_shapes=[pltpu.VMEM((columns, len(shifts), width // LANES, rows, slots, LANES), jnp.float32)],
        compiler_params=PARAMS,
        cost_estimate=cost(limit * slots * len(shifts) * (3 * columns - 2) * width, 60 if outs == 3 else 30),
    )(*inputs)


def halo_sums(kind, refs, columns, slots, limit, first, last, motion_ref, pressure_ref, shifted, sizes_m, sizes_p):
    spans_m, spans_p = bounds_of(sizes_m), bounds_of(sizes_p)
    for side in range(2):
        m_refs, p_refs = refs[side]
        column = columns - 1 if side == 0 else 0

        def field_of(ref, at, size):
            return ref.at[at : at + size]

        def piece(cells, ends, lo, hi):
            return (cells, ends.at[:, 0:LANES], ends.at[:, LANES : 2 * LANES], lo, hi)

        def motion_pieces(field):
            out = []
            for i, lo, hi in spans_m if field < 6 else [(len(sizes_m) - 1, 0, slots)]:
                size = sizes_m[i]
                ends = field_of(m_refs[i], (4 if i == len(sizes_m) - 1 else 3) * size, size)
                if field < 3 or field == 6:
                    cells = field_of(m_refs[i], min(field, 3) * size, size)
                else:
                    cells = field_of(p_refs[i], 4 * sizes_p[i] + (field - 3) * size, size)
                out.append(piece(cells, ends, lo, hi))
            return out

        def pressure_pieces(field):
            return [
                piece(field_of(p_refs[i], field * sizes_p[i], sizes_p[i]), field_of(p_refs[i], 3 * sizes_p[i], sizes_p[i]), lo, hi)
                for i, lo, hi in spans_p
            ]

        fill_column(shifted, side, kind, motion_pieces, pressure_pieces, lambda f: f * columns + column, SHIFTS)
        x, shift = (0, -1) if side == 0 else (columns - 1, 1)
        add_pairs(kind, motion_ref, pressure_ref, shifted, x, [(side, shift)], limit, first, last)


def density_rest(motion, partial, messages, sizes, density, entropy, counts, level, limit, slots_sent):
    columns, _, slots, width = motion.shape
    (m_left, m_right) = messages
    first = density is None
    inputs = [motion, partial, entropy, counts] + ([] if first else [density]) + m_left + m_right
    n_in, n_m = len(inputs), len(m_left)
    rows = 4

    def kernel(*refs):
        motion_ref, partial_ref, entropy_ref, counts_ref = refs[:4]
        old_ref = None if first else refs[4]
        m_refs = refs[n_in - 2 * n_m : n_in]
        press_ref, left_ref, right_ref, shifted, sums = refs[n_in:]
        sums[...] = partial_ref[...]

        def start(x, span, lanes):
            return (sums[x, 0, span, lanes],)

        def end(x, span, lanes, total):
            sums[x, 0, span, lanes] = total[0]

        sides = ((m_refs[:n_m], []), (m_refs[n_m:], []))
        halo_sums(DENSITY, sides, columns, slots, limit, start, end, motion_ref, None, shifted, sizes, [])
        for x in range(columns):
            count = counts_ref[level, x : x + 1, :]
            for lo in range(0, slots, ROWS):
                span = slice(lo, lo + ROWS)
                if lo >= limit:
                    if first:
                        value = jnp.ones((ROWS, width), jnp.float32)
                    else:
                        for f in range(3):
                            press_ref[x, f, span, :] = old_ref[x, f, span, :]
                        continue
                else:
                    slot = lax.broadcasted_iota(jnp.int32, (ROWS, width), 0) + lo
                    before = jnp.ones((ROWS, width), jnp.float32) if first else old_ref[x, 2, span, :]
                    value = jnp.where(slot < count, sums[x, 0, span, :], before)
                pressure = entropy_ref[x, span, :] * jnp.exp(jnp.log(value) * (GAMMA - 2.0))
                press_ref[x, 0, span, :] = pressure
                press_ref[x, 1, span, :] = jnp.sqrt(GAMMA * pressure * value)
                press_ref[x, 2, span, :] = value
        pack_ends(lambda f, c, last: end_block(press_ref, c, f, last, slots_sent), PRESSURE, columns, left_ref, right_ref)

    ends = jax.ShapeDtypeStruct((slots_sent, LANES), jnp.float32)
    return pl.pallas_call(
        kernel,
        out_shape=(jax.ShapeDtypeStruct((columns, PRESSURE, slots, width), jnp.float32), ends, ends),
        in_specs=[VMEM] * n_in,
        out_specs=(VMEM,) * 3,
        scratch_shapes=[
            pltpu.VMEM((2, 3, width // LANES, rows, slots, LANES), jnp.float32),
            pltpu.VMEM((columns, 1, limit, width), jnp.float32),
        ],
        compiler_params=PARAMS,
        cost_estimate=cost(limit * slots * 6 * width, 30),
    )(*inputs)


def force_rest(motion, pressure, partial, messages_m, messages_p, sizes_m, sizes_p, counts, level, limit, slots_sent):
    columns, _, slots, width = motion.shape
    n_m, n_p = len(messages_m[0]), len(messages_p[0])
    inputs = [motion, pressure, partial, counts] + messages_m[0] + messages_p[0] + messages_m[1] + messages_p[1]
    n_in = len(inputs)
    rows = 10
    ends = jax.ShapeDtypeStruct((slots_sent, LANES), jnp.float32)
    outs = (jax.ShapeDtypeStruct(motion.shape, jnp.float32),) + ((ends, ends) if slots_sent else ())

    def kernel(*refs):
        motion_ref, pressure_ref, partial_ref, counts_ref = refs[:4]
        sides = []
        for side in range(2):
            at = 4 + side * (n_m + n_p)
            sides.append((refs[at : at + n_m], refs[at + n_m : at + n_m + n_p]))
        new_ref = refs[n_in]
        shifted, sums = refs[-2:]
        sums[...] = partial_ref[...]

        def start(x, span, lanes):
            return tuple(sums[x, k, span, lanes] for k in range(3))

        def end(x, span, lanes, total):
            for k in range(3):
                sums[x, k, span, lanes] = total[k]

        halo_sums(
            FORCE, sides, columns, slots, limit, start, end, motion_ref, pressure_ref, shifted, sizes_m, sizes_p
        )
        for x in range(columns):
            count = counts_ref[level, x : x + 1, :]
            new_ref[x, 6, :, :] = motion_ref[x, 6, :, :]
            if limit < slots:
                for f in range(6):
                    new_ref[x, f, limit:, :] = motion_ref[x, f, limit:, :]
            for lo in range(0, limit, ROWS):
                span = slice(lo, lo + ROWS)
                active = lax.broadcasted_iota(jnp.int32, (ROWS, width), 0) + lo < count
                for k in range(3):
                    place, speed = motion_ref[x, k, span, :], motion_ref[x, 3 + k, span, :]
                    faster = speed + TIME_STEP * sums[x, k, span, :]
                    new_ref[x, 3 + k, span, :] = jnp.where(active, faster, speed)
                    new_ref[x, k, span, :] = jnp.where(active, place + TIME_STEP * faster, place)
        if slots_sent:
            left_ref, right_ref = refs[n_in + 1 : n_in + 3]
            pack_ends(lambda f, c, last: end_block(new_ref, c, f, last, slots_sent), 6, columns, left_ref, right_ref)

    made = pl.pallas_call(
        kernel,
        out_shape=outs,
        in_specs=[VMEM] * n_in,
        out_specs=(VMEM,) * len(outs),
        scratch_shapes=[
            pltpu.VMEM((2, 3, width // LANES, rows, slots, LANES), jnp.float32),
            pltpu.VMEM((columns, 3, limit, width), jnp.float32),
        ],
        compiler_params=PARAMS,
        cost_estimate=cost(limit * slots * 6 * width, 60),
    )(*inputs)
    return made if slots_sent else (made[0], None, None)


def ranks(destination, parts):
    rows, width = destination.shape

    def kernel(dest_ref, place_ref, meta_ref):
        dest = dest_ref[...]
        low = lax.broadcasted_iota(jnp.int32, (width, width), 0)
        upto = jnp.where(low <= lane_of((width, width)), 1.0, 0.0).astype(jnp.bfloat16)
        above = lax.broadcasted_iota(jnp.int32, (rows, rows), 0) > lane_of((rows, rows))
        above = jnp.where(above, 1.0, 0.0).astype(jnp.bfloat16)
        lane = lane_of((rows, LANES))
        meta = jnp.zeros((rows, LANES), jnp.float32)
        place = jnp.zeros((rows, width), jnp.float32)
        start = jnp.zeros((rows, 1), jnp.float32)
        for d in range(parts):
            mask = jnp.where(dest == d, 1.0, 0.0)
            inside = jnp.dot(mask.astype(jnp.bfloat16), upto, preferred_element_type=jnp.float32)
            count = inside[:, width - 1 : width]
            wide = jnp.broadcast_to(count, (rows, LANES))
            before = jnp.dot(above, wide.astype(jnp.bfloat16), preferred_element_type=jnp.float32)
            place = place + mask * (inside - 1.0 + start)
            meta = jnp.where(lane == d, before, meta)
            meta = jnp.where(lane == parts + d, jnp.broadcast_to(start, (rows, LANES)), meta)
            meta = jnp.where(lane == 2 * parts + d, before + wide, meta)
            start = start + count
        place_ref[...] = place.astype(jnp.int32)
        meta_ref[...] = meta.astype(jnp.int32)

    return pl.pallas_call(
        kernel,
        out_shape=(jax.ShapeDtypeStruct((rows, width), jnp.int32), jax.ShapeDtypeStruct((rows, LANES), jnp.int32)),
        in_specs=[VMEM],
        out_specs=(VMEM, VMEM),
        compiler_params=PARAMS,
    )(destination)


def compact(motion, pressure, place, meta, parts, capacity):
    columns, _, slots, width = motion.shape
    chunks = width // LANES
    total = -(-capacity // LANES)

    def kernel(motion_ref, pressure_ref, place_ref, meta_ref, out_ref, local, lists):
        lane = lane_of((ROWS, LANES))

        def do_group(group, carry):
            span = pl.ds(pl.multiple_of(group * ROWS, ROWS), ROWS)
            fields = [
                [motion_ref[x, f, span, :] for f in range(6)] + [pressure_ref[x, 2, span, :], motion_ref[x, 6, span, :]]
                for x in range(columns)
            ]
            for s in range(ROWS):
                for x in range(columns):
                    state = jnp.concatenate([v[s : s + 1, :] for v in fields[x]], axis=0)
                    high = state.astype(jnp.bfloat16).astype(jnp.float32)
                    rest = state - high
                    middle = rest.astype(jnp.bfloat16).astype(jnp.float32)
                    lowest = rest - middle
                    stacked = jnp.concatenate([high, middle, lowest], axis=0).astype(jnp.bfloat16)
                    row = (group * ROWS + s) * columns + x
                    wanted = place_ref[pl.ds(row, 1), :]
                    hot = jnp.where(lax.broadcasted_iota(jnp.int32, (width, width), 0) == wanted, 1.0, 0.0)
                    moved = lax.dot_general(
                        stacked, hot.astype(jnp.bfloat16), (((1,), (1,)), ((), ())), preferred_element_type=jnp.float32
                    )
                    moved = moved[0:8] + moved[8:16] + moved[16:24]
                    buffer = (s * columns + x) % 4
                    for c in range(chunks):
                        local[buffer, c + 1] = moved[:, c * LANES : (c + 1) * LANES]
                    for d in range(parts):
                        base = meta_ref[row, d]
                        begin = meta_ref[row, parts + d]
                        chunk = lax.shift_right_logical(base, 7)
                        off = lax.bitwise_and(base, LANES - 1)
                        turn = lax.bitwise_and(off - begin, LANES - 1)
                        at = lax.shift_right_logical(begin, 7)
                        at = at + jnp.where(off < lax.bitwise_and(begin, LANES - 1), 1, 0)
                        turned = [pltpu.roll(local[buffer, at + k], turn, 1) for k in range(chunks + 2)]
                        for k in range(chunks + 1):
                            value = jnp.where(lane >= turn, turned[k + 1], turned[k])
                            if k == 0:
                                value = jnp.where(lane >= off, value, lists[d, chunk])
                            lists[d, chunk + k] = value
            return carry

        lax.fori_loop(0, slots // ROWS, do_group, 0)
        for d in range(parts):
            count = meta_ref[slots * columns - 1, 2 * parts + d]
            for c in range(total):
                out_ref[d, :, c * LANES : (c + 1) * LANES] = jnp.where(lane + c * LANES < count, lists[d, c], 0.0)

    return pl.pallas_call(
        kernel,
        out_shape=jax.ShapeDtypeStruct((parts, 8, capacity), jnp.float32),
        in_specs=[VMEM, VMEM, VMEM, SMEM],
        out_specs=VMEM,
        scratch_shapes=[
            pltpu.VMEM((4, 2 * chunks + 4, ROWS, LANES), jnp.float32),
            pltpu.VMEM((parts, total + chunks + 2, ROWS, LANES), jnp.float32),
        ],
        compiler_params=PARAMS,
    )(motion, pressure, place, meta)


def pass_on(value, axis, step):
    count = lax.axis_size(axis)
    return lax.ppermute(value, axis, [(i, (i + step) % count) for i in range(count)])


def swap_ends(left_ends, right_ends):
    return pass_on(right_ends, "sub", 1), pass_on(left_ends, "sub", -1)


def swap_columns(parts_of):
    first = jnp.concatenate(parts_of(0), axis=0)
    final = jnp.concatenate(parts_of(-1), axis=0)
    return pass_on(final, "tile", 1), pass_on(first, "tile", -1)


def rows_of(fields):
    return fields.reshape(-1, fields.shape[-1])


def beside(ends, width):
    plane = jnp.concatenate(ends, axis=1)
    return jnp.pad(plane, ((0, 0), (0, width - plane.shape[1])))


def shards(offsets, velocity, mass, entropy, active_counts, targets):
    slots, columns, width = mass.shape
    levels = active_counts.shape[0]
    parts = lax.axis_size("sub")
    slot_index = lax.broadcasted_iota(jnp.int32, mass.shape, 0)
    mass_live = jnp.where(slot_index < active_counts[0][None], mass, 0.0)
    motion = jnp.concatenate([offsets, velocity, mass_live[None]], axis=0).transpose(2, 0, 1, 3)
    entropy = entropy.transpose(1, 0, 2)
    limits = (slots, slots // 2, slots // 4)
    pressure = None
    ends_m, ends_p, sizes_m, sizes_p = [], [], [], []
    left_m, right_m, left_p, right_p = [], [], [], []
    made = first_ends(motion)
    place, meta = ranks(targets.reshape(slots * columns, width), parts)
    for level in range(levels):
        limit = limits[level]
        sent = limits[max(level - 1, 0)]
        ends_m.insert(0, swap_ends(*made))
        partial = own_part(DENSITY, motion, None, ends_m, [], limit, (0,))
        ends_m[0], partial = lax.optimization_barrier((ends_m[0], partial))
        plane = beside(ends_m[0], width)
        masses = (lambda c: [motion[c, 6]]) if level == 0 else (lambda c: [])
        cells = swap_columns(lambda c: [rows_of(motion[c, :3, :sent]), *masses(c), plane])
        sizes_m.insert(0, sent)
        left_m.insert(0, cells[0])
        right_m.insert(0, cells[1])
        partial = own_part(DENSITY, motion, None, ends_m, [], limit, (-1, 1), partial)
        pressure, *made = density_rest(motion, partial, (left_m, right_m), sizes_m, pressure, entropy, active_counts, level, limit, limit)
        ends_p.insert(0, swap_ends(*made))
        partial = own_part(FORCE, motion, pressure, ends_m, ends_p, limit, (0,))
        ends_p[0], partial = lax.optimization_barrier((ends_p[0], partial))
        plane = beside(ends_p[0], width)
        cells = swap_columns(lambda c: [rows_of(pressure[c, :, :limit]), plane, rows_of(motion[c, 3:6, :sent])])
        sizes_p.insert(0, limit)
        left_p.insert(0, cells[0])
        right_p.insert(0, cells[1])
        partial = own_part(FORCE, motion, pressure, ends_m, ends_p, limit, (-1, 1), partial)
        more = limit if level < levels - 1 else 0
        motion, *made = force_rest(
            motion, pressure, partial, (left_m, right_m), (left_p, right_p), sizes_m, sizes_p, active_counts, level, limit, more
        )
    capacity = 3 * slots * columns * width // 8
    lists = compact(motion, pressure, place, meta[:, : 3 * parts], parts, capacity)
    arrived = lax.all_to_all(lists, "sub", split_axis=0, concat_axis=0, tiled=True)
    return arrived.transpose(1, 0, 2).reshape(8, parts * capacity)


def solution(mesh):
    placed = (
        P(None, None, "tile", "sub"),
        P(None, None, "tile", "sub"),
        P(None, "tile", "sub"),
        P(None, "tile", "sub"),
        P(None, "tile", "sub"),
        P(None, "tile", "sub"),
    )
    return jax.shard_map(
        shards, mesh=mesh, in_specs=placed, out_specs=P(None, ("tile", "sub")), check_vma=False
    )
```

```python
import functools
import math

import jax
import jax.numpy as jnp
from jax import lax
from jax.experimental import pallas as pl
from jax.experimental.pallas import tpu as pltpu
from jax.sharding import PartitionSpec as P

KERNEL_NORM = 21.0 / (2.0 * math.pi)
GAMMA = 5.0 / 3.0
TIME_STEP = 0.05
SOFTEN = 0.01
LANES = 128
ROWS = 8
VMEM = pl.BlockSpec(memory_space=pltpu.VMEM)
SMEM = pl.BlockSpec(memory_space=pltpu.SMEM)
PARAMS = pltpu.CompilerParams(vmem_limit_bytes=40 << 20)
MOTION, PRESSURE = 7, 3
SHIFTS = (-1, 0, 1)


def lane_of(shape):
    return lax.broadcasted_iota(jnp.int32, shape, 1)


def cost(pairs, ops):
    return pl.CostEstimate(flops=int(pairs * ops * 15), bytes_accessed=1 << 20, transcendentals=0)


def force_core(own, their):
    xi, yi, zi, ui, vi, wi, qi, ci, ri = own[:9]
    xj, yj, zj, uj, vj, wj, qj, cj, rj = their[:9]
    dx, dy, dz = xi - xj, yi - yj, zi - zj
    squared = dx * dx + dy * dy + dz * dz
    radius = squared * lax.rsqrt(jnp.maximum(squared, 1e-30))
    remain = jnp.maximum(1.0 - radius, 0.0)
    approach = dx * (ui - uj) + dy * (vi - vj) + dz * (wi - wj)
    closing = jnp.minimum(approach, 0.0) * pl.reciprocal(squared + SOFTEN, approx=True)
    viscous = closing * (closing - (ci + cj)) * pl.reciprocal(ri + rj, approx=True)
    return (dx, dy, dz), (qi + qj + viscous), remain


def density_core(own, their):
    xi, yi, zi = own[:3]
    xj, yj, zj = their[:3]
    dx, dy, dz = xi - xj, yi - yj, zi - zj
    squared = dx * dx + dy * dy + dz * dz
    radius = squared * lax.rsqrt(jnp.maximum(squared, 1e-30))
    return jnp.maximum(1.0 - radius, 0.0)


def pair_force(own, their, total):
    delta, pressure, remain = force_core(own, their)
    strength = pressure * ((remain * remain) * (remain * their[-1]))
    return tuple(t + strength * d for t, d in zip(total, delta))


def pair_density(own, their, total):
    remain = density_core(own, their)
    square = remain * remain
    return (total[0] + (square * square) * ((5.0 - 4.0 * remain) * their[-1]),)


def both_force(own, their, total):
    delta, pressure, remain = force_core(own, their)
    strength = pressure * ((remain * remain) * remain)
    on_own, on_their = strength * their[-1], strength * own[-1]
    return tuple(t + on_own * d for t, d in zip(total, delta)), tuple(on_their * d for d in delta)


def both_density(own, their, total):
    remain = density_core(own, their)
    square = remain * remain
    weight = (square * square) * (5.0 - 4.0 * remain)
    return (total[0] + weight * their[-1],), (weight * own[-1],)


DENSITY = ((0, 1.0), (1, 1.0), (2, 1.0)), (), ((6, KERNEL_NORM),), pair_density, 1
FORCE = (
    tuple((c, 1.0) for c in range(3)) + tuple((c, 4.0) for c in range(3, 6)),
    ((0, 1.0), (1, 1.0), (2, 4.0)),
    ((6, 20.0 * KERNEL_NORM),),
    pair_force,
    3,
)


def fill_shifted(shifted, col, row, pieces, scale, group, shifts, is_y):
    for cells, left, right, lo, hi in pieces:
        count = cells.shape[-1] // LANES
        blocks = [cells[lo:hi, b * LANES : (b + 1) * LANES] for b in range(count)]
        if scale != 1.0:
            blocks = [v * scale for v in blocks]
        lane = lane_of(blocks[0].shape)
        for at, shift in enumerate(shifts):
            values = blocks
            if shift == -1:
                turned = [pltpu.roll(v, 1, 1) for v in blocks]
                end = pltpu.roll(left[lo:hi, :], (LANES - group) % LANES, 1) if group else left[lo:hi, :]
                turned = [end if scale == 1.0 else end * scale] + turned
                values = [jnp.where(lane == 0, turned[b], turned[b + 1]) for b in range(count)]
            elif shift == 1:
                turned = [pltpu.roll(v, LANES - 1, 1) for v in blocks]
                end = pltpu.roll(right[lo:hi, :], LANES - 1 - group, 1)
                turned.append(end if scale == 1.0 else end * scale)
                values = [jnp.where(lane == LANES - 1, turned[b + 1], turned[b]) for b in range(count)]
            if is_y and shift:
                values = [v + float(shift) for v in values]
            for b in range(count):
                shifted[col, at, b, row, lo:hi, :] = values[b]


def fill_column(shifted, col, kind, motion, pressure, group_of, shifts):
    moved, pressed, massed, _, _ = kind
    row = 0
    for pieces, fields in ((motion, moved), (pressure, pressed), (motion, massed)):
        for field, scale in fields:
            is_y = fields is moved and field == 1
            fill_shifted(shifted, col, row, pieces(field), scale, group_of(field), shifts, is_y)
            row += 1


def add_pairs(kind, motion_ref, pressure_ref, shifted, x, sources, limit, first, last):
    moved, pressed, _, pair, width = kind
    slots = shifted.shape[-2]
    blocks = shifted.shape[2]
    rows = shifted.shape[3]
    group = min(limit // ROWS, 2 if width == 3 else 4)
    unroll = min(slots, 16 // group if width == 3 else 32 // group)
    forms = shifted.shape[1]
    low_col, low_shift = sources[0]

    def lane_block(b, carry):
        lanes = pl.ds(pl.multiple_of(b * LANES, LANES), LANES)
        for part in range(limit // (ROWS * group)):
            spans = [slice((part * group + v) * ROWS, (part * group + v + 1) * ROWS) for v in range(group)]
            own = []
            for span in spans:
                values = [motion_ref[x, f, span, lanes] * s if s != 1.0 else motion_ref[x, f, span, lanes] for f, s in moved]
                values += [pressure_ref[x, f, span, lanes] * s if s != 1.0 else pressure_ref[x, f, span, lanes] for f, s in pressed]
                own.append(values)

            def source(at, totals):
                col = at // forms
                shift = at - forms * col
                offset = (col + low_shift).astype(jnp.float32)
                mine = [[v[0] - offset] + v[1:] for v in own]

                def step(outer, totals):
                    totals = list(totals)
                    for inner in range(unroll):
                        slot = outer * unroll + inner
                        their = [
                            jnp.broadcast_to(shifted[col + low_col, shift, b, r, pl.ds(slot, 1), :], (ROWS, LANES))
                            for r in range(rows)
                        ]
                        for v in range(group):
                            totals[v] = pair(mine[v], their, totals[v])
                    return tuple(totals)

                return lax.fori_loop(0, slots // unroll, step, totals)

            totals = tuple(first(x, span, lanes) for span in spans)
            totals = lax.fori_loop(0, forms * len(sources), source, totals)
            for span, total in zip(spans, totals):
                last(x, span, lanes, total)
        return carry

    lax.fori_loop(0, blocks, lane_block, 0)


def own_sources(x, columns):
    return [(c, c - x) for c in range(columns) if abs(c - x) <= 1]


def pack_ends(field_of, fields, columns, left_ref, right_ref):
    for ref, at_last in ((left_ref, False), (right_ref, True)):
        lane = None
        packed = None
        for group in range(fields * columns):
            block = field_of(group // columns, group % columns, at_last)
            if lane is None:
                lane = lane_of(block.shape)
                packed = jnp.zeros(block.shape, jnp.float32)
            turn = (group + 1) % LANES if at_last else group
            packed = jnp.where(lane == group, pltpu.roll(block, turn, 1) if turn else block, packed)
        ref[...] = packed


def end_block(ref, column, field, at_last, limit):
    width = ref.shape[-1]
    lanes = slice(width - LANES, width) if at_last else slice(0, LANES)
    return ref[column, field, :limit, lanes]


def first_ends(motion):
    columns, _, slots, _ = motion.shape

    def kernel(motion_ref, left_ref, right_ref):
        pack_ends(
            lambda f, c, last: end_block(motion_ref, c, f, last, slots), MOTION, columns, left_ref, right_ref
        )

    ends = jax.ShapeDtypeStruct((slots, LANES), jnp.float32)
    return pl.pallas_call(kernel, out_shape=(ends, ends), in_specs=[VMEM], out_specs=(VMEM, VMEM), compiler_params=PARAMS)(motion)


def bounds_of(sizes):
    spans, lo = [], 0
    for index, hi in enumerate(sizes):
        if hi > lo:
            spans.append((index, lo, hi))
            lo = hi
    return spans


def own_part(kind, motion, pressure, ends_m, ends_p, limit, shifts, partial=None):
    columns, _, slots, width = motion.shape
    moved, pressed, massed, _, outs = kind
    inner = shifts == (0,)
    mutual = limit == slots
    if inner:
        ends_m = ends_p = []
    flat_m = [e for pair in ends_m for e in pair]
    flat_p = [e for pair in ends_p for e in pair]
    whole = [(0, 0, slots)]
    spans_m = whole if inner else bounds_of([e[0].shape[0] for e in ends_m])
    spans_p = whole if inner else bounds_of([e[0].shape[0] for e in ends_p])
    inputs = [motion] + ([pressure] if pressed else []) + flat_m + flat_p + ([] if partial is None else [partial])
    rows = len(moved) + len(pressed) + len(massed)

    def kernel(*refs):
        refs = list(refs)
        motion_ref = refs.pop(0)
        pressure_ref = refs.pop(0) if pressed else None
        m_refs = refs[: len(flat_m)]
        p_refs = refs[len(flat_m) : len(flat_m) + len(flat_p)]
        if mutual:
            *refs, parts, reaction, packed = refs
            mutual_refs = (parts, reaction, packed)
        partial_ref = None if partial is None else refs[-3]
        out_ref, shifted = refs[-2:]

        def pieces(cells, ends, spans):
            if inner:
                return [(cells, None, None, 0, slots)]
            return [(cells, ends[2 * i], ends[2 * i + 1], lo, hi) for i, lo, hi in spans]

        for c in range(columns):

            def motion_pieces(field):
                return pieces(motion_ref.at[c, field], m_refs, spans_m if field < 6 else [(len(ends_m) - 1, 0, slots)])

            def pressure_pieces(field):
                return pieces(pressure_ref.at[c, field], p_refs, spans_p)

            fill_column(shifted, c, kind, motion_pieces, pressure_pieces, lambda f: f * columns + c, shifts)
        zero = jnp.zeros((ROWS, LANES), jnp.float32)

        def first(x, span, lanes):
            if partial is None:
                return (zero,) * outs
            return tuple(partial_ref[x, k, span, lanes] for k in range(outs))

        def last(x, span, lanes, total):
            for k in range(outs):
                out_ref[x, k, span, lanes] = total[k]

        if not mutual:
            for x in range(columns):
                add_pairs(kind, motion_ref, pressure_ref, shifted, x, own_sources(x, columns), limit, first, last)
            return
        parts, reaction, packed = mutual_refs
        if inner:
            for x in range(columns):
                add_pairs(kind, motion_ref, pressure_ref, shifted, x, [(x, 0)], limit, first, last)
        else:
            out_ref[...] = partial_ref[...]
        edges = []
        for x in range(columns):
            for col in (x, x + 1):
                for shift in shifts:
                    if col == columns or (col == x and shift != 1):
                        continue
                    both_ways(kind, motion_ref, pressure_ref, shifted, x, col, shifts.index(shift), out_ref, parts, reaction)
                    take_reaction(out_ref, reaction, col, shift, outs)
                    if shift:
                        edges.append((col, x, -shift))
        if edges:
            edge_pairs(kind, motion_ref, pressure_ref, shifted, shifts, edges, out_ref, packed)

    return pl.pallas_call(
        kernel,
        out_shape=jax.ShapeDtypeStruct((columns, outs, limit, width), jnp.float32),
        in_specs=[VMEM] * len(inputs),
        out_specs=VMEM,
        scratch_shapes=[pltpu.VMEM((columns, len(shifts), width // LANES, rows, slots, LANES), jnp.float32)]
        + (
            [
                pltpu.VMEM((outs, slots, ROWS, LANES), jnp.float32),
                pltpu.VMEM((outs, width // LANES, slots, LANES), jnp.float32),
                pltpu.VMEM((rows, slots, LANES), jnp.float32),
            ]
            if mutual
            else []
        ),
        compiler_params=PARAMS,
        cost_estimate=cost(limit * slots * len(shifts) * (3 * columns - 2) * width, 60 if outs == 3 else 30),
    )(*inputs)


def sum_rows(values):
    row = lax.broadcasted_iota(jnp.int32, (ROWS, LANES), 0)
    step = 1
    while len(values) > 1:
        low = lax.bitwise_and(row, step) == 0
        values = [
            jnp.where(low, a, b) + pltpu.roll(jnp.where(low, b, a), step, 0) for a, b in zip(values[::2], values[1::2])
        ]
        step *= 2
    return values[0]


def own_rows(kind, motion_ref, pressure_ref, x, span, lanes):
    moved, pressed, massed = kind[:3]
    rows = [(motion_ref, f, s) for f, s in moved] + [(pressure_ref, f, s) for f, s in pressed] + [(motion_ref, f, s) for f, s in massed]
    return [ref[x, f, span, lanes] * s if s != 1.0 else ref[x, f, span, lanes] for ref, f, s in rows]


def both_ways(kind, motion_ref, pressure_ref, shifted, x, col, form, sums, parts, reaction):
    outs = kind[4]
    slots, blocks, rows = shifted.shape[-2], shifted.shape[2], shifted.shape[3]
    both = both_force if outs == 3 else both_density
    sign = -1.0 if outs == 3 else 1.0
    group = 2 if outs == 3 else 4
    unroll = 8

    def lane_block(b, carry):
        lanes = pl.ds(pl.multiple_of(b * LANES, LANES), LANES)
        for part in range(slots // (ROWS * group)):
            spans = [slice((part * group + v) * ROWS, (part * group + v + 1) * ROWS) for v in range(group)]
            mine = []
            for span in spans:
                values = own_rows(kind, motion_ref, pressure_ref, x, span, lanes)
                mine.append([values[0] - float(col - x)] + values[1:])

            def step(outer, totals):
                totals = list(totals)
                for inner in range(unroll):
                    slot = outer * unroll + inner
                    their = [jnp.broadcast_to(shifted[col, form, b, r, pl.ds(slot, 1), :], (ROWS, LANES)) for r in range(rows)]
                    back = None
                    for v in range(group):
                        totals[v], given = both(mine[v], their, totals[v])
                        back = given if back is None else tuple(p + q for p, q in zip(back, given))
                    for k in range(outs):
                        parts[k, slot] = back[k] if part == 0 else parts[k, slot] + back[k]
                return tuple(totals)

            totals = tuple(tuple(sums[x, k, span, lanes] for k in range(outs)) for span in spans)
            totals = lax.fori_loop(0, slots // unroll, step, totals)
            for span, total in zip(spans, totals):
                for k in range(outs):
                    sums[x, k, span, lanes] = total[k]
        for k in range(outs):
            for lo in range(0, slots, ROWS):
                reaction[k, b, lo : lo + ROWS, :] = sign * sum_rows([parts[k, lo + r] for r in range(ROWS)])
        return carry

    lax.fori_loop(0, blocks, lane_block, 0)


def take_reaction(sums, reaction, col, shift, outs):
    blocks, slots = reaction.shape[1], reaction.shape[2]
    lane = lane_of((slots, LANES))
    for k in range(outs):
        values = [reaction[k, b] for b in range(blocks)]
        if shift == 1:
            turned = [jnp.zeros((slots, LANES), jnp.float32)] + [pltpu.roll(v, 1, 1) for v in values]
            values = [jnp.where(lane == 0, turned[b], turned[b + 1]) for b in range(blocks)]
        elif shift == -1:
            turned = [pltpu.roll(v, LANES - 1, 1) for v in values] + [jnp.zeros((slots, LANES), jnp.float32)]
            values = [jnp.where(lane == LANES - 1, turned[b + 1], turned[b]) for b in range(blocks)]
        for b in range(blocks):
            lanes = slice(b * LANES, (b + 1) * LANES)
            sums[col, k, :, lanes] = sums[col, k, :, lanes] + values[b]


def edge_pairs(kind, motion_ref, pressure_ref, shifted, forms, edges, sums, packed):
    pair, outs = kind[3], kind[4]
    slots, blocks, rows = shifted.shape[-2], shifted.shape[2], shifted.shape[3]
    lane = lane_of((ROWS, LANES))
    width = blocks * LANES
    tall = lane_of((slots, LANES))
    for r in range(rows):
        value = jnp.zeros((slots, LANES), jnp.float32)
        for q, (x, col, shift) in enumerate(edges):
            block, turn = (0, q) if shift == -1 else (blocks - 1, q + 1)
            value = jnp.where(tall == q, pltpu.roll(shifted[col, forms.index(shift), block, r], turn, 1), value)
        packed[r] = value
    spans = [slice(lo, lo + ROWS) for lo in range(0, slots, ROWS)]
    group = 2 if outs == 3 else 4
    unroll = 8
    for part in range(len(spans) // group):
        mine = []
        for span in spans[part * group : (part + 1) * group]:
            values = None
            for q, (x, col, shift) in enumerate(edges):
                lanes, turn = (slice(0, LANES), q) if shift == -1 else (slice(width - LANES, width), q + 1)
                cell = own_rows(kind, motion_ref, pressure_ref, x, span, lanes)
                cell = [pltpu.roll(v, turn, 1) if turn else v for v in cell]
                cell[0] = cell[0] - float(col - x)
                values = cell if values is None else [jnp.where(lane == q, c, v) for c, v in zip(cell, values)]
            mine.append(values)

        def step(outer, totals):
            totals = list(totals)
            for inner in range(unroll):
                slot = outer * unroll + inner
                their = [jnp.broadcast_to(packed[r, pl.ds(slot, 1), :], (ROWS, LANES)) for r in range(rows)]
                for v in range(group):
                    totals[v] = pair(mine[v], their, totals[v])
            return tuple(totals)

        zero = jnp.zeros((ROWS, LANES), jnp.float32)
        totals = lax.fori_loop(0, slots // unroll, step, tuple((zero,) * outs for _ in range(group)))
        for v, span in enumerate(spans[part * group : (part + 1) * group]):
            for k in range(outs):
                for q, (x, col, shift) in enumerate(edges):
                    at = 0 if shift == -1 else LANES - 1
                    lanes = slice(0, LANES) if shift == -1 else slice(width - LANES, width)
                    back = pltpu.roll(totals[v][k], (at - q) % LANES, 1) if at != q else totals[v][k]
                    sums[x, k, span, lanes] = sums[x, k, span, lanes] + jnp.where(lane == at, back, 0.0)


def halo_sums(kind, refs, columns, slots, limit, first, last, motion_ref, pressure_ref, shifted, sizes_m, sizes_p):
    spans_m, spans_p = bounds_of(sizes_m), bounds_of(sizes_p)
    for side in range(2):
        m_refs, p_refs = refs[side]
        column = columns - 1 if side == 0 else 0

        def field_of(ref, at, size):
            return ref.at[at : at + size]

        def piece(cells, ends, lo, hi):
            return (cells, ends.at[:, 0:LANES], ends.at[:, LANES : 2 * LANES], lo, hi)

        def motion_pieces(field):
            out = []
            for i, lo, hi in spans_m if field < 6 else [(len(sizes_m) - 1, 0, slots)]:
                size = sizes_m[i]
                ends = field_of(m_refs[i], (4 if i == len(sizes_m) - 1 else 3) * size, size)
                if field < 3 or field == 6:
                    cells = field_of(m_refs[i], min(field, 3) * size, size)
                else:
                    cells = field_of(p_refs[i], 4 * sizes_p[i] + (field - 3) * size, size)
                out.append(piece(cells, ends, lo, hi))
            return out

        def pressure_pieces(field):
            return [
                piece(field_of(p_refs[i], field * sizes_p[i], sizes_p[i]), field_of(p_refs[i], 3 * sizes_p[i], sizes_p[i]), lo, hi)
                for i, lo, hi in spans_p
            ]

        fill_column(shifted, side, kind, motion_pieces, pressure_pieces, lambda f: f * columns + column, SHIFTS)
        x, shift = (0, -1) if side == 0 else (columns - 1, 1)
        add_pairs(kind, motion_ref, pressure_ref, shifted, x, [(side, shift)], limit, first, last)


def density_rest(motion, partial, messages, sizes, density, entropy, counts, level, limit, slots_sent):
    columns, _, slots, width = motion.shape
    (m_left, m_right) = messages
    first = density is None
    inputs = [motion, partial, entropy, counts] + ([] if first else [density]) + m_left + m_right
    n_in, n_m = len(inputs), len(m_left)
    rows = 4

    def kernel(*refs):
        motion_ref, partial_ref, entropy_ref, counts_ref = refs[:4]
        old_ref = None if first else refs[4]
        m_refs = refs[n_in - 2 * n_m : n_in]
        press_ref, left_ref, right_ref, shifted, sums = refs[n_in:]
        sums[...] = partial_ref[...]

        def start(x, span, lanes):
            return (sums[x, 0, span, lanes],)

        def end(x, span, lanes, total):
            sums[x, 0, span, lanes] = total[0]

        sides = ((m_refs[:n_m], []), (m_refs[n_m:], []))
        halo_sums(DENSITY, sides, columns, slots, limit, start, end, motion_ref, None, shifted, sizes, [])
        for x in range(columns):
            count = counts_ref[level, x : x + 1, :]
            for lo in range(0, slots, ROWS):
                span = slice(lo, lo + ROWS)
                if lo >= limit:
                    if first:
                        value = jnp.ones((ROWS, width), jnp.float32)
                    else:
                        for f in range(3):
                            press_ref[x, f, span, :] = old_ref[x, f, span, :]
                        continue
                else:
                    slot = lax.broadcasted_iota(jnp.int32, (ROWS, width), 0) + lo
                    before = jnp.ones((ROWS, width), jnp.float32) if first else old_ref[x, 2, span, :]
                    value = jnp.where(slot < count, sums[x, 0, span, :], before)
                pressure = entropy_ref[x, span, :] * jnp.exp(jnp.log(value) * (GAMMA - 2.0))
                press_ref[x, 0, span, :] = pressure
                press_ref[x, 1, span, :] = jnp.sqrt(GAMMA * pressure * value)
                press_ref[x, 2, span, :] = value
        pack_ends(lambda f, c, last: end_block(press_ref, c, f, last, slots_sent), PRESSURE, columns, left_ref, right_ref)

    ends = jax.ShapeDtypeStruct((slots_sent, LANES), jnp.float32)
    return pl.pallas_call(
        kernel,
        out_shape=(jax.ShapeDtypeStruct((columns, PRESSURE, slots, width), jnp.float32), ends, ends),
        in_specs=[VMEM] * n_in,
        out_specs=(VMEM,) * 3,
        scratch_shapes=[
            pltpu.VMEM((2, 3, width // LANES, rows, slots, LANES), jnp.float32),
            pltpu.VMEM((columns, 1, limit, width), jnp.float32),
        ],
        compiler_params=PARAMS,
        cost_estimate=cost(limit * slots * 6 * width, 30),
    )(*inputs)


def force_rest(motion, pressure, partial, messages_m, messages_p, sizes_m, sizes_p, counts, level, limit, slots_sent):
    columns, _, slots, width = motion.shape
    n_m, n_p = len(messages_m[0]), len(messages_p[0])
    inputs = [motion, pressure, partial, counts] + messages_m[0] + messages_p[0] + messages_m[1] + messages_p[1]
    n_in = len(inputs)
    rows = 10
    ends = jax.ShapeDtypeStruct((slots_sent, LANES), jnp.float32)
    outs = (jax.ShapeDtypeStruct(motion.shape, jnp.float32),) + ((ends, ends) if slots_sent else ())

    def kernel(*refs):
        motion_ref, pressure_ref, partial_ref, counts_ref = refs[:4]
        sides = []
        for side in range(2):
            at = 4 + side * (n_m + n_p)
            sides.append((refs[at : at + n_m], refs[at + n_m : at + n_m + n_p]))
        new_ref = refs[n_in]
        shifted, sums = refs[-2:]
        sums[...] = partial_ref[...]

        def start(x, span, lanes):
            return tuple(sums[x, k, span, lanes] for k in range(3))

        def end(x, span, lanes, total):
            for k in range(3):
                sums[x, k, span, lanes] = total[k]

        halo_sums(
            FORCE, sides, columns, slots, limit, start, end, motion_ref, pressure_ref, shifted, sizes_m, sizes_p
        )
        for x in range(columns):
            count = counts_ref[level, x : x + 1, :]
            new_ref[x, 6, :, :] = motion_ref[x, 6, :, :]
            if limit < slots:
                for f in range(6):
                    new_ref[x, f, limit:, :] = motion_ref[x, f, limit:, :]
            for lo in range(0, limit, ROWS):
                span = slice(lo, lo + ROWS)
                active = lax.broadcasted_iota(jnp.int32, (ROWS, width), 0) + lo < count
                for k in range(3):
                    place, speed = motion_ref[x, k, span, :], motion_ref[x, 3 + k, span, :]
                    faster = speed + TIME_STEP * sums[x, k, span, :]
                    new_ref[x, 3 + k, span, :] = jnp.where(active, faster, speed)
                    new_ref[x, k, span, :] = jnp.where(active, place + TIME_STEP * faster, place)
        if slots_sent:
            left_ref, right_ref = refs[n_in + 1 : n_in + 3]
            pack_ends(lambda f, c, last: end_block(new_ref, c, f, last, slots_sent), 6, columns, left_ref, right_ref)

    made = pl.pallas_call(
        kernel,
        out_shape=outs,
        in_specs=[VMEM] * n_in,
        out_specs=(VMEM,) * len(outs),
        scratch_shapes=[
            pltpu.VMEM((2, 3, width // LANES, rows, slots, LANES), jnp.float32),
            pltpu.VMEM((columns, 3, limit, width), jnp.float32),
        ],
        compiler_params=PARAMS,
        cost_estimate=cost(limit * slots * 6 * width, 60),
    )(*inputs)
    return made if slots_sent else (made[0], None, None)


def ranks(destination, parts):
    rows, width = destination.shape

    def kernel(dest_ref, place_ref, meta_ref):
        dest = dest_ref[...]
        low = lax.broadcasted_iota(jnp.int32, (width, width), 0)
        upto = jnp.where(low <= lane_of((width, width)), 1.0, 0.0).astype(jnp.bfloat16)
        above = lax.broadcasted_iota(jnp.int32, (rows, rows), 0) > lane_of((rows, rows))
        above = jnp.where(above, 1.0, 0.0).astype(jnp.bfloat16)
        lane = lane_of((rows, LANES))
        meta = jnp.zeros((rows, LANES), jnp.float32)
        place = jnp.zeros((rows, width), jnp.float32)
        start = jnp.zeros((rows, 1), jnp.float32)
        for d in range(parts):
            mask = jnp.where(dest == d, 1.0, 0.0)
            inside = jnp.dot(mask.astype(jnp.bfloat16), upto, preferred_element_type=jnp.float32)
            count = inside[:, width - 1 : width]
            wide = jnp.broadcast_to(count, (rows, LANES))
            before = jnp.dot(above, wide.astype(jnp.bfloat16), preferred_element_type=jnp.float32)
            place = place + mask * (inside - 1.0 + start)
            meta = jnp.where(lane == d, before, meta)
            meta = jnp.where(lane == parts + d, jnp.broadcast_to(start, (rows, LANES)), meta)
            meta = jnp.where(lane == 2 * parts + d, before + wide, meta)
            start = start + count
        place_ref[...] = place.astype(jnp.int32)
        meta_ref[...] = meta.astype(jnp.int32)

    return pl.pallas_call(
        kernel,
        out_shape=(jax.ShapeDtypeStruct((rows, width), jnp.int32), jax.ShapeDtypeStruct((rows, LANES), jnp.int32)),
        in_specs=[VMEM],
        out_specs=(VMEM, VMEM),
        compiler_params=PARAMS,
    )(destination)


def compact(motion, pressure, place, meta, parts, capacity):
    columns, _, slots, width = motion.shape
    chunks = width // LANES
    total = -(-capacity // LANES)

    def kernel(motion_ref, pressure_ref, place_ref, meta_ref, out_ref, local, lists):
        lane = lane_of((ROWS, LANES))

        def do_group(group, carry):
            span = pl.ds(pl.multiple_of(group * ROWS, ROWS), ROWS)
            fields = [
                [motion_ref[x, f, span, :] for f in range(6)] + [pressure_ref[x, 2, span, :], motion_ref[x, 6, span, :]]
                for x in range(columns)
            ]
            for s in range(ROWS):
                for x in range(columns):
                    state = jnp.concatenate([v[s : s + 1, :] for v in fields[x]], axis=0)
                    high = state.astype(jnp.bfloat16).astype(jnp.float32)
                    rest = state - high
                    middle = rest.astype(jnp.bfloat16).astype(jnp.float32)
                    lowest = rest - middle
                    stacked = jnp.concatenate([high, middle, lowest], axis=0).astype(jnp.bfloat16)
                    row = (group * ROWS + s) * columns + x
                    wanted = place_ref[pl.ds(row, 1), :]
                    hot = jnp.where(lax.broadcasted_iota(jnp.int32, (width, width), 0) == wanted, 1.0, 0.0)
                    moved = lax.dot_general(
                        stacked, hot.astype(jnp.bfloat16), (((1,), (1,)), ((), ())), preferred_element_type=jnp.float32
                    )
                    moved = moved[0:8] + moved[8:16] + moved[16:24]
                    buffer = (s * columns + x) % 4
                    for c in range(chunks):
                        local[buffer, c + 1] = moved[:, c * LANES : (c + 1) * LANES]
                    for d in range(parts):
                        base = meta_ref[row, d]
                        begin = meta_ref[row, parts + d]
                        chunk = lax.shift_right_logical(base, 7)
                        off = lax.bitwise_and(base, LANES - 1)
                        turn = lax.bitwise_and(off - begin, LANES - 1)
                        at = lax.shift_right_logical(begin, 7)
                        at = at + jnp.where(off < lax.bitwise_and(begin, LANES - 1), 1, 0)
                        turned = [pltpu.roll(local[buffer, at + k], turn, 1) for k in range(chunks + 2)]
                        for k in range(chunks + 1):
                            value = jnp.where(lane >= turn, turned[k + 1], turned[k])
                            if k == 0:
                                value = jnp.where(lane >= off, value, lists[d, chunk])
                            lists[d, chunk + k] = value
            return carry

        lax.fori_loop(0, slots // ROWS, do_group, 0)
        for d in range(parts):
            count = meta_ref[slots * columns - 1, 2 * parts + d]
            for c in range(total):
                out_ref[d, :, c * LANES : (c + 1) * LANES] = jnp.where(lane + c * LANES < count, lists[d, c], 0.0)

    return pl.pallas_call(
        kernel,
        out_shape=jax.ShapeDtypeStruct((parts, 8, capacity), jnp.float32),
        in_specs=[VMEM, VMEM, VMEM, SMEM],
        out_specs=VMEM,
        scratch_shapes=[
            pltpu.VMEM((4, 2 * chunks + 4, ROWS, LANES), jnp.float32),
            pltpu.VMEM((parts, total + chunks + 2, ROWS, LANES), jnp.float32),
        ],
        compiler_params=PARAMS,
    )(motion, pressure, place, meta)


def pass_on(value, axis, step):
    count = lax.axis_size(axis)
    return lax.ppermute(value, axis, [(i, (i + step) % count) for i in range(count)])


def swap_ends(left_ends, right_ends):
    return pass_on(right_ends, "sub", 1), pass_on(left_ends, "sub", -1)


def swap_columns(parts_of):
    first = jnp.concatenate(parts_of(0), axis=0)
    final = jnp.concatenate(parts_of(-1), axis=0)
    return pass_on(final, "tile", 1), pass_on(first, "tile", -1)


def rows_of(fields):
    return fields.reshape(-1, fields.shape[-1])


def beside(ends, width):
    plane = jnp.concatenate(ends, axis=1)
    return jnp.pad(plane, ((0, 0), (0, width - plane.shape[1])))


def shards(offsets, velocity, mass, entropy, active_counts, targets):
    slots, columns, width = mass.shape
    levels = active_counts.shape[0]
    parts = lax.axis_size("sub")
    slot_index = lax.broadcasted_iota(jnp.int32, mass.shape, 0)
    mass_live = jnp.where(slot_index < active_counts[0][None], mass, 0.0)
    motion = jnp.concatenate([offsets, velocity, mass_live[None]], axis=0).transpose(2, 0, 1, 3)
    entropy = entropy.transpose(1, 0, 2)
    limits = (slots, slots // 2, slots // 4)
    pressure = None
    ends_m, ends_p, sizes_m, sizes_p = [], [], [], []
    left_m, right_m, left_p, right_p = [], [], [], []
    made = first_ends(motion)
    place, meta = ranks(targets.reshape(slots * columns, width), parts)
    for level in range(levels):
        limit = limits[level]
        sent = limits[max(level - 1, 0)]
        ends_m.insert(0, swap_ends(*made))
        partial = own_part(DENSITY, motion, None, ends_m, [], limit, (0,))
        ends_m[0], partial = lax.optimization_barrier((ends_m[0], partial))
        plane = beside(ends_m[0], width)
        masses = (lambda c: [motion[c, 6]]) if level == 0 else (lambda c: [])
        cells = swap_columns(lambda c: [rows_of(motion[c, :3, :sent]), *masses(c), plane])
        sizes_m.insert(0, sent)
        left_m.insert(0, cells[0])
        right_m.insert(0, cells[1])
        partial = own_part(DENSITY, motion, None, ends_m, [], limit, (-1, 1), partial)
        pressure, *made = density_rest(motion, partial, (left_m, right_m), sizes_m, pressure, entropy, active_counts, level, limit, limit)
        ends_p.insert(0, swap_ends(*made))
        partial = own_part(FORCE, motion, pressure, ends_m, ends_p, limit, (0,))
        ends_p[0], partial = lax.optimization_barrier((ends_p[0], partial))
        plane = beside(ends_p[0], width)
        cells = swap_columns(lambda c: [rows_of(pressure[c, :, :limit]), plane, rows_of(motion[c, 3:6, :sent])])
        sizes_p.insert(0, limit)
        left_p.insert(0, cells[0])
        right_p.insert(0, cells[1])
        partial = own_part(FORCE, motion, pressure, ends_m, ends_p, limit, (-1, 1), partial)
        more = limit if level < levels - 1 else 0
        motion, *made = force_rest(
            motion, pressure, partial, (left_m, right_m), (left_p, right_p), sizes_m, sizes_p, active_counts, level, limit, more
        )
    capacity = 3 * slots * columns * width // 8
    lists = compact(motion, pressure, place, meta[:, : 3 * parts], parts, capacity)
    arrived = lax.all_to_all(lists, "sub", split_axis=0, concat_axis=0, tiled=True)
    return arrived.transpose(1, 0, 2).reshape(8, parts * capacity)


def solution(mesh):
    placed = (
        P(None, None, "tile", "sub"),
        P(None, None, "tile", "sub"),
        P(None, "tile", "sub"),
        P(None, "tile", "sub"),
        P(None, "tile", "sub"),
        P(None, "tile", "sub"),
    )
    return jax.shard_map(
        shards, mesh=mesh, in_specs=placed, out_specs=P(None, ("tile", "sub")), check_vma=False
    )
```

```python
import functools
import math

import jax
import jax.numpy as jnp
from jax import lax
from jax.experimental import pallas as pl
from jax.experimental.pallas import tpu as pltpu
from jax.sharding import PartitionSpec as P

KERNEL_NORM = 21.0 / (2.0 * math.pi)
GAMMA = 5.0 / 3.0
TIME_STEP = 0.05
SOFTEN = 0.01
LANES = 128
ROWS = 8
VMEM = pl.BlockSpec(memory_space=pltpu.VMEM)
SMEM = pl.BlockSpec(memory_space=pltpu.SMEM)
PARAMS = pltpu.CompilerParams(vmem_limit_bytes=40 << 20)
MOTION, PRESSURE = 7, 3
SHIFTS = (-1, 0, 1)


def lane_of(shape):
    return lax.broadcasted_iota(jnp.int32, shape, 1)


def cost(pairs, ops):
    return pl.CostEstimate(flops=int(pairs * ops * 15), bytes_accessed=1 << 20, transcendentals=0)


def force_core(own, their):
    xi, yi, zi, ui, vi, wi, qi, ci, ri = own[:9]
    xj, yj, zj, uj, vj, wj, qj, cj, rj = their[:9]
    dx, dy, dz = xi - xj, yi - yj, zi - zj
    squared = dx * dx + dy * dy + dz * dz
    radius = squared * lax.rsqrt(jnp.maximum(squared, 1e-30))
    remain = jnp.maximum(1.0 - radius, 0.0)
    approach = dx * (ui - uj) + dy * (vi - vj) + dz * (wi - wj)
    closing = jnp.minimum(approach, 0.0) * pl.reciprocal(squared + SOFTEN, approx=True)
    viscous = closing * (closing - (ci + cj)) * pl.reciprocal(ri + rj, approx=True)
    return (dx, dy, dz), (qi + qj + viscous), remain


def density_core(own, their):
    xi, yi, zi = own[:3]
    xj, yj, zj = their[:3]
    dx, dy, dz = xi - xj, yi - yj, zi - zj
    squared = dx * dx + dy * dy + dz * dz
    radius = squared * lax.rsqrt(jnp.maximum(squared, 1e-30))
    return jnp.maximum(1.0 - radius, 0.0)


def pair_force(own, their, total):
    delta, pressure, remain = force_core(own, their)
    strength = pressure * ((remain * remain) * (remain * their[-1]))
    return tuple(t + strength * d for t, d in zip(total, delta))


def pair_density(own, their, total):
    remain = density_core(own, their)
    square = remain * remain
    return (total[0] + (square * square) * ((5.0 - 4.0 * remain) * their[-1]),)


def both_force(own, their, total):
    delta, pressure, remain = force_core(own, their)
    strength = pressure * ((remain * remain) * remain)
    on_own, on_their = strength * their[-1], strength * own[-1]
    return tuple(t + on_own * d for t, d in zip(total, delta)), tuple(on_their * d for d in delta)


def both_density(own, their, total):
    remain = density_core(own, their)
    square = remain * remain
    weight = (square * square) * (5.0 - 4.0 * remain)
    return (total[0] + weight * their[-1],), (weight * own[-1],)


DENSITY = ((0, 1.0), (1, 1.0), (2, 1.0)), (), ((6, KERNEL_NORM),), pair_density, 1
FORCE = (
    tuple((c, 1.0) for c in range(3)) + tuple((c, 4.0) for c in range(3, 6)),
    ((0, 1.0), (1, 1.0), (2, 4.0)),
    ((6, 20.0 * KERNEL_NORM),),
    pair_force,
    3,
)


def fill_shifted(shifted, col, row, pieces, scale, group, shifts, is_y):
    for cells, left, right, lo, hi in pieces:
        count = cells.shape[-1] // LANES
        blocks = [cells[lo:hi, b * LANES : (b + 1) * LANES] for b in range(count)]
        if scale != 1.0:
            blocks = [v * scale for v in blocks]
        lane = lane_of(blocks[0].shape)
        for at, shift in enumerate(shifts):
            values = blocks
            if shift == -1:
                turned = [pltpu.roll(v, 1, 1) for v in blocks]
                end = pltpu.roll(left[lo:hi, :], (LANES - group) % LANES, 1) if group else left[lo:hi, :]
                turned = [end if scale == 1.0 else end * scale] + turned
                values = [jnp.where(lane == 0, turned[b], turned[b + 1]) for b in range(count)]
            elif shift == 1:
                turned = [pltpu.roll(v, LANES - 1, 1) for v in blocks]
                end = pltpu.roll(right[lo:hi, :], LANES - 1 - group, 1)
                turned.append(end if scale == 1.0 else end * scale)
                values = [jnp.where(lane == LANES - 1, turned[b + 1], turned[b]) for b in range(count)]
            if is_y and shift:
                values = [v + float(shift) for v in values]
            for b in range(count):
                shifted[col, at, b, row, lo:hi, :] = values[b]


def fill_column(shifted, col, kind, motion, pressure, group_of, shifts):
    moved, pressed, massed, _, _ = kind
    row = 0
    for pieces, fields in ((motion, moved), (pressure, pressed), (motion, massed)):
        for field, scale in fields:
            is_y = fields is moved and field == 1
            fill_shifted(shifted, col, row, pieces(field), scale, group_of(field), shifts, is_y)
            row += 1


def add_pairs(kind, motion_ref, pressure_ref, shifted, x, sources, limit, first, last, start=0):
    moved, pressed, _, pair, width = kind
    slots = shifted.shape[-2]
    blocks = shifted.shape[2]
    rows = shifted.shape[3]
    group = min(limit // ROWS, 2 if width == 3 else 4)
    unroll = min(slots - start, 16 // group if width == 3 else 32 // group)
    forms = shifted.shape[1]
    low_col, low_shift = sources[0]

    def lane_block(b, carry):
        lanes = pl.ds(pl.multiple_of(b * LANES, LANES), LANES)
        for part in range(limit // (ROWS * group)):
            spans = [slice((part * group + v) * ROWS, (part * group + v + 1) * ROWS) for v in range(group)]
            own = []
            for span in spans:
                values = [motion_ref[x, f, span, lanes] * s if s != 1.0 else motion_ref[x, f, span, lanes] for f, s in moved]
                values += [pressure_ref[x, f, span, lanes] * s if s != 1.0 else pressure_ref[x, f, span, lanes] for f, s in pressed]
                own.append(values)

            def source(at, totals):
                col = at // forms
                shift = at - forms * col
                offset = (col + low_shift).astype(jnp.float32)
                mine = [[v[0] - offset] + v[1:] for v in own]

                def step(outer, totals):
                    totals = list(totals)
                    for inner in range(unroll):
                        slot = outer * unroll + inner
                        their = [
                            jnp.broadcast_to(shifted[col + low_col, shift, b, r, pl.ds(slot, 1), :], (ROWS, LANES))
                            for r in range(rows)
                        ]
                        for v in range(group):
                            totals[v] = pair(mine[v], their, totals[v])
                    return tuple(totals)

                return lax.fori_loop(start // unroll, slots // unroll, step, totals)

            totals = tuple(first(x, span, lanes) for span in spans)
            totals = lax.fori_loop(0, forms * len(sources), source, totals)
            for span, total in zip(spans, totals):
                last(x, span, lanes, total)
        return carry

    lax.fori_loop(0, blocks, lane_block, 0)


def own_sources(x, columns):
    return [(c, c - x) for c in range(columns) if abs(c - x) <= 1]


def pack_ends(field_of, fields, columns, left_ref, right_ref):
    for ref, at_last in ((left_ref, False), (right_ref, True)):
        lane = None
        packed = None
        for group in range(fields * columns):
            block = field_of(group // columns, group % columns, at_last)
            if lane is None:
                lane = lane_of(block.shape)
                packed = jnp.zeros(block.shape, jnp.float32)
            turn = (group + 1) % LANES if at_last else group
            packed = jnp.where(lane == group, pltpu.roll(block, turn, 1) if turn else block, packed)
        ref[...] = packed


def end_block(ref, column, field, at_last, limit):
    width = ref.shape[-1]
    lanes = slice(width - LANES, width) if at_last else slice(0, LANES)
    return ref[column, field, :limit, lanes]


def first_ends(motion):
    columns, _, slots, _ = motion.shape

    def kernel(motion_ref, left_ref, right_ref):
        pack_ends(
            lambda f, c, last: end_block(motion_ref, c, f, last, slots), MOTION, columns, left_ref, right_ref
        )

    ends = jax.ShapeDtypeStruct((slots, LANES), jnp.float32)
    return pl.pallas_call(kernel, out_shape=(ends, ends), in_specs=[VMEM], out_specs=(VMEM, VMEM), compiler_params=PARAMS)(motion)


def bounds_of(sizes):
    spans, lo = [], 0
    for index, hi in enumerate(sizes):
        if hi > lo:
            spans.append((index, lo, hi))
            lo = hi
    return spans


def own_part(kind, motion, pressure, ends_m, ends_p, limit, shifts, partial=None):
    columns, _, slots, width = motion.shape
    moved, pressed, massed, _, outs = kind
    inner = shifts == (0,)
    mutual = 2 * limit >= slots
    if inner:
        ends_m = ends_p = []
    flat_m = [e for pair in ends_m for e in pair]
    flat_p = [e for pair in ends_p for e in pair]
    whole = [(0, 0, slots)]
    spans_m = whole if inner else bounds_of([e[0].shape[0] for e in ends_m])
    spans_p = whole if inner else bounds_of([e[0].shape[0] for e in ends_p])
    inputs = [motion] + ([pressure] if pressed else []) + flat_m + flat_p + ([] if partial is None else [partial])
    rows = len(moved) + len(pressed) + len(massed)

    def kernel(*refs):
        refs = list(refs)
        motion_ref = refs.pop(0)
        pressure_ref = refs.pop(0) if pressed else None
        m_refs = refs[: len(flat_m)]
        p_refs = refs[len(flat_m) : len(flat_m) + len(flat_p)]
        if mutual:
            *refs, parts, reaction, packed = refs
            mutual_refs = (parts, reaction, packed)
        partial_ref = None if partial is None else refs[-3]
        out_ref, shifted = refs[-2:]

        def pieces(cells, ends, spans):
            if inner:
                return [(cells, None, None, 0, slots)]
            return [(cells, ends[2 * i], ends[2 * i + 1], lo, hi) for i, lo, hi in spans]

        for c in range(columns):

            def motion_pieces(field):
                return pieces(motion_ref.at[c, field], m_refs, spans_m if field < 6 else [(len(ends_m) - 1, 0, slots)])

            def pressure_pieces(field):
                return pieces(pressure_ref.at[c, field], p_refs, spans_p)

            fill_column(shifted, c, kind, motion_pieces, pressure_pieces, lambda f: f * columns + c, shifts)
        zero = jnp.zeros((ROWS, LANES), jnp.float32)

        def first(x, span, lanes):
            if partial is None:
                return (zero,) * outs
            return tuple(partial_ref[x, k, span, lanes] for k in range(outs))

        def last(x, span, lanes, total):
            for k in range(outs):
                out_ref[x, k, span, lanes] = total[k]

        if not mutual:
            for x in range(columns):
                add_pairs(kind, motion_ref, pressure_ref, shifted, x, own_sources(x, columns), limit, first, last)
            return
        parts, reaction, packed = mutual_refs

        def so_far(x, span, lanes):
            return tuple(out_ref[x, k, span, lanes] for k in range(outs))

        out_ref[...] = jnp.zeros(out_ref.shape, jnp.float32) if partial is None else partial_ref[...]
        for x in range(columns):
            for at in own_sources(x, columns):
                start = 0 if inner and at[0] == x else limit
                if start < slots:
                    add_pairs(kind, motion_ref, pressure_ref, shifted, x, [at], limit, so_far, last, start)
        edges = []
        for x in range(columns):
            for col in (x, x + 1):
                for shift in shifts:
                    if col == columns or (col == x and shift != 1):
                        continue
                    both_ways(kind, motion_ref, pressure_ref, shifted, x, col, shifts.index(shift), out_ref, parts, reaction, limit)
                    take_reaction(out_ref, reaction, col, shift, outs)
                    if shift:
                        edges.append((col, x, -shift))
        if edges:
            edge_pairs(kind, motion_ref, pressure_ref, shifted, shifts, edges, out_ref, packed, limit)

    return pl.pallas_call(
        kernel,
        out_shape=jax.ShapeDtypeStruct((columns, outs, limit, width), jnp.float32),
        in_specs=[VMEM] * len(inputs),
        out_specs=VMEM,
        scratch_shapes=[pltpu.VMEM((columns, len(shifts), width // LANES, rows, slots, LANES), jnp.float32)]
        + (
            [
                pltpu.VMEM((outs, limit, ROWS, LANES), jnp.float32),
                pltpu.VMEM((outs, width // LANES, limit, LANES), jnp.float32),
                pltpu.VMEM((rows, limit, LANES), jnp.float32),
            ]
            if mutual
            else []
        ),
        compiler_params=PARAMS,
        cost_estimate=cost(limit * slots * len(shifts) * (3 * columns - 2) * width, 60 if outs == 3 else 30),
    )(*inputs)


def sum_rows(values):
    row = lax.broadcasted_iota(jnp.int32, (ROWS, LANES), 0)
    step = 1
    while len(values) > 1:
        low = lax.bitwise_and(row, step) == 0
        values = [
            jnp.where(low, a, b) + pltpu.roll(jnp.where(low, b, a), step, 0) for a, b in zip(values[::2], values[1::2])
        ]
        step *= 2
    return values[0]


def own_rows(kind, motion_ref, pressure_ref, x, span, lanes):
    moved, pressed, massed = kind[:3]
    rows = [(motion_ref, f, s) for f, s in moved] + [(pressure_ref, f, s) for f, s in pressed] + [(motion_ref, f, s) for f, s in massed]
    return [ref[x, f, span, lanes] * s if s != 1.0 else ref[x, f, span, lanes] for ref, f, s in rows]


def both_ways(kind, motion_ref, pressure_ref, shifted, x, col, form, sums, parts, reaction, limit):
    outs = kind[4]
    blocks, rows = shifted.shape[2], shifted.shape[3]
    both = both_force if outs == 3 else both_density
    sign = -1.0 if outs == 3 else 1.0
    group = min(limit // ROWS, 2 if outs == 3 else 4)
    unroll = 8

    def lane_block(b, carry):
        lanes = pl.ds(pl.multiple_of(b * LANES, LANES), LANES)
        for part in range(limit // (ROWS * group)):
            spans = [slice((part * group + v) * ROWS, (part * group + v + 1) * ROWS) for v in range(group)]
            mine = []
            for span in spans:
                values = own_rows(kind, motion_ref, pressure_ref, x, span, lanes)
                mine.append([values[0] - float(col - x)] + values[1:])

            def step(outer, totals):
                totals = list(totals)
                for inner in range(unroll):
                    slot = outer * unroll + inner
                    their = [jnp.broadcast_to(shifted[col, form, b, r, pl.ds(slot, 1), :], (ROWS, LANES)) for r in range(rows)]
                    back = None
                    for v in range(group):
                        totals[v], given = both(mine[v], their, totals[v])
                        back = given if back is None else tuple(p + q for p, q in zip(back, given))
                    for k in range(outs):
                        parts[k, slot] = back[k] if part == 0 else parts[k, slot] + back[k]
                return tuple(totals)

            totals = tuple(tuple(sums[x, k, span, lanes] for k in range(outs)) for span in spans)
            totals = lax.fori_loop(0, limit // unroll, step, totals)
            for span, total in zip(spans, totals):
                for k in range(outs):
                    sums[x, k, span, lanes] = total[k]
        for k in range(outs):
            for lo in range(0, limit, ROWS):
                reaction[k, b, lo : lo + ROWS, :] = sign * sum_rows([parts[k, lo + r] for r in range(ROWS)])
        return carry

    lax.fori_loop(0, blocks, lane_block, 0)


def take_reaction(sums, reaction, col, shift, outs):
    blocks, slots = reaction.shape[1], reaction.shape[2]
    lane = lane_of((slots, LANES))
    for k in range(outs):
        values = [reaction[k, b] for b in range(blocks)]
        if shift == 1:
            turned = [jnp.zeros((slots, LANES), jnp.float32)] + [pltpu.roll(v, 1, 1) for v in values]
            values = [jnp.where(lane == 0, turned[b], turned[b + 1]) for b in range(blocks)]
        elif shift == -1:
            turned = [pltpu.roll(v, LANES - 1, 1) for v in values] + [jnp.zeros((slots, LANES), jnp.float32)]
            values = [jnp.where(lane == LANES - 1, turned[b + 1], turned[b]) for b in range(blocks)]
        for b in range(blocks):
            lanes = slice(b * LANES, (b + 1) * LANES)
            sums[col, k, :, lanes] = sums[col, k, :, lanes] + values[b]


def edge_pairs(kind, motion_ref, pressure_ref, shifted, forms, edges, sums, packed, limit):
    pair, outs = kind[3], kind[4]
    blocks, rows = shifted.shape[2], shifted.shape[3]
    lane = lane_of((ROWS, LANES))
    width = blocks * LANES
    tall = lane_of((limit, LANES))
    for r in range(rows):
        value = jnp.zeros((limit, LANES), jnp.float32)
        for q, (x, col, shift) in enumerate(edges):
            block, turn = (0, q) if shift == -1 else (blocks - 1, q + 1)
            value = jnp.where(tall == q, pltpu.roll(shifted[col, forms.index(shift), block, r, :limit, :], turn, 1), value)
        packed[r] = value
    spans = [slice(lo, lo + ROWS) for lo in range(0, limit, ROWS)]
    group = min(limit // ROWS, 2 if outs == 3 else 4)
    unroll = 8
    for part in range(len(spans) // group):
        mine = []
        for span in spans[part * group : (part + 1) * group]:
            values = None
            for q, (x, col, shift) in enumerate(edges):
                lanes, turn = (slice(0, LANES), q) if shift == -1 else (slice(width - LANES, width), q + 1)
                cell = own_rows(kind, motion_ref, pressure_ref, x, span, lanes)
                cell = [pltpu.roll(v, turn, 1) if turn else v for v in cell]
                cell[0] = cell[0] - float(col - x)
                values = cell if values is None else [jnp.where(lane == q, c, v) for c, v in zip(cell, values)]
            mine.append(values)

        def step(outer, totals):
            totals = list(totals)
            for inner in range(unroll):
                slot = outer * unroll + inner
                their = [jnp.broadcast_to(packed[r, pl.ds(slot, 1), :], (ROWS, LANES)) for r in range(rows)]
                for v in range(group):
                    totals[v] = pair(mine[v], their, totals[v])
            return tuple(totals)

        zero = jnp.zeros((ROWS, LANES), jnp.float32)
        totals = lax.fori_loop(0, limit // unroll, step, tuple((zero,) * outs for _ in range(group)))
        for v, span in enumerate(spans[part * group : (part + 1) * group]):
            for k in range(outs):
                for q, (x, col, shift) in enumerate(edges):
                    at = 0 if shift == -1 else LANES - 1
                    lanes = slice(0, LANES) if shift == -1 else slice(width - LANES, width)
                    back = pltpu.roll(totals[v][k], (at - q) % LANES, 1) if at != q else totals[v][k]
                    sums[x, k, span, lanes] = sums[x, k, span, lanes] + jnp.where(lane == at, back, 0.0)


def halo_sums(kind, refs, columns, slots, limit, first, last, motion_ref, pressure_ref, shifted, sizes_m, sizes_p):
    spans_m, spans_p = bounds_of(sizes_m), bounds_of(sizes_p)
    for side in range(2):
        m_refs, p_refs = refs[side]
        column = columns - 1 if side == 0 else 0

        def field_of(ref, at, size):
            return ref.at[at : at + size]

        def piece(cells, ends, lo, hi):
            return (cells, ends.at[:, 0:LANES], ends.at[:, LANES : 2 * LANES], lo, hi)

        def motion_pieces(field):
            out = []
            for i, lo, hi in spans_m if field < 6 else [(len(sizes_m) - 1, 0, slots)]:
                size = sizes_m[i]
                ends = field_of(m_refs[i], (4 if i == len(sizes_m) - 1 else 3) * size, size)
                if field < 3 or field == 6:
                    cells = field_of(m_refs[i], min(field, 3) * size, size)
                else:
                    cells = field_of(p_refs[i], 4 * sizes_p[i] + (field - 3) * size, size)
                out.append(piece(cells, ends, lo, hi))
            return out

        def pressure_pieces(field):
            return [
                piece(field_of(p_refs[i], field * sizes_p[i], sizes_p[i]), field_of(p_refs[i], 3 * sizes_p[i], sizes_p[i]), lo, hi)
                for i, lo, hi in spans_p
            ]

        fill_column(shifted, side, kind, motion_pieces, pressure_pieces, lambda f: f * columns + column, SHIFTS)
        x, shift = (0, -1) if side == 0 else (columns - 1, 1)
        add_pairs(kind, motion_ref, pressure_ref, shifted, x, [(side, shift)], limit, first, last)


def density_rest(motion, partial, messages, sizes, density, entropy, counts, level, limit, slots_sent):
    columns, _, slots, width = motion.shape
    (m_left, m_right) = messages
    first = density is None
    inputs = [motion, partial, entropy, counts] + ([] if first else [density]) + m_left + m_right
    n_in, n_m = len(inputs), len(m_left)
    rows = 4

    def kernel(*refs):
        motion_ref, partial_ref, entropy_ref, counts_ref = refs[:4]
        old_ref = None if first else refs[4]
        m_refs = refs[n_in - 2 * n_m : n_in]
        press_ref, left_ref, right_ref, shifted, sums = refs[n_in:]
        sums[...] = partial_ref[...]

        def start(x, span, lanes):
            return (sums[x, 0, span, lanes],)

        def end(x, span, lanes, total):
            sums[x, 0, span, lanes] = total[0]

        sides = ((m_refs[:n_m], []), (m_refs[n_m:], []))
        halo_sums(DENSITY, sides, columns, slots, limit, start, end, motion_ref, None, shifted, sizes, [])
        for x in range(columns):
            count = counts_ref[level, x : x + 1, :]
            for lo in range(0, slots, ROWS):
                span = slice(lo, lo + ROWS)
                if lo >= limit:
                    if first:
                        value = jnp.ones((ROWS, width), jnp.float32)
                    else:
                        for f in range(3):
                            press_ref[x, f, span, :] = old_ref[x, f, span, :]
                        continue
                else:
                    slot = lax.broadcasted_iota(jnp.int32, (ROWS, width), 0) + lo
                    before = jnp.ones((ROWS, width), jnp.float32) if first else old_ref[x, 2, span, :]
                    value = jnp.where(slot < count, sums[x, 0, span, :], before)
                pressure = entropy_ref[x, span, :] * jnp.exp(jnp.log(value) * (GAMMA - 2.0))
                press_ref[x, 0, span, :] = pressure
                press_ref[x, 1, span, :] = jnp.sqrt(GAMMA * pressure * value)
                press_ref[x, 2, span, :] = value
        pack_ends(lambda f, c, last: end_block(press_ref, c, f, last, slots_sent), PRESSURE, columns, left_ref, right_ref)

    ends = jax.ShapeDtypeStruct((slots_sent, LANES), jnp.float32)
    return pl.pallas_call(
        kernel,
        out_shape=(jax.ShapeDtypeStruct((columns, PRESSURE, slots, width), jnp.float32), ends, ends),
        in_specs=[VMEM] * n_in,
        out_specs=(VMEM,) * 3,
        scratch_shapes=[
            pltpu.VMEM((2, 3, width // LANES, rows, slots, LANES), jnp.float32),
            pltpu.VMEM((columns, 1, limit, width), jnp.float32),
        ],
        compiler_params=PARAMS,
        cost_estimate=cost(limit * slots * 6 * width, 30),
    )(*inputs)


def force_rest(motion, pressure, partial, messages_m, messages_p, sizes_m, sizes_p, counts, level, limit, slots_sent):
    columns, _, slots, width = motion.shape
    n_m, n_p = len(messages_m[0]), len(messages_p[0])
    inputs = [motion, pressure, partial, counts] + messages_m[0] + messages_p[0] + messages_m[1] + messages_p[1]
    n_in = len(inputs)
    rows = 10
    ends = jax.ShapeDtypeStruct((slots_sent, LANES), jnp.float32)
    outs = (jax.ShapeDtypeStruct(motion.shape, jnp.float32),) + ((ends, ends) if slots_sent else ())

    def kernel(*refs):
        motion_ref, pressure_ref, partial_ref, counts_ref = refs[:4]
        sides = []
        for side in range(2):
            at = 4 + side * (n_m + n_p)
            sides.append((refs[at : at + n_m], refs[at + n_m : at + n_m + n_p]))
        new_ref = refs[n_in]
        shifted, sums = refs[-2:]
        sums[...] = partial_ref[...]

        def start(x, span, lanes):
            return tuple(sums[x, k, span, lanes] for k in range(3))

        def end(x, span, lanes, total):
            for k in range(3):
                sums[x, k, span, lanes] = total[k]

        halo_sums(
            FORCE, sides, columns, slots, limit, start, end, motion_ref, pressure_ref, shifted, sizes_m, sizes_p
        )
        for x in range(columns):
            count = counts_ref[level, x : x + 1, :]
            new_ref[x, 6, :, :] = motion_ref[x, 6, :, :]
            if limit < slots:
                for f in range(6):
                    new_ref[x, f, limit:, :] = motion_ref[x, f, limit:, :]
            for lo in range(0, limit, ROWS):
                span = slice(lo, lo + ROWS)
                active = lax.broadcasted_iota(jnp.int32, (ROWS, width), 0) + lo < count
                for k in range(3):
                    place, speed = motion_ref[x, k, span, :], motion_ref[x, 3 + k, span, :]
                    faster = speed + TIME_STEP * sums[x, k, span, :]
                    new_ref[x, 3 + k, span, :] = jnp.where(active, faster, speed)
                    new_ref[x, k, span, :] = jnp.where(active, place + TIME_STEP * faster, place)
        if slots_sent:
            left_ref, right_ref = refs[n_in + 1 : n_in + 3]
            pack_ends(lambda f, c, last: end_block(new_ref, c, f, last, slots_sent), 6, columns, left_ref, right_ref)

    made = pl.pallas_call(
        kernel,
        out_shape=outs,
        in_specs=[VMEM] * n_in,
        out_specs=(VMEM,) * len(outs),
        scratch_shapes=[
            pltpu.VMEM((2, 3, width // LANES, rows, slots, LANES), jnp.float32),
            pltpu.VMEM((columns, 3, limit, width), jnp.float32),
        ],
        compiler_params=PARAMS,
        cost_estimate=cost(limit * slots * 6 * width, 60),
    )(*inputs)
    return made if slots_sent else (made[0], None, None)


def ranks(destination, parts):
    rows, width = destination.shape

    def kernel(dest_ref, place_ref, meta_ref):
        dest = dest_ref[...]
        low = lax.broadcasted_iota(jnp.int32, (width, width), 0)
        upto = jnp.where(low <= lane_of((width, width)), 1.0, 0.0).astype(jnp.bfloat16)
        above = lax.broadcasted_iota(jnp.int32, (rows, rows), 0) > lane_of((rows, rows))
        above = jnp.where(above, 1.0, 0.0).astype(jnp.bfloat16)
        lane = lane_of((rows, LANES))
        meta = jnp.zeros((rows, LANES), jnp.float32)
        place = jnp.zeros((rows, width), jnp.float32)
        start = jnp.zeros((rows, 1), jnp.float32)
        for d in range(parts):
            mask = jnp.where(dest == d, 1.0, 0.0)
            inside = jnp.dot(mask.astype(jnp.bfloat16), upto, preferred_element_type=jnp.float32)
            count = inside[:, width - 1 : width]
            wide = jnp.broadcast_to(count, (rows, LANES))
            before = jnp.dot(above, wide.astype(jnp.bfloat16), preferred_element_type=jnp.float32)
            place = place + mask * (inside - 1.0 + start)
            meta = jnp.where(lane == d, before, meta)
            meta = jnp.where(lane == parts + d, jnp.broadcast_to(start, (rows, LANES)), meta)
            meta = jnp.where(lane == 2 * parts + d, before + wide, meta)
            start = start + count
        place_ref[...] = place.astype(jnp.int32)
        meta_ref[...] = meta.astype(jnp.int32)

    return pl.pallas_call(
        kernel,
        out_shape=(jax.ShapeDtypeStruct((rows, width), jnp.int32), jax.ShapeDtypeStruct((rows, LANES), jnp.int32)),
        in_specs=[VMEM],
        out_specs=(VMEM, VMEM),
        compiler_params=PARAMS,
    )(destination)


def compact(motion, pressure, place, meta, here, parts, capacity):
    columns, _, slots, width = motion.shape
    chunks = width // LANES
    total = -(-capacity // LANES)

    def kernel(motion_ref, pressure_ref, place_ref, meta_ref, here_ref, *refs):
        out_refs, (local, lists) = refs[:parts], refs[parts:]
        target = [lax.rem(here_ref[0] + k, parts) for k in range(parts)]
        lane = lane_of((ROWS, LANES))

        def do_group(group, carry):
            span = pl.ds(pl.multiple_of(group * ROWS, ROWS), ROWS)
            fields = [
                [motion_ref[x, f, span, :] for f in range(6)] + [pressure_ref[x, 2, span, :], motion_ref[x, 6, span, :]]
                for x in range(columns)
            ]
            for s in range(ROWS):
                for x in range(columns):
                    state = jnp.concatenate([v[s : s + 1, :] for v in fields[x]], axis=0)
                    high = state.astype(jnp.bfloat16).astype(jnp.float32)
                    rest = state - high
                    middle = rest.astype(jnp.bfloat16).astype(jnp.float32)
                    lowest = rest - middle
                    stacked = jnp.concatenate([high, middle, lowest], axis=0).astype(jnp.bfloat16)
                    row = (group * ROWS + s) * columns + x
                    wanted = place_ref[pl.ds(row, 1), :]
                    hot = jnp.where(lax.broadcasted_iota(jnp.int32, (width, width), 0) == wanted, 1.0, 0.0)
                    moved = lax.dot_general(
                        stacked, hot.astype(jnp.bfloat16), (((1,), (1,)), ((), ())), preferred_element_type=jnp.float32
                    )
                    moved = moved[0:8] + moved[8:16] + moved[16:24]
                    buffer = (s * columns + x) % 4
                    for c in range(chunks):
                        local[buffer, c + 1] = moved[:, c * LANES : (c + 1) * LANES]
                    for d in range(parts):
                        base = meta_ref[row, target[d]]
                        begin = meta_ref[row, parts + target[d]]
                        chunk = lax.shift_right_logical(base, 7)
                        off = lax.bitwise_and(base, LANES - 1)
                        turn = lax.bitwise_and(off - begin, LANES - 1)
                        at = lax.shift_right_logical(begin, 7)
                        at = at + jnp.where(off < lax.bitwise_and(begin, LANES - 1), 1, 0)
                        turned = [pltpu.roll(local[buffer, at + k], turn, 1) for k in range(chunks + 2)]
                        for k in range(chunks + 1):
                            value = jnp.where(lane >= turn, turned[k + 1], turned[k])
                            if k == 0:
                                value = jnp.where(lane >= off, value, lists[d, chunk])
                            lists[d, chunk + k] = value
            return carry

        lax.fori_loop(0, slots // ROWS, do_group, 0)
        for d in range(parts):
            count = meta_ref[slots * columns - 1, 2 * parts + target[d]]
            for c in range(total):
                out_refs[d][:, c * LANES : (c + 1) * LANES] = jnp.where(lane + c * LANES < count, lists[d, c], 0.0)

    return pl.pallas_call(
        kernel,
        out_shape=(jax.ShapeDtypeStruct((8, capacity), jnp.float32),) * parts,
        in_specs=[VMEM, VMEM, VMEM, SMEM, SMEM],
        out_specs=(VMEM,) * parts,
        scratch_shapes=[
            pltpu.VMEM((4, 2 * chunks + 4, ROWS, LANES), jnp.float32),
            pltpu.VMEM((parts, total + chunks + 2, ROWS, LANES), jnp.float32),
        ],
        compiler_params=PARAMS,
    )(motion, pressure, place, meta, here)


def in_order(here, received):
    parts = len(received)
    rows, capacity = received[0].shape

    def kernel(here_ref, *refs):
        out_ref = refs[parts]
        for k in range(parts):

            @pl.when(pl.program_id(0) == k)
            def _():
                out_ref[...] = refs[k][...]

    return pl.pallas_call(
        kernel,
        out_shape=jax.ShapeDtypeStruct((rows, parts * capacity), jnp.float32),
        grid_spec=pltpu.PrefetchScalarGridSpec(
            num_scalar_prefetch=1,
            grid=(parts,),
            in_specs=[VMEM] * parts,
            out_specs=pl.BlockSpec((rows, capacity), lambda k, here_ref: (0, lax.rem(here_ref[0] - k + parts, parts))),
        ),
        compiler_params=PARAMS,
    )(here, *received)


def pass_on(value, axis, step):
    count = lax.axis_size(axis)
    return lax.ppermute(value, axis, [(i, (i + step) % count) for i in range(count)])


def swap_ends(left_ends, right_ends):
    return pass_on(right_ends, "sub", 1), pass_on(left_ends, "sub", -1)


def swap_columns(parts_of):
    first = jnp.concatenate(parts_of(0), axis=0)
    final = jnp.concatenate(parts_of(-1), axis=0)
    return pass_on(final, "tile", 1), pass_on(first, "tile", -1)


def rows_of(fields):
    return fields.reshape(-1, fields.shape[-1])


def beside(ends, width):
    plane = jnp.concatenate(ends, axis=1)
    return jnp.pad(plane, ((0, 0), (0, width - plane.shape[1])))


def shards(offsets, velocity, mass, entropy, active_counts, targets):
    slots, columns, width = mass.shape
    levels = active_counts.shape[0]
    parts = lax.axis_size("sub")
    slot_index = lax.broadcasted_iota(jnp.int32, mass.shape, 0)
    mass_live = jnp.where(slot_index < active_counts[0][None], mass, 0.0)
    motion = jnp.concatenate([offsets, velocity, mass_live[None]], axis=0).transpose(2, 0, 1, 3)
    entropy = entropy.transpose(1, 0, 2)
    limits = (slots, slots // 2, slots // 4)
    pressure = None
    ends_m, ends_p, sizes_m, sizes_p = [], [], [], []
    left_m, right_m, left_p, right_p = [], [], [], []
    made = first_ends(motion)
    place, meta = ranks(targets.reshape(slots * columns, width), parts)
    for level in range(levels):
        limit = limits[level]
        sent = limits[max(level - 1, 0)]
        ends_m.insert(0, swap_ends(*made))
        partial = own_part(DENSITY, motion, None, ends_m, [], limit, (0,))
        ends_m[0], partial = lax.optimization_barrier((ends_m[0], partial))
        plane = beside(ends_m[0], width)
        masses = (lambda c: [motion[c, 6]]) if level == 0 else (lambda c: [])
        cells = swap_columns(lambda c: [rows_of(motion[c, :3, :sent]), *masses(c), plane])
        sizes_m.insert(0, sent)
        left_m.insert(0, cells[0])
        right_m.insert(0, cells[1])
        partial = own_part(DENSITY, motion, None, ends_m, [], limit, (-1, 1), partial)
        pressure, *made = density_rest(motion, partial, (left_m, right_m), sizes_m, pressure, entropy, active_counts, level, limit, limit)
        ends_p.insert(0, swap_ends(*made))
        partial = own_part(FORCE, motion, pressure, ends_m, ends_p, limit, (0,))
        ends_p[0], partial = lax.optimization_barrier((ends_p[0], partial))
        plane = beside(ends_p[0], width)
        cells = swap_columns(lambda c: [rows_of(pressure[c, :, :limit]), plane, rows_of(motion[c, 3:6, :sent])])
        sizes_p.insert(0, limit)
        left_p.insert(0, cells[0])
        right_p.insert(0, cells[1])
        partial = own_part(FORCE, motion, pressure, ends_m, ends_p, limit, (-1, 1), partial)
        more = limit if level < levels - 1 else 0
        motion, *made = force_rest(
            motion, pressure, partial, (left_m, right_m), (left_p, right_p), sizes_m, sizes_p, active_counts, level, limit, more
        )
    capacity = 3 * slots * columns * width // 8
    here = lax.axis_index("sub").astype(jnp.int32).reshape(1)
    lists = compact(motion, pressure, place, meta[:, : 3 * parts], here, parts, capacity)
    received = {0: lists[0]}
    for k in sorted(range(1, parts), key=lambda k: -min(k, parts - k)):
        received[k] = pass_on(lists[k], "sub", k)
    return in_order(here, [received[k] for k in range(parts)])


def solution(mesh):
    placed = (
        P(None, None, "tile", "sub"),
        P(None, None, "tile", "sub"),
        P(None, "tile", "sub"),
        P(None, "tile", "sub"),
        P(None, "tile", "sub"),
        P(None, "tile", "sub"),
    )
    return jax.shard_map(
        shards, mesh=mesh, in_specs=placed, out_specs=P(None, ("tile", "sub")), check_vma=False
    )
```

```python
import functools
import math

import jax
import jax.numpy as jnp
from jax import lax
from jax.experimental import pallas as pl
from jax.experimental.pallas import tpu as pltpu
from jax.sharding import PartitionSpec as P

KERNEL_NORM = 21.0 / (2.0 * math.pi)
GAMMA = 5.0 / 3.0
TIME_STEP = 0.05
SOFTEN = 0.01
LANES = 128
ROWS = 8
VMEM = pl.BlockSpec(memory_space=pltpu.VMEM)
SMEM = pl.BlockSpec(memory_space=pltpu.SMEM)
PARAMS = pltpu.CompilerParams(vmem_limit_bytes=24 << 20)
MOTION, PRESSURE = 7, 3
SHIFTS = (-1, 0, 1)
KEEP = ((True, True, True), (True, True, True), (False, False, False))


def lane_of(shape):
    return lax.broadcasted_iota(jnp.int32, shape, 1)


def cost(pairs, ops):
    return pl.CostEstimate(flops=int(pairs * ops * 15), bytes_accessed=1 << 20, transcendentals=0)


def closeness(delta):
    dx, dy, dz = delta
    squared = dx * dx + dy * dy + dz * dz
    radius = squared * lax.rsqrt(jnp.maximum(squared, 1e-30))
    return jnp.maximum(1.0 - radius, 0.0)


def displacement(own, their):
    return tuple(i - j for i, j in zip(own[:3], their[:3]))


def force_core(own, their, remain):
    ui, vi, wi, qi, ci, ri = own[3:9]
    uj, vj, wj, qj, cj, rj = their[3:9]
    dx, dy, dz = displacement(own, their)
    radius = 1.0 - remain
    approach = dx * (ui - uj) + dy * (vi - vj) + dz * (wi - wj)
    closing = jnp.minimum(approach, 0.0) * pl.reciprocal(radius * radius + SOFTEN, approx=True)
    viscous = closing * (closing - (ci + cj)) * pl.reciprocal(ri + rj, approx=True)
    return (dx, dy, dz), qi + qj + viscous


def pair_force(own, their, total, remain):
    delta, pressure = force_core(own, their, remain)
    strength = pressure * ((remain * remain) * (remain * their[-1]))
    return tuple(t + strength * d for t, d in zip(total, delta))


def pair_density(own, their, total, remain):
    square = remain * remain
    return (total[0] + (square * square) * ((5.0 - 4.0 * remain) * their[-1]),)


def both_force(own, their, total, remain):
    delta, pressure = force_core(own, their, remain)
    strength = pressure * ((remain * remain) * remain)
    on_own, on_their = strength * their[-1], strength * own[-1]
    return tuple(t + on_own * d for t, d in zip(total, delta)), tuple(on_their * d for d in delta)


def both_density(own, their, total, remain):
    square = remain * remain
    weight = (square * square) * (5.0 - 4.0 * remain)
    return (total[0] + weight * their[-1],), (weight * own[-1],)


def kept(kept_ref, at, own, their, first):
    if kept_ref is not None and not first:
        return kept_ref[at]
    value = closeness(displacement(own, their))
    if kept_ref is not None:
        kept_ref[at] = value
    return value


DENSITY = ((0, 1.0), (1, 1.0), (2, 1.0)), (), ((6, KERNEL_NORM),), pair_density, 1
FORCE = (
    tuple((c, 1.0) for c in range(3)) + tuple((c, 4.0) for c in range(3, 6)),
    ((0, 1.0), (1, 1.0), (2, 4.0)),
    ((6, 20.0 * KERNEL_NORM),),
    pair_force,
    3,
)


def fill_shifted(shifted, col, row, pieces, scale, group, shifts, is_y):
    for cells, left, right, lo, hi in pieces:
        count = cells.shape[-1] // LANES
        blocks = [cells[lo:hi, b * LANES : (b + 1) * LANES] for b in range(count)]
        if scale != 1.0:
            blocks = [v * scale for v in blocks]
        lane = lane_of(blocks[0].shape)
        for at, shift in enumerate(shifts):
            values = blocks
            if shift == -1:
                turned = [pltpu.roll(v, 1, 1) for v in blocks]
                end = pltpu.roll(left[lo:hi, :], (LANES - group) % LANES, 1) if group else left[lo:hi, :]
                turned = [end if scale == 1.0 else end * scale] + turned
                values = [jnp.where(lane == 0, turned[b], turned[b + 1]) for b in range(count)]
            elif shift == 1:
                turned = [pltpu.roll(v, LANES - 1, 1) for v in blocks]
                end = pltpu.roll(right[lo:hi, :], LANES - 1 - group, 1)
                turned.append(end if scale == 1.0 else end * scale)
                values = [jnp.where(lane == LANES - 1, turned[b + 1], turned[b]) for b in range(count)]
            if is_y and shift:
                values = [v + float(shift) for v in values]
            for b in range(count):
                shifted[col, at, b, row, lo:hi, :] = values[b]


def fill_column(shifted, col, kind, motion, pressure, group_of, shifts):
    moved, pressed, massed, _, _ = kind
    row = 0
    for pieces, fields in ((motion, moved), (pressure, pressed), (motion, massed)):
        for field, scale in fields:
            is_y = fields is moved and field == 1
            fill_shifted(shifted, col, row, pieces(field), scale, group_of(field), shifts, is_y)
            row += 1


def add_pairs(kind, motion_ref, pressure_ref, shifted, x, sources, limit, first, last, kept_ref, unit, start=0):
    moved, pressed, _, pair, width = kind
    slots = shifted.shape[-2]
    blocks = shifted.shape[2]
    rows = shifted.shape[3]
    group = min(limit // ROWS, 2 if width == 3 else 4)
    unroll = min(slots - start, 16 // group if width == 3 else 32 // group)
    forms = shifted.shape[1]
    low_col, low_shift = sources[0]

    def lane_block(b, carry):
        lanes = pl.ds(pl.multiple_of(b * LANES, LANES), LANES)
        for part in range(limit // (ROWS * group)):
            spans = [slice((part * group + v) * ROWS, (part * group + v + 1) * ROWS) for v in range(group)]
            own = []
            for span in spans:
                values = [motion_ref[x, f, span, lanes] * s if s != 1.0 else motion_ref[x, f, span, lanes] for f, s in moved]
                values += [pressure_ref[x, f, span, lanes] * s if s != 1.0 else pressure_ref[x, f, span, lanes] for f, s in pressed]
                own.append(values)

            def source(at, totals):
                col = at // forms
                shift = at - forms * col
                offset = (col + low_shift).astype(jnp.float32)
                mine = [[v[0] - offset] + v[1:] for v in own]

                def step(outer, totals):
                    totals = list(totals)
                    for inner in range(unroll):
                        slot = outer * unroll + inner
                        their = [
                            jnp.broadcast_to(shifted[col + low_col, shift, b, r, pl.ds(slot, 1), :], (ROWS, LANES))
                            for r in range(rows)
                        ]
                        for v in range(group):
                            place = (unit + at, b, slot, part * group + v)
                            remain = kept(kept_ref, place, mine[v], their, width == 1)
                            totals[v] = pair(mine[v], their, totals[v], remain)
                    return tuple(totals)

                return lax.fori_loop(start // unroll, slots // unroll, step, totals)

            totals = tuple(first(x, span, lanes) for span in spans)
            totals = lax.fori_loop(0, forms * len(sources), source, totals)
            for span, total in zip(spans, totals):
                last(x, span, lanes, total)
        return carry

    lax.fori_loop(0, blocks, lane_block, 0)


def own_sources(x, columns):
    return [(c, c - x) for c in range(columns) if abs(c - x) <= 1]


def pack_ends(field_of, fields, columns, left_ref, right_ref):
    for ref, at_last in ((left_ref, False), (right_ref, True)):
        lane = None
        packed = None
        for group in range(fields * columns):
            block = field_of(group // columns, group % columns, at_last)
            if lane is None:
                lane = lane_of(block.shape)
                packed = jnp.zeros(block.shape, jnp.float32)
            turn = (group + 1) % LANES if at_last else group
            packed = jnp.where(lane == group, pltpu.roll(block, turn, 1) if turn else block, packed)
        ref[...] = packed


def end_block(ref, column, field, at_last, limit):
    width = ref.shape[-1]
    lanes = slice(width - LANES, width) if at_last else slice(0, LANES)
    return ref[column, field, :limit, lanes]


def first_ends(motion):
    columns, _, slots, _ = motion.shape

    def kernel(motion_ref, left_ref, right_ref):
        pack_ends(
            lambda f, c, last: end_block(motion_ref, c, f, last, slots), MOTION, columns, left_ref, right_ref
        )

    ends = jax.ShapeDtypeStruct((slots, LANES), jnp.float32)
    return pl.pallas_call(kernel, out_shape=(ends, ends), in_specs=[VMEM], out_specs=(VMEM, VMEM), compiler_params=PARAMS)(motion)


def bounds_of(sizes):
    spans, lo = [], 0
    for index, hi in enumerate(sizes):
        if hi > lo:
            spans.append((index, lo, hi))
            lo = hi
    return spans


def own_part(kind, motion, pressure, ends_m, ends_p, limit, shifts, partial=None, closeness_kept=None, keep=False):
    columns, _, slots, width = motion.shape
    moved, pressed, massed, _, outs = kind
    inner = shifts == (0,)
    mutual = 2 * limit >= slots
    if inner:
        ends_m = ends_p = []
    flat_m = [e for pair in ends_m for e in pair]
    flat_p = [e for pair in ends_p for e in pair]
    whole = [(0, 0, slots)]
    spans_m = whole if inner else bounds_of([e[0].shape[0] for e in ends_m])
    spans_p = whole if inner else bounds_of([e[0].shape[0] for e in ends_p])
    inputs = [motion] + ([pressure] if pressed else []) + flat_m + flat_p + ([] if partial is None else [partial])
    n_in = len(inputs)
    calls = []
    for x in range(columns):
        for col, _ in own_sources(x, columns):
            start = limit if mutual and not (inner and col == x) else 0
            if start < slots:
                calls.append((x, col, start, None))
    if mutual:
        for x in range(columns):
            for col in (x, x + 1):
                for form, shift in enumerate(shifts):
                    if col < columns and (col != x or shift == 1):
                        calls.append((x, col, 0, form))
    units = sum(len(shifts) if form is None else 1 for *_, form in calls)
    kept_shape = jax.ShapeDtypeStruct((units, width // LANES, slots, limit // ROWS, ROWS, LANES), jnp.float32)
    keep = keep and not pressed
    if closeness_kept is not None:
        inputs.append(closeness_kept)
    rows = len(moved) + len(pressed) + len(massed)

    def kernel(*own_refs):
        refs = list(own_refs)
        motion_ref = refs.pop(0)
        pressure_ref = refs.pop(0) if pressed else None
        m_refs = refs[: len(flat_m)]
        p_refs = refs[len(flat_m) : len(flat_m) + len(flat_p)]
        partial_ref = None if partial is None else own_refs[n_in - 1]
        left = list(own_refs[n_in:])
        kept_ref = None if closeness_kept is None else left.pop(0)
        out_ref = left.pop(0)
        if keep:
            kept_ref = left.pop(0)
        shifted, *mutual_refs = left

        def pieces(cells, ends, spans):
            if inner:
                return [(cells, None, None, 0, slots)]
            return [(cells, ends[2 * i], ends[2 * i + 1], lo, hi) for i, lo, hi in spans]

        for c in range(columns):

            def motion_pieces(field):
                return pieces(motion_ref.at[c, field], m_refs, spans_m if field < 6 else [(len(ends_m) - 1, 0, slots)])

            def pressure_pieces(field):
                return pieces(pressure_ref.at[c, field], p_refs, spans_p)

            fill_column(shifted, c, kind, motion_pieces, pressure_pieces, lambda f: f * columns + c, shifts)

        def first(x, span, lanes):
            return tuple(out_ref[x, k, span, lanes] for k in range(outs))

        def last(x, span, lanes, total):
            for k in range(outs):
                out_ref[x, k, span, lanes] = total[k]

        out_ref[...] = jnp.zeros(out_ref.shape, jnp.float32) if partial is None else partial_ref[...]
        edges, unit = [], 0
        for x, col, start, form in calls:
            if form is None:
                add_pairs(
                    kind, motion_ref, pressure_ref, shifted, x, [(col, col - x)], limit, first, last, kept_ref, unit, start
                )
                unit += len(shifts)
                continue
            parts, reaction, packed = mutual_refs
            both_ways(
                kind, motion_ref, pressure_ref, shifted, x, col, form, out_ref, parts, reaction, limit, kept_ref, unit
            )
            take_reaction(out_ref, reaction, col, shifts[form], outs)
            unit += 1
            if shifts[form]:
                edges.append((col, x, -shifts[form]))
        if edges:
            edge_pairs(kind, motion_ref, pressure_ref, shifted, shifts, edges, out_ref, packed, limit)

    sums_shape = jax.ShapeDtypeStruct((columns, outs, limit, width), jnp.float32)
    return pl.pallas_call(
        kernel,
        out_shape=(sums_shape, kept_shape) if keep else (sums_shape,),
        in_specs=[VMEM] * len(inputs),
        out_specs=(VMEM, VMEM) if keep else (VMEM,),
        scratch_shapes=[pltpu.VMEM((columns, len(shifts), width // LANES, rows, slots, LANES), jnp.float32)]
        + (
            [
                pltpu.VMEM((outs, limit, ROWS, LANES), jnp.float32),
                pltpu.VMEM((outs, width // LANES, limit, LANES), jnp.float32),
                pltpu.VMEM((rows, limit, LANES), jnp.float32),
            ]
            if mutual
            else []
        ),
        compiler_params=PARAMS,
        cost_estimate=cost(limit * slots * len(shifts) * (3 * columns - 2) * width, 60 if outs == 3 else 30),
    )(*inputs)


def sum_rows(values):
    row = lax.broadcasted_iota(jnp.int32, (ROWS, LANES), 0)
    step = 1
    while len(values) > 1:
        low = lax.bitwise_and(row, step) == 0
        values = [
            jnp.where(low, a, b) + pltpu.roll(jnp.where(low, b, a), step, 0) for a, b in zip(values[::2], values[1::2])
        ]
        step *= 2
    return values[0]


def own_rows(kind, motion_ref, pressure_ref, x, span, lanes):
    moved, pressed, massed = kind[:3]
    rows = [(motion_ref, f, s) for f, s in moved] + [(pressure_ref, f, s) for f, s in pressed] + [(motion_ref, f, s) for f, s in massed]
    return [ref[x, f, span, lanes] * s if s != 1.0 else ref[x, f, span, lanes] for ref, f, s in rows]


def both_ways(kind, motion_ref, pressure_ref, shifted, x, col, form, sums, parts, reaction, limit, kept_ref, unit):
    outs = kind[4]
    blocks, rows = shifted.shape[2], shifted.shape[3]
    both = both_force if outs == 3 else both_density
    sign = -1.0 if outs == 3 else 1.0
    group = min(limit // ROWS, 2 if outs == 3 else 4)
    unroll = 8

    def lane_block(b, carry):
        lanes = pl.ds(pl.multiple_of(b * LANES, LANES), LANES)
        for part in range(limit // (ROWS * group)):
            spans = [slice((part * group + v) * ROWS, (part * group + v + 1) * ROWS) for v in range(group)]
            mine = []
            for span in spans:
                values = own_rows(kind, motion_ref, pressure_ref, x, span, lanes)
                mine.append([values[0] - float(col - x)] + values[1:])

            def step(outer, totals):
                totals = list(totals)
                for inner in range(unroll):
                    slot = outer * unroll + inner
                    their = [jnp.broadcast_to(shifted[col, form, b, r, pl.ds(slot, 1), :], (ROWS, LANES)) for r in range(rows)]
                    back = None
                    for v in range(group):
                        place = (unit, b, slot, part * group + v)
                        remain = kept(kept_ref, place, mine[v], their, outs == 1)
                        totals[v], given = both(mine[v], their, totals[v], remain)
                        back = given if back is None else tuple(p + q for p, q in zip(back, given))
                    for k in range(outs):
                        parts[k, slot] = back[k] if part == 0 else parts[k, slot] + back[k]
                return tuple(totals)

            totals = tuple(tuple(sums[x, k, span, lanes] for k in range(outs)) for span in spans)
            totals = lax.fori_loop(0, limit // unroll, step, totals)
            for span, total in zip(spans, totals):
                for k in range(outs):
                    sums[x, k, span, lanes] = total[k]
        for k in range(outs):
            for lo in range(0, limit, ROWS):
                reaction[k, b, lo : lo + ROWS, :] = sign * sum_rows([parts[k, lo + r] for r in range(ROWS)])
        return carry

    lax.fori_loop(0, blocks, lane_block, 0)


def take_reaction(sums, reaction, col, shift, outs):
    blocks, slots = reaction.shape[1], reaction.shape[2]
    lane = lane_of((slots, LANES))
    for k in range(outs):
        values = [reaction[k, b] for b in range(blocks)]
        if shift == 1:
            turned = [jnp.zeros((slots, LANES), jnp.float32)] + [pltpu.roll(v, 1, 1) for v in values]
            values = [jnp.where(lane == 0, turned[b], turned[b + 1]) for b in range(blocks)]
        elif shift == -1:
            turned = [pltpu.roll(v, LANES - 1, 1) for v in values] + [jnp.zeros((slots, LANES), jnp.float32)]
            values = [jnp.where(lane == LANES - 1, turned[b + 1], turned[b]) for b in range(blocks)]
        for b in range(blocks):
            lanes = slice(b * LANES, (b + 1) * LANES)
            sums[col, k, :, lanes] = sums[col, k, :, lanes] + values[b]


def edge_pairs(kind, motion_ref, pressure_ref, shifted, forms, edges, sums, packed, limit):
    pair, outs = kind[3], kind[4]
    blocks, rows = shifted.shape[2], shifted.shape[3]
    lane = lane_of((ROWS, LANES))
    width = blocks * LANES
    tall = lane_of((limit, LANES))
    for r in range(rows):
        value = jnp.zeros((limit, LANES), jnp.float32)
        for q, (x, col, shift) in enumerate(edges):
            block, turn = (0, q) if shift == -1 else (blocks - 1, q + 1)
            value = jnp.where(tall == q, pltpu.roll(shifted[col, forms.index(shift), block, r, :limit, :], turn, 1), value)
        packed[r] = value
    spans = [slice(lo, lo + ROWS) for lo in range(0, limit, ROWS)]
    group = min(limit // ROWS, 2 if outs == 3 else 4)
    unroll = 8
    for part in range(len(spans) // group):
        mine = []
        for span in spans[part * group : (part + 1) * group]:
            values = None
            for q, (x, col, shift) in enumerate(edges):
                lanes, turn = (slice(0, LANES), q) if shift == -1 else (slice(width - LANES, width), q + 1)
                cell = own_rows(kind, motion_ref, pressure_ref, x, span, lanes)
                cell = [pltpu.roll(v, turn, 1) if turn else v for v in cell]
                cell[0] = cell[0] - float(col - x)
                values = cell if values is None else [jnp.where(lane == q, c, v) for c, v in zip(cell, values)]
            mine.append(values)

        def step(outer, totals):
            totals = list(totals)
            for inner in range(unroll):
                slot = outer * unroll + inner
                their = [jnp.broadcast_to(packed[r, pl.ds(slot, 1), :], (ROWS, LANES)) for r in range(rows)]
                for v in range(group):
                    totals[v] = pair(mine[v], their, totals[v], closeness(displacement(mine[v], their)))
            return tuple(totals)

        zero = jnp.zeros((ROWS, LANES), jnp.float32)
        totals = lax.fori_loop(0, limit // unroll, step, tuple((zero,) * outs for _ in range(group)))
        for v, span in enumerate(spans[part * group : (part + 1) * group]):
            for k in range(outs):
                for q, (x, col, shift) in enumerate(edges):
                    at = 0 if shift == -1 else LANES - 1
                    lanes = slice(0, LANES) if shift == -1 else slice(width - LANES, width)
                    back = pltpu.roll(totals[v][k], (at - q) % LANES, 1) if at != q else totals[v][k]
                    sums[x, k, span, lanes] = sums[x, k, span, lanes] + jnp.where(lane == at, back, 0.0)


def halo_sums(kind, refs, columns, slots, limit, first, last, motion_ref, pressure_ref, shifted, sizes_m, sizes_p, kept_ref):
    spans_m, spans_p = bounds_of(sizes_m), bounds_of(sizes_p)
    for side in range(2):
        m_refs, p_refs = refs[side]
        column = columns - 1 if side == 0 else 0

        def field_of(ref, at, size):
            return ref.at[at : at + size]

        def piece(cells, ends, lo, hi):
            return (cells, ends.at[:, 0:LANES], ends.at[:, LANES : 2 * LANES], lo, hi)

        def motion_pieces(field):
            out = []
            for i, lo, hi in spans_m if field < 6 else [(len(sizes_m) - 1, 0, slots)]:
                size = sizes_m[i]
                ends = field_of(m_refs[i], (4 if i == len(sizes_m) - 1 else 3) * size, size)
                if field < 3 or field == 6:
                    cells = field_of(m_refs[i], min(field, 3) * size, size)
                else:
                    cells = field_of(p_refs[i], 4 * sizes_p[i] + (field - 3) * size, size)
                out.append(piece(cells, ends, lo, hi))
            return out

        def pressure_pieces(field):
            return [
                piece(field_of(p_refs[i], field * sizes_p[i], sizes_p[i]), field_of(p_refs[i], 3 * sizes_p[i], sizes_p[i]), lo, hi)
                for i, lo, hi in spans_p
            ]

        fill_column(shifted, side, kind, motion_pieces, pressure_pieces, lambda f: f * columns + column, SHIFTS)
        x, shift = (0, -1) if side == 0 else (columns - 1, 1)
        add_pairs(
            kind, motion_ref, pressure_ref, shifted, x, [(side, shift)], limit, first, last, kept_ref, side * len(SHIFTS)
        )


def density_rest(motion, partial, messages, sizes, density, entropy, counts, level, limit, slots_sent, keep):
    columns, _, slots, width = motion.shape
    (m_left, m_right) = messages
    first = density is None
    inputs = [motion, partial, entropy, counts] + ([] if first else [density]) + m_left + m_right
    n_in, n_m = len(inputs), len(m_left)
    rows = 4
    kept_shape = jax.ShapeDtypeStruct((2 * len(SHIFTS), width // LANES, slots, limit // ROWS, ROWS, LANES), jnp.float32)

    def kernel(*refs):
        motion_ref, partial_ref, entropy_ref, counts_ref = refs[:4]
        old_ref = None if first else refs[4]
        m_refs = refs[n_in - 2 * n_m : n_in]
        press_ref, left_ref, right_ref, *left = refs[n_in:]
        kept_ref = left[0] if keep else None
        shifted, sums = left[-2:]
        sums[...] = partial_ref[...]

        def start(x, span, lanes):
            return (sums[x, 0, span, lanes],)

        def end(x, span, lanes, total):
            sums[x, 0, span, lanes] = total[0]

        sides = ((m_refs[:n_m], []), (m_refs[n_m:], []))
        halo_sums(DENSITY, sides, columns, slots, limit, start, end, motion_ref, None, shifted, sizes, [], kept_ref)
        for x in range(columns):
            count = counts_ref[level, x : x + 1, :]
            for lo in range(0, slots, ROWS):
                span = slice(lo, lo + ROWS)
                if lo >= limit:
                    if first:
                        value = jnp.ones((ROWS, width), jnp.float32)
                    else:
                        for f in range(3):
                            press_ref[x, f, span, :] = old_ref[x, f, span, :]
                        continue
                else:
                    slot = lax.broadcasted_iota(jnp.int32, (ROWS, width), 0) + lo
                    before = jnp.ones((ROWS, width), jnp.float32) if first else old_ref[x, 2, span, :]
                    value = jnp.where(slot < count, sums[x, 0, span, :], before)
                pressure = entropy_ref[x, span, :] * jnp.exp(jnp.log(value) * (GAMMA - 2.0))
                press_ref[x, 0, span, :] = pressure
                press_ref[x, 1, span, :] = jnp.sqrt(GAMMA * pressure * value)
                press_ref[x, 2, span, :] = value
        pack_ends(lambda f, c, last: end_block(press_ref, c, f, last, slots_sent), PRESSURE, columns, left_ref, right_ref)

    ends = jax.ShapeDtypeStruct((slots_sent, LANES), jnp.float32)
    return pl.pallas_call(
        kernel,
        out_shape=(
            jax.ShapeDtypeStruct((columns, PRESSURE, slots, width), jnp.float32),
            ends,
            ends,
        )
        + ((kept_shape,) if keep else ()),
        in_specs=[VMEM] * n_in,
        out_specs=(VMEM,) * (4 if keep else 3),
        scratch_shapes=[
            pltpu.VMEM((2, 3, width // LANES, rows, slots, LANES), jnp.float32),
            pltpu.VMEM((columns, 1, limit, width), jnp.float32),
        ],
        compiler_params=PARAMS,
        cost_estimate=cost(limit * slots * 6 * width, 30),
    )(*inputs)


def force_rest(motion, pressure, partial, messages_m, messages_p, sizes_m, sizes_p, counts, level, limit, slots_sent, closeness_kept):
    columns, _, slots, width = motion.shape
    n_m, n_p = len(messages_m[0]), len(messages_p[0])
    inputs = [motion, pressure, partial, counts] + messages_m[0] + messages_p[0] + messages_m[1] + messages_p[1]
    inputs += [] if closeness_kept is None else [closeness_kept]
    n_in = len(inputs)
    rows = 10
    ends = jax.ShapeDtypeStruct((slots_sent, LANES), jnp.float32)
    outs = (jax.ShapeDtypeStruct(motion.shape, jnp.float32),) + ((ends, ends) if slots_sent else ())

    def kernel(*refs):
        motion_ref, pressure_ref, partial_ref, counts_ref = refs[:4]
        sides = []
        for side in range(2):
            at = 4 + side * (n_m + n_p)
            sides.append((refs[at : at + n_m], refs[at + n_m : at + n_m + n_p]))
        new_ref = refs[n_in]
        shifted, sums = refs[-2:]
        sums[...] = partial_ref[...]

        def start(x, span, lanes):
            return tuple(sums[x, k, span, lanes] for k in range(3))

        def end(x, span, lanes, total):
            for k in range(3):
                sums[x, k, span, lanes] = total[k]

        halo_sums(
            FORCE, sides, columns, slots, limit, start, end, motion_ref, pressure_ref, shifted, sizes_m, sizes_p,
            None if closeness_kept is None else refs[n_in - 1],
        )
        for x in range(columns):
            count = counts_ref[level, x : x + 1, :]
            new_ref[x, 6, :, :] = motion_ref[x, 6, :, :]
            if limit < slots:
                for f in range(6):
                    new_ref[x, f, limit:, :] = motion_ref[x, f, limit:, :]
            for lo in range(0, limit, ROWS):
                span = slice(lo, lo + ROWS)
                active = lax.broadcasted_iota(jnp.int32, (ROWS, width), 0) + lo < count
                for k in range(3):
                    place, speed = motion_ref[x, k, span, :], motion_ref[x, 3 + k, span, :]
                    faster = speed + TIME_STEP * sums[x, k, span, :]
                    new_ref[x, 3 + k, span, :] = jnp.where(active, faster, speed)
                    new_ref[x, k, span, :] = jnp.where(active, place + TIME_STEP * faster, place)
        if slots_sent:
            left_ref, right_ref = refs[n_in + 1 : n_in + 3]
            pack_ends(lambda f, c, last: end_block(new_ref, c, f, last, slots_sent), 6, columns, left_ref, right_ref)

    made = pl.pallas_call(
        kernel,
        out_shape=outs,
        in_specs=[VMEM] * n_in,
        out_specs=(VMEM,) * len(outs),
        scratch_shapes=[
            pltpu.VMEM((2, 3, width // LANES, rows, slots, LANES), jnp.float32),
            pltpu.VMEM((columns, 3, limit, width), jnp.float32),
        ],
        compiler_params=PARAMS,
        cost_estimate=cost(limit * slots * 6 * width, 60),
    )(*inputs)
    return made if slots_sent else (made[0], None, None)


def ranks(destination, parts):
    rows, width = destination.shape

    def kernel(dest_ref, place_ref, meta_ref):
        dest = dest_ref[...]
        low = lax.broadcasted_iota(jnp.int32, (width, width), 0)
        upto = jnp.where(low <= lane_of((width, width)), 1.0, 0.0).astype(jnp.bfloat16)
        above = lax.broadcasted_iota(jnp.int32, (rows, rows), 0) > lane_of((rows, rows))
        above = jnp.where(above, 1.0, 0.0).astype(jnp.bfloat16)
        lane = lane_of((rows, LANES))
        meta = jnp.zeros((rows, LANES), jnp.float32)
        place = jnp.zeros((rows, width), jnp.float32)
        start = jnp.zeros((rows, 1), jnp.float32)
        for d in range(parts):
            mask = jnp.where(dest == d, 1.0, 0.0)
            inside = jnp.dot(mask.astype(jnp.bfloat16), upto, preferred_element_type=jnp.float32)
            count = inside[:, width - 1 : width]
            wide = jnp.broadcast_to(count, (rows, LANES))
            before = jnp.dot(above, wide.astype(jnp.bfloat16), preferred_element_type=jnp.float32)
            place = place + mask * (inside - 1.0 + start)
            meta = jnp.where(lane == d, before, meta)
            meta = jnp.where(lane == parts + d, jnp.broadcast_to(start, (rows, LANES)), meta)
            meta = jnp.where(lane == 2 * parts + d, before + wide, meta)
            start = start + count
        place_ref[...] = place.astype(jnp.int32)
        meta_ref[...] = meta.astype(jnp.int32)

    return pl.pallas_call(
        kernel,
        out_shape=(jax.ShapeDtypeStruct((rows, width), jnp.int32), jax.ShapeDtypeStruct((rows, LANES), jnp.int32)),
        in_specs=[VMEM],
        out_specs=(VMEM, VMEM),
        compiler_params=PARAMS,
    )(destination)


def compact(motion, pressure, place, meta, here, parts, capacity):
    columns, _, slots, width = motion.shape
    chunks = width // LANES
    total = -(-capacity // LANES)

    def kernel(motion_ref, pressure_ref, place_ref, meta_ref, here_ref, *refs):
        out_refs, (local, lists) = refs[:parts], refs[parts:]
        target = [lax.rem(here_ref[0] + k, parts) for k in range(parts)]
        lane = lane_of((ROWS, LANES))

        def do_group(group, carry):
            span = pl.ds(pl.multiple_of(group * ROWS, ROWS), ROWS)
            fields = [
                [motion_ref[x, f, span, :] for f in range(6)] + [pressure_ref[x, 2, span, :], motion_ref[x, 6, span, :]]
                for x in range(columns)
            ]
            for s in range(ROWS):
                for x in range(columns):
                    state = jnp.concatenate([v[s : s + 1, :] for v in fields[x]], axis=0)
                    high = state.astype(jnp.bfloat16).astype(jnp.float32)
                    rest = state - high
                    middle = rest.astype(jnp.bfloat16).astype(jnp.float32)
                    lowest = rest - middle
                    stacked = jnp.concatenate([high, middle, lowest], axis=0).astype(jnp.bfloat16)
                    row = (group * ROWS + s) * columns + x
                    wanted = place_ref[pl.ds(row, 1), :]
                    hot = jnp.where(lax.broadcasted_iota(jnp.int32, (width, width), 0) == wanted, 1.0, 0.0)
                    moved = lax.dot_general(
                        stacked, hot.astype(jnp.bfloat16), (((1,), (1,)), ((), ())), preferred_element_type=jnp.float32
                    )
                    moved = moved[0:8] + moved[8:16] + moved[16:24]
                    buffer = (s * columns + x) % 4
                    for c in range(chunks):
                        local[buffer, c + 1] = moved[:, c * LANES : (c + 1) * LANES]
                    for d in range(parts):
                        base = meta_ref[row, target[d]]
                        begin = meta_ref[row, parts + target[d]]
                        chunk = lax.shift_right_logical(base, 7)
                        off = lax.bitwise_and(base, LANES - 1)
                        turn = lax.bitwise_and(off - begin, LANES - 1)
                        at = lax.shift_right_logical(begin, 7)
                        at = at + jnp.where(off < lax.bitwise_and(begin, LANES - 1), 1, 0)
                        turned = [pltpu.roll(local[buffer, at + k], turn, 1) for k in range(chunks + 2)]
                        for k in range(chunks + 1):
                            value = jnp.where(lane >= turn, turned[k + 1], turned[k])
                            if k == 0:
                                value = jnp.where(lane >= off, value, lists[d, chunk])
                            lists[d, chunk + k] = value
            return carry

        lax.fori_loop(0, slots // ROWS, do_group, 0)
        for d in range(parts):
            count = meta_ref[slots * columns - 1, 2 * parts + target[d]]
            for c in range(total):
                out_refs[d][:, c * LANES : (c + 1) * LANES] = jnp.where(lane + c * LANES < count, lists[d, c], 0.0)

    return pl.pallas_call(
        kernel,
        out_shape=(jax.ShapeDtypeStruct((8, capacity), jnp.float32),) * parts,
        in_specs=[VMEM, VMEM, VMEM, SMEM, SMEM],
        out_specs=(VMEM,) * parts,
        scratch_shapes=[
            pltpu.VMEM((4, 2 * chunks + 4, ROWS, LANES), jnp.float32),
            pltpu.VMEM((parts, total + chunks + 2, ROWS, LANES), jnp.float32),
        ],
        compiler_params=PARAMS,
    )(motion, pressure, place, meta, here)


def in_order(here, received):
    parts = len(received)
    rows, capacity = received[0].shape

    def kernel(here_ref, *refs):
        out_ref = refs[parts]
        for k in range(parts):

            @pl.when(pl.program_id(0) == k)
            def _():
                out_ref[...] = refs[k][...]

    return pl.pallas_call(
        kernel,
        out_shape=jax.ShapeDtypeStruct((rows, parts * capacity), jnp.float32),
        grid_spec=pltpu.PrefetchScalarGridSpec(
            num_scalar_prefetch=1,
            grid=(parts,),
            in_specs=[VMEM] * parts,
            out_specs=pl.BlockSpec((rows, capacity), lambda k, here_ref: (0, lax.rem(here_ref[0] - k + parts, parts))),
        ),
        compiler_params=PARAMS,
    )(here, *received)


def pass_on(value, axis, step):
    count = lax.axis_size(axis)
    return lax.ppermute(value, axis, [(i, (i + step) % count) for i in range(count)])


def swap_ends(left_ends, right_ends):
    return pass_on(right_ends, "sub", 1), pass_on(left_ends, "sub", -1)


def swap_columns(parts_of):
    first = jnp.concatenate(parts_of(0), axis=0)
    final = jnp.concatenate(parts_of(-1), axis=0)
    return pass_on(final, "tile", 1), pass_on(first, "tile", -1)


def rows_of(fields):
    return fields.reshape(-1, fields.shape[-1])


def beside(ends, width):
    plane = jnp.concatenate(ends, axis=1)
    return jnp.pad(plane, ((0, 0), (0, width - plane.shape[1])))


def shards(offsets, velocity, mass, entropy, active_counts, targets):
    slots, columns, width = mass.shape
    levels = active_counts.shape[0]
    parts = lax.axis_size("sub")
    slot_index = lax.broadcasted_iota(jnp.int32, mass.shape, 0)
    mass_live = jnp.where(slot_index < active_counts[0][None], mass, 0.0)
    motion = jnp.concatenate([offsets, velocity, mass_live[None]], axis=0).transpose(2, 0, 1, 3)
    entropy = entropy.transpose(1, 0, 2)
    limits = (slots, slots // 2, slots // 4)
    pressure = None
    ends_m, ends_p, sizes_m, sizes_p = [], [], [], []
    left_m, right_m, left_p, right_p = [], [], [], []
    made = first_ends(motion)
    place, meta = ranks(targets.reshape(slots * columns, width), parts)
    for level in range(levels):
        limit = limits[level]
        sent = limits[max(level - 1, 0)]
        ends_m.insert(0, swap_ends(*made))
        partial, *inner_kept = own_part(DENSITY, motion, None, ends_m, [], limit, (0,), keep=KEEP[level][0])
        ends_m[0], partial = lax.optimization_barrier((ends_m[0], partial))
        plane = beside(ends_m[0], width)
        masses = (lambda c: [motion[c, 6]]) if level == 0 else (lambda c: [])
        cells = swap_columns(lambda c: [rows_of(motion[c, :3, :sent]), *masses(c), plane])
        sizes_m.insert(0, sent)
        left_m.insert(0, cells[0])
        right_m.insert(0, cells[1])
        partial, *outer_kept = own_part(DENSITY, motion, None, ends_m, [], limit, (-1, 1), partial, keep=KEEP[level][1])
        pressure, *made = density_rest(motion, partial, (left_m, right_m), sizes_m, pressure, entropy, active_counts, level, limit, limit, KEEP[level][2])
        rest_kept = made.pop() if KEEP[level][2] else None
        ends_p.insert(0, swap_ends(*made))
        (partial,) = own_part(FORCE, motion, pressure, ends_m, ends_p, limit, (0,), None, *inner_kept)
        ends_p[0], partial = lax.optimization_barrier((ends_p[0], partial))
        plane = beside(ends_p[0], width)
        cells = swap_columns(lambda c: [rows_of(pressure[c, :, :limit]), plane, rows_of(motion[c, 3:6, :sent])])
        sizes_p.insert(0, limit)
        left_p.insert(0, cells[0])
        right_p.insert(0, cells[1])
        (partial,) = own_part(FORCE, motion, pressure, ends_m, ends_p, limit, (-1, 1), partial, *outer_kept)
        more = limit if level < levels - 1 else 0
        motion, *made = force_rest(
            motion, pressure, partial, (left_m, right_m), (left_p, right_p), sizes_m, sizes_p, active_counts, level, limit, more, rest_kept
        )
    capacity = 3 * slots * columns * width // 8
    here = lax.axis_index("sub").astype(jnp.int32).reshape(1)
    lists = compact(motion, pressure, place, meta[:, : 3 * parts], here, parts, capacity)
    received = {0: lists[0]}
    for k in sorted(range(1, parts), key=lambda k: -min(k, parts - k)):
        received[k] = pass_on(lists[k], "sub", k)
    return in_order(here, [received[k] for k in range(parts)])


def solution(mesh):
    placed = (
        P(None, None, "tile", "sub"),
        P(None, None, "tile", "sub"),
        P(None, "tile", "sub"),
        P(None, "tile", "sub"),
        P(None, "tile", "sub"),
        P(None, "tile", "sub"),
    )
    return jax.shard_map(
        shards, mesh=mesh, in_specs=placed, out_specs=P(None, ("tile", "sub")), check_vma=False
    )
```

```python
import functools
import math

import jax
import jax.numpy as jnp
from jax import lax
from jax.experimental import pallas as pl
from jax.experimental.pallas import tpu as pltpu
from jax.sharding import PartitionSpec as P

KERNEL_NORM = 21.0 / (2.0 * math.pi)
GAMMA = 5.0 / 3.0
TIME_STEP = 0.05
SOFTEN = 0.01
LANES = 128
ROWS = 8
VMEM = pl.BlockSpec(memory_space=pltpu.VMEM)
SMEM = pl.BlockSpec(memory_space=pltpu.SMEM)
PARAMS = pltpu.CompilerParams(vmem_limit_bytes=24 << 20)
MOTION, PRESSURE = 7, 3
SHIFTS = (-1, 0, 1)
KEEP = ((True, True, True), (True, True, True), (False, False, False))


def lane_of(shape):
    return lax.broadcasted_iota(jnp.int32, shape, 1)


def cost(pairs, ops):
    return pl.CostEstimate(flops=int(pairs * ops * 15), bytes_accessed=1 << 20, transcendentals=0)


def closeness(delta):
    dx, dy, dz = delta
    squared = dx * dx + dy * dy + dz * dz
    radius = squared * lax.rsqrt(jnp.maximum(squared, 1e-30))
    return jnp.maximum(1.0 - radius, 0.0), squared


def displacement(own, their):
    return tuple(i - j for i, j in zip(own[:3], their[:3]))


def force_core(own, their, near):
    remain, squared = near
    if squared is None:
        squared = (1.0 - remain) * (1.0 - remain)
    ui, vi, wi, qi, ci, ri = own[3:9]
    uj, vj, wj, qj, cj, rj = their[3:9]
    dx, dy, dz = displacement(own, their)
    approach = dx * (ui - uj) + dy * (vi - vj) + dz * (wi - wj)
    closing = jnp.minimum(approach, 0.0) * pl.reciprocal(squared + SOFTEN, approx=True)
    viscous = closing * (closing - (ci + cj)) * pl.reciprocal(ri + rj, approx=True)
    return (dx, dy, dz), qi + qj + viscous


def pair_force(own, their, total, near):
    remain = near[0]
    delta, pressure = force_core(own, their, near)
    strength = pressure * ((remain * remain) * (remain * their[-1]))
    return tuple(t + strength * d for t, d in zip(total, delta))


def pair_density(own, their, total, near):
    remain = near[0]
    square = remain * remain
    return (total[0] + (square * square) * ((5.0 - 4.0 * remain) * their[-1]),)


def both_force(own, their, total, near):
    remain = near[0]
    delta, pressure = force_core(own, their, near)
    strength = pressure * ((remain * remain) * remain)
    on_own, on_their = strength * their[-1], strength * own[-1]
    return tuple(t + on_own * d for t, d in zip(total, delta)), tuple(on_their * d for d in delta)


def both_density(own, their, total, near):
    remain = near[0]
    square = remain * remain
    weight = (square * square) * (5.0 - 4.0 * remain)
    return (total[0] + weight * their[-1],), (weight * own[-1],)


def kept(kept_ref, at, own, their, first):
    if kept_ref is not None and not first:
        return kept_ref[at], None
    near = closeness(displacement(own, their))
    if kept_ref is not None:
        kept_ref[at] = near[0]
    return near


DENSITY = ((0, 1.0), (1, 1.0), (2, 1.0)), (), ((6, KERNEL_NORM),), pair_density, 1
FORCE = (
    tuple((c, 1.0) for c in range(3)) + tuple((c, 4.0) for c in range(3, 6)),
    ((0, 1.0), (1, 1.0), (2, 4.0)),
    ((6, 20.0 * KERNEL_NORM),),
    pair_force,
    3,
)


def fill_shifted(shifted, col, row, pieces, scale, group, shifts, is_y):
    for cells, left, right, lo, hi in pieces:
        count = cells.shape[-1] // LANES
        blocks = [cells[lo:hi, b * LANES : (b + 1) * LANES] for b in range(count)]
        if scale != 1.0:
            blocks = [v * scale for v in blocks]
        lane = lane_of(blocks[0].shape)
        for at, shift in enumerate(shifts):
            values = blocks
            if shift == -1:
                turned = [pltpu.roll(v, 1, 1) for v in blocks]
                end = pltpu.roll(left[lo:hi, :], (LANES - group) % LANES, 1) if group else left[lo:hi, :]
                turned = [end if scale == 1.0 else end * scale] + turned
                values = [jnp.where(lane == 0, turned[b], turned[b + 1]) for b in range(count)]
            elif shift == 1:
                turned = [pltpu.roll(v, LANES - 1, 1) for v in blocks]
                end = pltpu.roll(right[lo:hi, :], LANES - 1 - group, 1)
                turned.append(end if scale == 1.0 else end * scale)
                values = [jnp.where(lane == LANES - 1, turned[b + 1], turned[b]) for b in range(count)]
            if is_y and shift:
                values = [v + float(shift) for v in values]
            for b in range(count):
                shifted[col, at, b, row, lo:hi, :] = values[b]


def fill_column(shifted, col, kind, motion, pressure, group_of, shifts):
    moved, pressed, massed, _, _ = kind
    row = 0
    for pieces, fields in ((motion, moved), (pressure, pressed), (motion, massed)):
        for field, scale in fields:
            is_y = fields is moved and field == 1
            fill_shifted(shifted, col, row, pieces(field), scale, group_of(field), shifts, is_y)
            row += 1


def add_pairs(kind, motion_ref, pressure_ref, shifted, x, sources, limit, first, last, kept_ref, unit, start=0):
    moved, pressed, _, pair, width = kind
    slots = shifted.shape[-2]
    blocks = shifted.shape[2]
    rows = shifted.shape[3]
    group = min(limit // ROWS, 2 if width == 3 else 4)
    unroll = min(slots - start, 16 // group if width == 3 else 32 // group)
    forms = shifted.shape[1]
    low_col, low_shift = sources[0]

    def lane_block(b, carry):
        lanes = pl.ds(pl.multiple_of(b * LANES, LANES), LANES)
        for part in range(limit // (ROWS * group)):
            spans = [slice((part * group + v) * ROWS, (part * group + v + 1) * ROWS) for v in range(group)]
            own = []
            for span in spans:
                values = [motion_ref[x, f, span, lanes] * s if s != 1.0 else motion_ref[x, f, span, lanes] for f, s in moved]
                values += [pressure_ref[x, f, span, lanes] * s if s != 1.0 else pressure_ref[x, f, span, lanes] for f, s in pressed]
                own.append(values)

            def source(at, totals):
                col = at // forms
                shift = at - forms * col
                offset = (col + low_shift).astype(jnp.float32)
                mine = [[v[0] - offset] + v[1:] for v in own]

                def step(outer, totals):
                    totals = list(totals)
                    for inner in range(unroll):
                        slot = outer * unroll + inner
                        their = [
                            jnp.broadcast_to(shifted[col + low_col, shift, b, r, pl.ds(slot, 1), :], (ROWS, LANES))
                            for r in range(rows)
                        ]
                        for v in range(group):
                            place = (unit + at, b, slot * (limit // ROWS) + part * group + v)
                            remain = kept(kept_ref, place, mine[v], their, width == 1)
                            totals[v] = pair(mine[v], their, totals[v], remain)
                    return tuple(totals)

                return lax.fori_loop(start // unroll, slots // unroll, step, totals)

            totals = tuple(first(x, span, lanes) for span in spans)
            totals = lax.fori_loop(0, forms * len(sources), source, totals)
            for span, total in zip(spans, totals):
                last(x, span, lanes, total)
        return carry

    lax.fori_loop(0, blocks, lane_block, 0)


def own_sources(x, columns):
    return [(c, c - x) for c in range(columns) if abs(c - x) <= 1]


def pack_ends(field_of, fields, columns, left_ref, right_ref):
    for ref, at_last in ((left_ref, False), (right_ref, True)):
        lane = None
        packed = None
        for group in range(fields * columns):
            block = field_of(group // columns, group % columns, at_last)
            if lane is None:
                lane = lane_of(block.shape)
                packed = jnp.zeros(block.shape, jnp.float32)
            turn = (group + 1) % LANES if at_last else group
            packed = jnp.where(lane == group, pltpu.roll(block, turn, 1) if turn else block, packed)
        ref[...] = packed


def end_block(ref, column, field, at_last, limit):
    width = ref.shape[-1]
    lanes = slice(width - LANES, width) if at_last else slice(0, LANES)
    return ref[column, field, :limit, lanes]


def first_ends(motion):
    columns, _, slots, _ = motion.shape

    def kernel(motion_ref, left_ref, right_ref):
        pack_ends(
            lambda f, c, last: end_block(motion_ref, c, f, last, slots), MOTION, columns, left_ref, right_ref
        )

    ends = jax.ShapeDtypeStruct((slots, LANES), jnp.float32)
    return pl.pallas_call(kernel, out_shape=(ends, ends), in_specs=[VMEM], out_specs=(VMEM, VMEM), compiler_params=PARAMS)(motion)


def bounds_of(sizes):
    spans, lo = [], 0
    for index, hi in enumerate(sizes):
        if hi > lo:
            spans.append((index, lo, hi))
            lo = hi
    return spans


def own_part(kind, motion, pressure, ends_m, ends_p, limit, shifts, partial=None, closeness_kept=None, keep=False):
    columns, _, slots, width = motion.shape
    moved, pressed, massed, _, outs = kind
    inner = shifts == (0,)
    mutual = 2 * limit >= slots
    if inner:
        ends_m = ends_p = []
    flat_m = [e for pair in ends_m for e in pair]
    flat_p = [e for pair in ends_p for e in pair]
    whole = [(0, 0, slots)]
    spans_m = whole if inner else bounds_of([e[0].shape[0] for e in ends_m])
    spans_p = whole if inner else bounds_of([e[0].shape[0] for e in ends_p])
    inputs = [motion] + ([pressure] if pressed else []) + flat_m + flat_p + ([] if partial is None else [partial])
    n_in = len(inputs)
    calls = []
    for x in range(columns):
        for col, _ in own_sources(x, columns):
            start = limit if mutual and not (inner and col == x) else 0
            if start < slots:
                calls.append((x, col, start, None))
    if mutual:
        for x in range(columns):
            for col in (x, x + 1):
                for form, shift in enumerate(shifts):
                    if col < columns and (col != x or shift == 1):
                        calls.append((x, col, 0, form))
    units = sum(len(shifts) if form is None else 1 for *_, form in calls)
    kept_shape = jax.ShapeDtypeStruct((units, width // LANES, slots * limit // ROWS, ROWS, LANES), jnp.float32)
    keep = keep and not pressed
    if closeness_kept is not None:
        inputs.append(closeness_kept)
    rows = len(moved) + len(pressed) + len(massed)

    def kernel(*own_refs):
        refs = list(own_refs)
        motion_ref = refs.pop(0)
        pressure_ref = refs.pop(0) if pressed else None
        m_refs = refs[: len(flat_m)]
        p_refs = refs[len(flat_m) : len(flat_m) + len(flat_p)]
        partial_ref = None if partial is None else own_refs[n_in - 1]
        left = list(own_refs[n_in:])
        kept_ref = None if closeness_kept is None else left.pop(0)
        out_ref = left.pop(0)
        if keep:
            kept_ref = left.pop(0)
        shifted, *mutual_refs = left

        def pieces(cells, ends, spans):
            if inner:
                return [(cells, None, None, 0, slots)]
            return [(cells, ends[2 * i], ends[2 * i + 1], lo, hi) for i, lo, hi in spans]

        for c in range(columns):

            def motion_pieces(field):
                return pieces(motion_ref.at[c, field], m_refs, spans_m if field < 6 else [(len(ends_m) - 1, 0, slots)])

            def pressure_pieces(field):
                return pieces(pressure_ref.at[c, field], p_refs, spans_p)

            fill_column(shifted, c, kind, motion_pieces, pressure_pieces, lambda f: f * columns + c, shifts)

        def first(x, span, lanes):
            return tuple(out_ref[x, k, span, lanes] for k in range(outs))

        def last(x, span, lanes, total):
            for k in range(outs):
                out_ref[x, k, span, lanes] = total[k]

        out_ref[...] = jnp.zeros(out_ref.shape, jnp.float32) if partial is None else partial_ref[...]
        edges, unit = [], 0
        for x, col, start, form in calls:
            if form is None:
                add_pairs(
                    kind, motion_ref, pressure_ref, shifted, x, [(col, col - x)], limit, first, last, kept_ref, unit, start
                )
                unit += len(shifts)
                continue
            parts, reaction, packed = mutual_refs
            both_ways(
                kind, motion_ref, pressure_ref, shifted, x, col, form, out_ref, parts, reaction, limit, kept_ref, unit
            )
            take_reaction(out_ref, reaction, col, shifts[form], outs)
            unit += 1
            if shifts[form]:
                edges.append((col, x, -shifts[form]))
        if edges:
            edge_pairs(kind, motion_ref, pressure_ref, shifted, shifts, edges, out_ref, packed, limit)

    sums_shape = jax.ShapeDtypeStruct((columns, outs, limit, width), jnp.float32)
    return pl.pallas_call(
        kernel,
        out_shape=(sums_shape, kept_shape) if keep else (sums_shape,),
        in_specs=[VMEM] * len(inputs),
        out_specs=(VMEM, VMEM) if keep else (VMEM,),
        scratch_shapes=[pltpu.VMEM((columns, len(shifts), width // LANES, rows, slots, LANES), jnp.float32)]
        + (
            [
                pltpu.VMEM((outs, limit, ROWS, LANES), jnp.float32),
                pltpu.VMEM((outs, width // LANES, limit, LANES), jnp.float32),
                pltpu.VMEM((rows, limit, LANES), jnp.float32),
            ]
            if mutual
            else []
        ),
        compiler_params=PARAMS,
        cost_estimate=cost(limit * slots * len(shifts) * (3 * columns - 2) * width, 60 if outs == 3 else 30),
    )(*inputs)


def sum_rows(values):
    row = lax.broadcasted_iota(jnp.int32, (ROWS, LANES), 0)
    step = 1
    while len(values) > 1:
        low = lax.bitwise_and(row, step) == 0
        values = [
            jnp.where(low, a, b) + pltpu.roll(jnp.where(low, b, a), step, 0) for a, b in zip(values[::2], values[1::2])
        ]
        step *= 2
    return values[0]


def own_rows(kind, motion_ref, pressure_ref, x, span, lanes):
    moved, pressed, massed = kind[:3]
    rows = [(motion_ref, f, s) for f, s in moved] + [(pressure_ref, f, s) for f, s in pressed] + [(motion_ref, f, s) for f, s in massed]
    return [ref[x, f, span, lanes] * s if s != 1.0 else ref[x, f, span, lanes] for ref, f, s in rows]


def both_ways(kind, motion_ref, pressure_ref, shifted, x, col, form, sums, parts, reaction, limit, kept_ref, unit):
    outs = kind[4]
    blocks, rows = shifted.shape[2], shifted.shape[3]
    both = both_force if outs == 3 else both_density
    sign = -1.0 if outs == 3 else 1.0
    group = min(limit // ROWS, 2 if outs == 3 else 4)
    unroll = 8

    def lane_block(b, carry):
        lanes = pl.ds(pl.multiple_of(b * LANES, LANES), LANES)
        for part in range(limit // (ROWS * group)):
            spans = [slice((part * group + v) * ROWS, (part * group + v + 1) * ROWS) for v in range(group)]
            mine = []
            for span in spans:
                values = own_rows(kind, motion_ref, pressure_ref, x, span, lanes)
                mine.append([values[0] - float(col - x)] + values[1:])

            def step(outer, totals):
                totals = list(totals)
                for inner in range(unroll):
                    slot = outer * unroll + inner
                    their = [jnp.broadcast_to(shifted[col, form, b, r, pl.ds(slot, 1), :], (ROWS, LANES)) for r in range(rows)]
                    back = None
                    for v in range(group):
                        place = (unit, b, slot * (limit // ROWS) + part * group + v)
                        remain = kept(kept_ref, place, mine[v], their, outs == 1)
                        totals[v], given = both(mine[v], their, totals[v], remain)
                        back = given if back is None else tuple(p + q for p, q in zip(back, given))
                    for k in range(outs):
                        parts[k, slot] = back[k] if part == 0 else parts[k, slot] + back[k]
                return tuple(totals)

            totals = tuple(tuple(sums[x, k, span, lanes] for k in range(outs)) for span in spans)
            totals = lax.fori_loop(0, limit // unroll, step, totals)
            for span, total in zip(spans, totals):
                for k in range(outs):
                    sums[x, k, span, lanes] = total[k]
        for k in range(outs):
            for lo in range(0, limit, ROWS):
                reaction[k, b, lo : lo + ROWS, :] = sign * sum_rows([parts[k, lo + r] for r in range(ROWS)])
        return carry

    lax.fori_loop(0, blocks, lane_block, 0)


def take_reaction(sums, reaction, col, shift, outs):
    blocks, slots = reaction.shape[1], reaction.shape[2]
    lane = lane_of((slots, LANES))
    for k in range(outs):
        values = [reaction[k, b] for b in range(blocks)]
        if shift == 1:
            turned = [jnp.zeros((slots, LANES), jnp.float32)] + [pltpu.roll(v, 1, 1) for v in values]
            values = [jnp.where(lane == 0, turned[b], turned[b + 1]) for b in range(blocks)]
        elif shift == -1:
            turned = [pltpu.roll(v, LANES - 1, 1) for v in values] + [jnp.zeros((slots, LANES), jnp.float32)]
            values = [jnp.where(lane == LANES - 1, turned[b + 1], turned[b]) for b in range(blocks)]
        for b in range(blocks):
            lanes = slice(b * LANES, (b + 1) * LANES)
            sums[col, k, :, lanes] = sums[col, k, :, lanes] + values[b]


def edge_pairs(kind, motion_ref, pressure_ref, shifted, forms, edges, sums, packed, limit):
    pair, outs = kind[3], kind[4]
    blocks, rows = shifted.shape[2], shifted.shape[3]
    lane = lane_of((ROWS, LANES))
    width = blocks * LANES
    tall = lane_of((limit, LANES))
    for r in range(rows):
        value = jnp.zeros((limit, LANES), jnp.float32)
        for q, (x, col, shift) in enumerate(edges):
            block, turn = (0, q) if shift == -1 else (blocks - 1, q + 1)
            value = jnp.where(tall == q, pltpu.roll(shifted[col, forms.index(shift), block, r, :limit, :], turn, 1), value)
        packed[r] = value
    spans = [slice(lo, lo + ROWS) for lo in range(0, limit, ROWS)]
    group = min(limit // ROWS, 2 if outs == 3 else 4)
    unroll = 8
    for part in range(len(spans) // group):
        mine = []
        for span in spans[part * group : (part + 1) * group]:
            values = None
            for q, (x, col, shift) in enumerate(edges):
                lanes, turn = (slice(0, LANES), q) if shift == -1 else (slice(width - LANES, width), q + 1)
                cell = own_rows(kind, motion_ref, pressure_ref, x, span, lanes)
                cell = [pltpu.roll(v, turn, 1) if turn else v for v in cell]
                cell[0] = cell[0] - float(col - x)
                values = cell if values is None else [jnp.where(lane == q, c, v) for c, v in zip(cell, values)]
            mine.append(values)

        def step(outer, totals):
            totals = list(totals)
            for inner in range(unroll):
                slot = outer * unroll + inner
                their = [jnp.broadcast_to(packed[r, pl.ds(slot, 1), :], (ROWS, LANES)) for r in range(rows)]
                for v in range(group):
                    totals[v] = pair(mine[v], their, totals[v], closeness(displacement(mine[v], their)))
            return tuple(totals)

        zero = jnp.zeros((ROWS, LANES), jnp.float32)
        totals = lax.fori_loop(0, limit // unroll, step, tuple((zero,) * outs for _ in range(group)))
        for v, span in enumerate(spans[part * group : (part + 1) * group]):
            for k in range(outs):
                for q, (x, col, shift) in enumerate(edges):
                    at = 0 if shift == -1 else LANES - 1
                    lanes = slice(0, LANES) if shift == -1 else slice(width - LANES, width)
                    back = pltpu.roll(totals[v][k], (at - q) % LANES, 1) if at != q else totals[v][k]
                    sums[x, k, span, lanes] = sums[x, k, span, lanes] + jnp.where(lane == at, back, 0.0)


def halo_sums(kind, refs, columns, slots, limit, first, last, motion_ref, pressure_ref, shifted, sizes_m, sizes_p, kept_ref):
    spans_m, spans_p = bounds_of(sizes_m), bounds_of(sizes_p)
    for side in range(2):
        m_refs, p_refs = refs[side]
        column = columns - 1 if side == 0 else 0

        def field_of(ref, at, size):
            return ref.at[at : at + size]

        def piece(cells, ends, lo, hi):
            return (cells, ends.at[:, 0:LANES], ends.at[:, LANES : 2 * LANES], lo, hi)

        def motion_pieces(field):
            out = []
            for i, lo, hi in spans_m if field < 6 else [(len(sizes_m) - 1, 0, slots)]:
                size = sizes_m[i]
                ends = field_of(m_refs[i], (4 if i == len(sizes_m) - 1 else 3) * size, size)
                if field < 3 or field == 6:
                    cells = field_of(m_refs[i], min(field, 3) * size, size)
                else:
                    cells = field_of(p_refs[i], 4 * sizes_p[i] + (field - 3) * size, size)
                out.append(piece(cells, ends, lo, hi))
            return out

        def pressure_pieces(field):
            return [
                piece(field_of(p_refs[i], field * sizes_p[i], sizes_p[i]), field_of(p_refs[i], 3 * sizes_p[i], sizes_p[i]), lo, hi)
                for i, lo, hi in spans_p
            ]

        fill_column(shifted, side, kind, motion_pieces, pressure_pieces, lambda f: f * columns + column, SHIFTS)
        x, shift = (0, -1) if side == 0 else (columns - 1, 1)
        add_pairs(
            kind, motion_ref, pressure_ref, shifted, x, [(side, shift)], limit, first, last, kept_ref, side * len(SHIFTS)
        )


def density_rest(motion, partial, messages, sizes, density, entropy, counts, level, limit, slots_sent, keep):
    columns, _, slots, width = motion.shape
    (m_left, m_right) = messages
    first = density is None
    inputs = [motion, partial, entropy, counts] + ([] if first else [density]) + m_left + m_right
    n_in, n_m = len(inputs), len(m_left)
    rows = 4
    kept_shape = jax.ShapeDtypeStruct((2 * len(SHIFTS), width // LANES, slots * limit // ROWS, ROWS, LANES), jnp.float32)

    def kernel(*refs):
        motion_ref, partial_ref, entropy_ref, counts_ref = refs[:4]
        old_ref = None if first else refs[4]
        m_refs = refs[n_in - 2 * n_m : n_in]
        press_ref, left_ref, right_ref, *left = refs[n_in:]
        kept_ref = left[0] if keep else None
        shifted, sums = left[-2:]
        sums[...] = partial_ref[...]

        def start(x, span, lanes):
            return (sums[x, 0, span, lanes],)

        def end(x, span, lanes, total):
            sums[x, 0, span, lanes] = total[0]

        sides = ((m_refs[:n_m], []), (m_refs[n_m:], []))
        halo_sums(DENSITY, sides, columns, slots, limit, start, end, motion_ref, None, shifted, sizes, [], kept_ref)
        for x in range(columns):
            count = counts_ref[level, x : x + 1, :]
            for lo in range(0, slots, ROWS):
                span = slice(lo, lo + ROWS)
                if lo >= limit:
                    if first:
                        value = jnp.ones((ROWS, width), jnp.float32)
                    else:
                        for f in range(3):
                            press_ref[x, f, span, :] = old_ref[x, f, span, :]
                        continue
                else:
                    slot = lax.broadcasted_iota(jnp.int32, (ROWS, width), 0) + lo
                    before = jnp.ones((ROWS, width), jnp.float32) if first else old_ref[x, 2, span, :]
                    value = jnp.where(slot < count, sums[x, 0, span, :], before)
                pressure = entropy_ref[x, span, :] * jnp.exp(jnp.log(value) * (GAMMA - 2.0))
                press_ref[x, 0, span, :] = pressure
                press_ref[x, 1, span, :] = jnp.sqrt(GAMMA * pressure * value)
                press_ref[x, 2, span, :] = value
        pack_ends(lambda f, c, last: end_block(press_ref, c, f, last, slots_sent), PRESSURE, columns, left_ref, right_ref)

    ends = jax.ShapeDtypeStruct((slots_sent, LANES), jnp.float32)
    return pl.pallas_call(
        kernel,
        out_shape=(
            jax.ShapeDtypeStruct((columns, PRESSURE, slots, width), jnp.float32),
            ends,
            ends,
        )
        + ((kept_shape,) if keep else ()),
        in_specs=[VMEM] * n_in,
        out_specs=(VMEM,) * (4 if keep else 3),
        scratch_shapes=[
            pltpu.VMEM((2, 3, width // LANES, rows, slots, LANES), jnp.float32),
            pltpu.VMEM((columns, 1, limit, width), jnp.float32),
        ],
        compiler_params=PARAMS,
        cost_estimate=cost(limit * slots * 6 * width, 30),
    )(*inputs)


def force_rest(motion, pressure, partial, messages_m, messages_p, sizes_m, sizes_p, counts, level, limit, slots_sent, closeness_kept):
    columns, _, slots, width = motion.shape
    n_m, n_p = len(messages_m[0]), len(messages_p[0])
    inputs = [motion, pressure, partial, counts] + messages_m[0] + messages_p[0] + messages_m[1] + messages_p[1]
    inputs += [] if closeness_kept is None else [closeness_kept]
    n_in = len(inputs)
    rows = 10
    ends = jax.ShapeDtypeStruct((slots_sent, LANES), jnp.float32)
    outs = (jax.ShapeDtypeStruct(motion.shape, jnp.float32),) + ((ends, ends) if slots_sent else ())

    def kernel(*refs):
        motion_ref, pressure_ref, partial_ref, counts_ref = refs[:4]
        sides = []
        for side in range(2):
            at = 4 + side * (n_m + n_p)
            sides.append((refs[at : at + n_m], refs[at + n_m : at + n_m + n_p]))
        new_ref = refs[n_in]
        shifted, sums = refs[-2:]
        sums[...] = partial_ref[...]

        def start(x, span, lanes):
            return tuple(sums[x, k, span, lanes] for k in range(3))

        def end(x, span, lanes, total):
            for k in range(3):
                sums[x, k, span, lanes] = total[k]

        halo_sums(
            FORCE, sides, columns, slots, limit, start, end, motion_ref, pressure_ref, shifted, sizes_m, sizes_p,
            None if closeness_kept is None else refs[n_in - 1],
        )
        for x in range(columns):
            count = counts_ref[level, x : x + 1, :]
            new_ref[x, 6, :, :] = motion_ref[x, 6, :, :]
            if limit < slots:
                for f in range(6):
                    new_ref[x, f, limit:, :] = motion_ref[x, f, limit:, :]
            for lo in range(0, limit, ROWS):
                span = slice(lo, lo + ROWS)
                active = lax.broadcasted_iota(jnp.int32, (ROWS, width), 0) + lo < count
                for k in range(3):
                    place, speed = motion_ref[x, k, span, :], motion_ref[x, 3 + k, span, :]
                    faster = speed + TIME_STEP * sums[x, k, span, :]
                    new_ref[x, 3 + k, span, :] = jnp.where(active, faster, speed)
                    new_ref[x, k, span, :] = jnp.where(active, place + TIME_STEP * faster, place)
        if slots_sent:
            left_ref, right_ref = refs[n_in + 1 : n_in + 3]
            pack_ends(lambda f, c, last: end_block(new_ref, c, f, last, slots_sent), 6, columns, left_ref, right_ref)

    made = pl.pallas_call(
        kernel,
        out_shape=outs,
        in_specs=[VMEM] * n_in,
        out_specs=(VMEM,) * len(outs),
        scratch_shapes=[
            pltpu.VMEM((2, 3, width // LANES, rows, slots, LANES), jnp.float32),
            pltpu.VMEM((columns, 3, limit, width), jnp.float32),
        ],
        compiler_params=PARAMS,
        cost_estimate=cost(limit * slots * 6 * width, 60),
    )(*inputs)
    return made if slots_sent else (made[0], None, None)


def ranks(destination, parts):
    rows, width = destination.shape

    def kernel(dest_ref, place_ref, meta_ref):
        dest = dest_ref[...]
        low = lax.broadcasted_iota(jnp.int32, (width, width), 0)
        upto = jnp.where(low <= lane_of((width, width)), 1.0, 0.0).astype(jnp.bfloat16)
        above = lax.broadcasted_iota(jnp.int32, (rows, rows), 0) > lane_of((rows, rows))
        above = jnp.where(above, 1.0, 0.0).astype(jnp.bfloat16)
        lane = lane_of((rows, LANES))
        meta = jnp.zeros((rows, LANES), jnp.float32)
        place = jnp.zeros((rows, width), jnp.float32)
        start = jnp.zeros((rows, 1), jnp.float32)
        for d in range(parts):
            mask = jnp.where(dest == d, 1.0, 0.0)
            inside = jnp.dot(mask.astype(jnp.bfloat16), upto, preferred_element_type=jnp.float32)
            count = inside[:, width - 1 : width]
            wide = jnp.broadcast_to(count, (rows, LANES))
            before = jnp.dot(above, wide.astype(jnp.bfloat16), preferred_element_type=jnp.float32)
            place = place + mask * (inside - 1.0 + start)
            meta = jnp.where(lane == d, before, meta)
            meta = jnp.where(lane == parts + d, jnp.broadcast_to(start, (rows, LANES)), meta)
            meta = jnp.where(lane == 2 * parts + d, before + wide, meta)
            start = start + count
        place_ref[...] = place.astype(jnp.int32)
        meta_ref[...] = meta.astype(jnp.int32)

    return pl.pallas_call(
        kernel,
        out_shape=(jax.ShapeDtypeStruct((rows, width), jnp.int32), jax.ShapeDtypeStruct((rows, LANES), jnp.int32)),
        in_specs=[VMEM],
        out_specs=(VMEM, VMEM),
        compiler_params=PARAMS,
    )(destination)


def compact(motion, pressure, place, meta, here, parts, capacity):
    columns, _, slots, width = motion.shape
    chunks = width // LANES
    total = -(-capacity // LANES)

    def kernel(motion_ref, pressure_ref, place_ref, meta_ref, here_ref, *refs):
        out_refs, (local, lists) = refs[:parts], refs[parts:]
        target = [lax.rem(here_ref[0] + k, parts) for k in range(parts)]
        lane = lane_of((ROWS, LANES))

        def do_group(group, carry):
            span = pl.ds(pl.multiple_of(group * ROWS, ROWS), ROWS)
            fields = [
                [motion_ref[x, f, span, :] for f in range(6)] + [pressure_ref[x, 2, span, :], motion_ref[x, 6, span, :]]
                for x in range(columns)
            ]
            for s in range(ROWS):
                for x in range(columns):
                    state = jnp.concatenate([v[s : s + 1, :] for v in fields[x]], axis=0)
                    high = state.astype(jnp.bfloat16).astype(jnp.float32)
                    rest = state - high
                    middle = rest.astype(jnp.bfloat16).astype(jnp.float32)
                    lowest = rest - middle
                    stacked = jnp.concatenate([high, middle, lowest], axis=0).astype(jnp.bfloat16)
                    row = (group * ROWS + s) * columns + x
                    wanted = place_ref[pl.ds(row, 1), :]
                    hot = jnp.where(lax.broadcasted_iota(jnp.int32, (width, width), 0) == wanted, 1.0, 0.0)
                    moved = lax.dot_general(
                        stacked, hot.astype(jnp.bfloat16), (((1,), (1,)), ((), ())), preferred_element_type=jnp.float32
                    )
                    moved = moved[0:8] + moved[8:16] + moved[16:24]
                    buffer = (s * columns + x) % 4
                    for c in range(chunks):
                        local[buffer, c + 1] = moved[:, c * LANES : (c + 1) * LANES]
                    for d in range(parts):
                        base = meta_ref[row, target[d]]
                        begin = meta_ref[row, parts + target[d]]
                        chunk = lax.shift_right_logical(base, 7)
                        off = lax.bitwise_and(base, LANES - 1)
                        turn = lax.bitwise_and(off - begin, LANES - 1)
                        at = lax.shift_right_logical(begin, 7)
                        at = at + jnp.where(off < lax.bitwise_and(begin, LANES - 1), 1, 0)
                        turned = [pltpu.roll(local[buffer, at + k], turn, 1) for k in range(chunks + 2)]
                        for k in range(chunks + 1):
                            value = jnp.where(lane >= turn, turned[k + 1], turned[k])
                            if k == 0:
                                value = jnp.where(lane >= off, value, lists[d, chunk])
                            lists[d, chunk + k] = value
            return carry

        lax.fori_loop(0, slots // ROWS, do_group, 0)
        for d in range(parts):
            count = meta_ref[slots * columns - 1, 2 * parts + target[d]]
            for c in range(total):
                out_refs[d][:, c * LANES : (c + 1) * LANES] = jnp.where(lane + c * LANES < count, lists[d, c], 0.0)

    return pl.pallas_call(
        kernel,
        out_shape=(jax.ShapeDtypeStruct((8, capacity), jnp.float32),) * parts,
        in_specs=[VMEM, VMEM, VMEM, SMEM, SMEM],
        out_specs=(VMEM,) * parts,
        scratch_shapes=[
            pltpu.VMEM((4, 2 * chunks + 4, ROWS, LANES), jnp.float32),
            pltpu.VMEM((parts, total + chunks + 2, ROWS, LANES), jnp.float32),
        ],
        compiler_params=PARAMS,
    )(motion, pressure, place, meta, here)


def in_order(here, received):
    parts = len(received)
    rows, capacity = received[0].shape

    def kernel(here_ref, *refs):
        out_ref = refs[parts]
        for k in range(parts):

            @pl.when(pl.program_id(0) == k)
            def _():
                out_ref[...] = refs[k][...]

    return pl.pallas_call(
        kernel,
        out_shape=jax.ShapeDtypeStruct((rows, parts * capacity), jnp.float32),
        grid_spec=pltpu.PrefetchScalarGridSpec(
            num_scalar_prefetch=1,
            grid=(parts,),
            in_specs=[VMEM] * parts,
            out_specs=pl.BlockSpec((rows, capacity), lambda k, here_ref: (0, lax.rem(here_ref[0] - k + parts, parts))),
        ),
        compiler_params=PARAMS,
    )(here, *received)


def pass_on(value, axis, step):
    count = lax.axis_size(axis)
    return lax.ppermute(value, axis, [(i, (i + step) % count) for i in range(count)])


def swap_ends(left_ends, right_ends):
    return pass_on(right_ends, "sub", 1), pass_on(left_ends, "sub", -1)


def swap_columns(parts_of):
    first = jnp.concatenate(parts_of(0), axis=0)
    final = jnp.concatenate(parts_of(-1), axis=0)
    return pass_on(final, "tile", 1), pass_on(first, "tile", -1)


def rows_of(fields):
    return fields.reshape(-1, fields.shape[-1])


def beside(ends, width):
    plane = jnp.concatenate(ends, axis=1)
    return jnp.pad(plane, ((0, 0), (0, width - plane.shape[1])))


def shards(offsets, velocity, mass, entropy, active_counts, targets):
    slots, columns, width = mass.shape
    levels = active_counts.shape[0]
    parts = lax.axis_size("sub")
    slot_index = lax.broadcasted_iota(jnp.int32, mass.shape, 0)
    mass_live = jnp.where(slot_index < active_counts[0][None], mass, 0.0)
    motion = jnp.concatenate([offsets, velocity, mass_live[None]], axis=0).transpose(2, 0, 1, 3)
    entropy = entropy.transpose(1, 0, 2)
    limits = (slots, slots // 2, slots // 4)
    pressure = None
    ends_m, ends_p, sizes_m, sizes_p = [], [], [], []
    left_m, right_m, left_p, right_p = [], [], [], []
    made = first_ends(motion)
    place, meta = ranks(targets.reshape(slots * columns, width), parts)
    for level in range(levels):
        limit = limits[level]
        sent = limits[max(level - 1, 0)]
        ends_m.insert(0, swap_ends(*made))
        partial, *inner_kept = own_part(DENSITY, motion, None, ends_m, [], limit, (0,), keep=KEEP[level][0])
        ends_m[0], partial = lax.optimization_barrier((ends_m[0], partial))
        plane = beside(ends_m[0], width)
        masses = (lambda c: [motion[c, 6]]) if level == 0 else (lambda c: [])
        cells = swap_columns(lambda c: [rows_of(motion[c, :3, :sent]), *masses(c), plane])
        sizes_m.insert(0, sent)
        left_m.insert(0, cells[0])
        right_m.insert(0, cells[1])
        partial, *outer_kept = own_part(DENSITY, motion, None, ends_m, [], limit, (-1, 1), partial, keep=KEEP[level][1])
        pressure, *made = density_rest(motion, partial, (left_m, right_m), sizes_m, pressure, entropy, active_counts, level, limit, limit, KEEP[level][2])
        rest_kept = made.pop() if KEEP[level][2] else None
        ends_p.insert(0, swap_ends(*made))
        (partial,) = own_part(FORCE, motion, pressure, ends_m, ends_p, limit, (0,), None, *inner_kept)
        ends_p[0], partial = lax.optimization_barrier((ends_p[0], partial))
        plane = beside(ends_p[0], width)
        cells = swap_columns(lambda c: [rows_of(pressure[c, :, :limit]), plane, rows_of(motion[c, 3:6, :sent])])
        sizes_p.insert(0, limit)
        left_p.insert(0, cells[0])
        right_p.insert(0, cells[1])
        (partial,) = own_part(FORCE, motion, pressure, ends_m, ends_p, limit, (-1, 1), partial, *outer_kept)
        more = limit if level < levels - 1 else 0
        motion, *made = force_rest(
            motion, pressure, partial, (left_m, right_m), (left_p, right_p), sizes_m, sizes_p, active_counts, level, limit, more, rest_kept
        )
    capacity = 3 * slots * columns * width // 8
    here = lax.axis_index("sub").astype(jnp.int32).reshape(1)
    lists = compact(motion, pressure, place, meta[:, : 3 * parts], here, parts, capacity)
    received = {0: lists[0]}
    for k in sorted(range(1, parts), key=lambda k: -min(k, parts - k)):
        received[k] = pass_on(lists[k], "sub", k)
    return in_order(here, [received[k] for k in range(parts)])


def solution(mesh):
    placed = (
        P(None, None, "tile", "sub"),
        P(None, None, "tile", "sub"),
        P(None, "tile", "sub"),
        P(None, "tile", "sub"),
        P(None, "tile", "sub"),
        P(None, "tile", "sub"),
    )
    return jax.shard_map(
        shards, mesh=mesh, in_specs=placed, out_specs=P(None, ("tile", "sub")), check_vma=False
    )
```

```python
import functools
import math

import jax
import jax.numpy as jnp
from jax import lax
from jax.experimental import pallas as pl
from jax.experimental.pallas import tpu as pltpu
from jax.sharding import PartitionSpec as P

KERNEL_NORM = 21.0 / (2.0 * math.pi)
GAMMA = 5.0 / 3.0
TIME_STEP = 0.05
SOFTEN = 0.01
LANES = 128
ROWS = 8
VMEM = pl.BlockSpec(memory_space=pltpu.VMEM)
SMEM = pl.BlockSpec(memory_space=pltpu.SMEM)
PARAMS = pltpu.CompilerParams(vmem_limit_bytes=24 << 20)
MOTION, PRESSURE = 7, 3
SHIFTS = (-1, 0, 1)
KEEP = ((True, True, True), (True, True, True), (False, False, False))


def lane_of(shape):
    return lax.broadcasted_iota(jnp.int32, shape, 1)


def cost(pairs, ops):
    return pl.CostEstimate(flops=int(pairs * ops * 15), bytes_accessed=1 << 20, transcendentals=0)


def closeness(delta):
    dx, dy, dz = delta
    squared = dx * dx + dy * dy + dz * dz
    radius = squared * lax.rsqrt(jnp.maximum(squared, 1e-30))
    return jnp.maximum(1.0 - radius, 0.0), squared


def displacement(own, their):
    return tuple(i - j for i, j in zip(own[:3], their[:3]))


def force_core(own, their, near):
    remain, squared = near
    if squared is None:
        squared = (1.0 - remain) * (1.0 - remain)
    ui, vi, wi, qi, ci, ri = own[3:9]
    uj, vj, wj, qj, cj, rj = their[3:9]
    dx, dy, dz = displacement(own, their)
    approach = dx * (ui - uj) + dy * (vi - vj) + dz * (wi - wj)
    closing = jnp.minimum(approach, 0.0) * pl.reciprocal(squared + SOFTEN, approx=True)
    viscous = closing * (closing - (ci + cj)) * pl.reciprocal(ri + rj, approx=True)
    return (dx, dy, dz), qi + qj + viscous


def pair_force(own, their, total, near):
    remain = near[0]
    delta, pressure = force_core(own, their, near)
    strength = pressure * ((remain * remain) * (remain * their[-1]))
    return tuple(t + strength * d for t, d in zip(total, delta))


def pair_density(own, their, total, near):
    remain = near[0]
    square = remain * remain
    return (total[0] + (square * square) * ((5.0 - 4.0 * remain) * their[-1]),)


def both_force(own, their, total, near):
    remain = near[0]
    delta, pressure = force_core(own, their, near)
    strength = pressure * ((remain * remain) * remain)
    on_own, on_their = strength * their[-1], strength * own[-1]
    return tuple(t + on_own * d for t, d in zip(total, delta)), tuple(on_their * d for d in delta)


def both_density(own, their, total, near):
    remain = near[0]
    square = remain * remain
    weight = (square * square) * (5.0 - 4.0 * remain)
    return (total[0] + weight * their[-1],), (weight * own[-1],)


def kept(kept_ref, at, own, their, first):
    if kept_ref is not None and not first:
        return kept_ref[at], None
    near = closeness(displacement(own, their))
    if kept_ref is not None:
        kept_ref[at] = near[0]
    return near


DENSITY = ((0, 1.0), (1, 1.0), (2, 1.0)), (), ((6, KERNEL_NORM),), pair_density, 1
FORCE = (
    tuple((c, 1.0) for c in range(3)) + tuple((c, 4.0) for c in range(3, 6)),
    ((0, 1.0), (1, 1.0), (2, 4.0)),
    ((6, 20.0 * KERNEL_NORM),),
    pair_force,
    3,
)


def fill_shifted(shifted, col, row, pieces, scale, group, shifts, is_y):
    for cells, left, right, lo, hi in pieces:
        count = cells.shape[-1] // LANES
        blocks = [cells[lo:hi, b * LANES : (b + 1) * LANES] for b in range(count)]
        if scale != 1.0:
            blocks = [v * scale for v in blocks]
        lane = lane_of(blocks[0].shape)
        for at, shift in enumerate(shifts):
            values = blocks
            if shift == -1:
                turned = [pltpu.roll(v, 1, 1) for v in blocks]
                end = pltpu.roll(left[lo:hi, :], (LANES - group) % LANES, 1) if group else left[lo:hi, :]
                turned = [end if scale == 1.0 else end * scale] + turned
                values = [jnp.where(lane == 0, turned[b], turned[b + 1]) for b in range(count)]
            elif shift == 1:
                turned = [pltpu.roll(v, LANES - 1, 1) for v in blocks]
                end = pltpu.roll(right[lo:hi, :], LANES - 1 - group, 1)
                turned.append(end if scale == 1.0 else end * scale)
                values = [jnp.where(lane == LANES - 1, turned[b + 1], turned[b]) for b in range(count)]
            if is_y and shift:
                values = [v + float(shift) for v in values]
            for b in range(count):
                shifted[col, at, b, row, lo:hi, :] = values[b]


def fill_column(shifted, col, kind, motion, pressure, group_of, shifts):
    moved, pressed, massed, _, _ = kind
    row = 0
    for pieces, fields in ((motion, moved), (pressure, pressed), (motion, massed)):
        for field, scale in fields:
            is_y = fields is moved and field == 1
            fill_shifted(shifted, col, row, pieces(field), scale, group_of(field), shifts, is_y)
            row += 1


def add_pairs(kind, motion_ref, pressure_ref, shifted, x, sources, limit, first, last, kept_ref, unit, start=0):
    moved, pressed, _, pair, width = kind
    slots = shifted.shape[-2]
    blocks = shifted.shape[2]
    rows = shifted.shape[3]
    group = min(limit // ROWS, 2 if width == 3 else 4)
    unroll = min(slots - start, 32 // group)
    forms = shifted.shape[1]
    low_col, low_shift = sources[0]

    def lane_block(b, carry):
        lanes = pl.ds(pl.multiple_of(b * LANES, LANES), LANES)
        for part in range(limit // (ROWS * group)):
            spans = [slice((part * group + v) * ROWS, (part * group + v + 1) * ROWS) for v in range(group)]
            own = []
            for span in spans:
                values = [motion_ref[x, f, span, lanes] * s if s != 1.0 else motion_ref[x, f, span, lanes] for f, s in moved]
                values += [pressure_ref[x, f, span, lanes] * s if s != 1.0 else pressure_ref[x, f, span, lanes] for f, s in pressed]
                own.append(values)

            def source(at, totals):
                col = at // forms
                shift = at - forms * col
                offset = (col + low_shift).astype(jnp.float32)
                mine = [[v[0] - offset] + v[1:] for v in own]

                def step(outer, totals):
                    totals = list(totals)
                    for inner in range(unroll):
                        slot = outer * unroll + inner
                        their = [
                            jnp.broadcast_to(shifted[col + low_col, shift, b, r, pl.ds(slot, 1), :], (ROWS, LANES))
                            for r in range(rows)
                        ]
                        for v in range(group):
                            place = (unit + at, b, slot * (limit // ROWS) + part * group + v)
                            remain = kept(kept_ref, place, mine[v], their, width == 1)
                            totals[v] = pair(mine[v], their, totals[v], remain)
                    return tuple(totals)

                return lax.fori_loop(start // unroll, slots // unroll, step, totals)

            totals = tuple(first(x, span, lanes) for span in spans)
            totals = lax.fori_loop(0, forms * len(sources), source, totals)
            for span, total in zip(spans, totals):
                last(x, span, lanes, total)
        return carry

    lax.fori_loop(0, blocks, lane_block, 0)


def own_sources(x, columns):
    return [(c, c - x) for c in range(columns) if abs(c - x) <= 1]


def pack_ends(field_of, fields, columns, left_ref, right_ref):
    for ref, at_last in ((left_ref, False), (right_ref, True)):
        lane = None
        packed = None
        for group in range(fields * columns):
            block = field_of(group // columns, group % columns, at_last)
            if lane is None:
                lane = lane_of(block.shape)
                packed = jnp.zeros(block.shape, jnp.float32)
            turn = (group + 1) % LANES if at_last else group
            packed = jnp.where(lane == group, pltpu.roll(block, turn, 1) if turn else block, packed)
        ref[...] = packed


def end_block(ref, column, field, at_last, limit):
    width = ref.shape[-1]
    lanes = slice(width - LANES, width) if at_last else slice(0, LANES)
    return ref[column, field, :limit, lanes]


def first_ends(motion):
    columns, _, slots, _ = motion.shape

    def kernel(motion_ref, left_ref, right_ref):
        pack_ends(
            lambda f, c, last: end_block(motion_ref, c, f, last, slots), MOTION, columns, left_ref, right_ref
        )

    ends = jax.ShapeDtypeStruct((slots, LANES), jnp.float32)
    return pl.pallas_call(kernel, out_shape=(ends, ends), in_specs=[VMEM], out_specs=(VMEM, VMEM), compiler_params=PARAMS)(motion)


def bounds_of(sizes):
    spans, lo = [], 0
    for index, hi in enumerate(sizes):
        if hi > lo:
            spans.append((index, lo, hi))
            lo = hi
    return spans


def own_part(kind, motion, pressure, ends_m, ends_p, limit, shifts, partial=None, closeness_kept=None, keep=False):
    columns, _, slots, width = motion.shape
    moved, pressed, massed, _, outs = kind
    inner = shifts == (0,)
    mutual = 2 * limit >= slots
    if inner:
        ends_m = ends_p = []
    flat_m = [e for pair in ends_m for e in pair]
    flat_p = [e for pair in ends_p for e in pair]
    whole = [(0, 0, slots)]
    spans_m = whole if inner else bounds_of([e[0].shape[0] for e in ends_m])
    spans_p = whole if inner else bounds_of([e[0].shape[0] for e in ends_p])
    inputs = [motion] + ([pressure] if pressed else []) + flat_m + flat_p + ([] if partial is None else [partial])
    n_in = len(inputs)
    calls = []
    for x in range(columns):
        for col, _ in own_sources(x, columns):
            start = limit if mutual and not (inner and col == x) else 0
            if start < slots:
                calls.append((x, col, start, None))
    if mutual:
        for x in range(columns):
            for col in (x, x + 1):
                for form, shift in enumerate(shifts):
                    if col < columns and (col != x or shift == 1):
                        calls.append((x, col, 0, form))
    units = sum(len(shifts) if form is None else 1 for *_, form in calls)
    kept_shape = jax.ShapeDtypeStruct((units, width // LANES, slots * limit // ROWS, ROWS, LANES), jnp.float32)
    keep = keep and not pressed
    if closeness_kept is not None:
        inputs.append(closeness_kept)
    rows = len(moved) + len(pressed) + len(massed)

    def kernel(*own_refs):
        refs = list(own_refs)
        motion_ref = refs.pop(0)
        pressure_ref = refs.pop(0) if pressed else None
        m_refs = refs[: len(flat_m)]
        p_refs = refs[len(flat_m) : len(flat_m) + len(flat_p)]
        partial_ref = None if partial is None else own_refs[n_in - 1]
        left = list(own_refs[n_in:])
        kept_ref = None if closeness_kept is None else left.pop(0)
        out_ref = left.pop(0)
        if keep:
            kept_ref = left.pop(0)
        shifted, *mutual_refs = left

        def pieces(cells, ends, spans):
            if inner:
                return [(cells, None, None, 0, slots)]
            return [(cells, ends[2 * i], ends[2 * i + 1], lo, hi) for i, lo, hi in spans]

        for c in range(columns):

            def motion_pieces(field):
                return pieces(motion_ref.at[c, field], m_refs, spans_m if field < 6 else [(len(ends_m) - 1, 0, slots)])

            def pressure_pieces(field):
                return pieces(pressure_ref.at[c, field], p_refs, spans_p)

            fill_column(shifted, c, kind, motion_pieces, pressure_pieces, lambda f: f * columns + c, shifts)

        def first(x, span, lanes):
            return tuple(out_ref[x, k, span, lanes] for k in range(outs))

        def last(x, span, lanes, total):
            for k in range(outs):
                out_ref[x, k, span, lanes] = total[k]

        out_ref[...] = jnp.zeros(out_ref.shape, jnp.float32) if partial is None else partial_ref[...]
        edges, unit = [], 0
        for x, col, start, form in calls:
            if form is None:
                add_pairs(
                    kind, motion_ref, pressure_ref, shifted, x, [(col, col - x)], limit, first, last, kept_ref, unit, start
                )
                unit += len(shifts)
                continue
            parts, reaction, packed = mutual_refs
            both_ways(
                kind, motion_ref, pressure_ref, shifted, x, col, form, out_ref, parts, reaction, limit, kept_ref, unit
            )
            take_reaction(out_ref, reaction, col, shifts[form], outs)
            unit += 1
            if shifts[form]:
                edges.append((col, x, -shifts[form]))
        if edges:
            edge_pairs(kind, motion_ref, pressure_ref, shifted, shifts, edges, out_ref, packed, limit)

    sums_shape = jax.ShapeDtypeStruct((columns, outs, limit, width), jnp.float32)
    return pl.pallas_call(
        kernel,
        out_shape=(sums_shape, kept_shape) if keep else (sums_shape,),
        in_specs=[VMEM] * len(inputs),
        out_specs=(VMEM, VMEM) if keep else (VMEM,),
        scratch_shapes=[pltpu.VMEM((columns, len(shifts), width // LANES, rows, slots, LANES), jnp.float32)]
        + (
            [
                pltpu.VMEM((outs, limit, ROWS, LANES), jnp.float32),
                pltpu.VMEM((outs, width // LANES, limit, LANES), jnp.float32),
                pltpu.VMEM((rows, limit, LANES), jnp.float32),
            ]
            if mutual
            else []
        ),
        compiler_params=PARAMS,
        cost_estimate=cost(limit * slots * len(shifts) * (3 * columns - 2) * width, 60 if outs == 3 else 30),
    )(*inputs)


def sum_rows(values):
    row = lax.broadcasted_iota(jnp.int32, (ROWS, LANES), 0)
    step = 1
    while len(values) > 1:
        low = lax.bitwise_and(row, step) == 0
        values = [
            jnp.where(low, a, b) + pltpu.roll(jnp.where(low, b, a), step, 0) for a, b in zip(values[::2], values[1::2])
        ]
        step *= 2
    return values[0]


def own_rows(kind, motion_ref, pressure_ref, x, span, lanes):
    moved, pressed, massed = kind[:3]
    rows = [(motion_ref, f, s) for f, s in moved] + [(pressure_ref, f, s) for f, s in pressed] + [(motion_ref, f, s) for f, s in massed]
    return [ref[x, f, span, lanes] * s if s != 1.0 else ref[x, f, span, lanes] for ref, f, s in rows]


def both_ways(kind, motion_ref, pressure_ref, shifted, x, col, form, sums, parts, reaction, limit, kept_ref, unit):
    outs = kind[4]
    blocks, rows = shifted.shape[2], shifted.shape[3]
    both = both_force if outs == 3 else both_density
    sign = -1.0 if outs == 3 else 1.0
    group = min(limit // ROWS, 2 if outs == 3 else 4)
    unroll = 16

    def lane_block(b, carry):
        lanes = pl.ds(pl.multiple_of(b * LANES, LANES), LANES)
        for part in range(limit // (ROWS * group)):
            spans = [slice((part * group + v) * ROWS, (part * group + v + 1) * ROWS) for v in range(group)]
            mine = []
            for span in spans:
                values = own_rows(kind, motion_ref, pressure_ref, x, span, lanes)
                mine.append([values[0] - float(col - x)] + values[1:])

            def step(outer, totals):
                totals = list(totals)
                for inner in range(unroll):
                    slot = outer * unroll + inner
                    their = [jnp.broadcast_to(shifted[col, form, b, r, pl.ds(slot, 1), :], (ROWS, LANES)) for r in range(rows)]
                    back = None
                    for v in range(group):
                        place = (unit, b, slot * (limit // ROWS) + part * group + v)
                        remain = kept(kept_ref, place, mine[v], their, outs == 1)
                        totals[v], given = both(mine[v], their, totals[v], remain)
                        back = given if back is None else tuple(p + q for p, q in zip(back, given))
                    for k in range(outs):
                        parts[k, slot] = back[k] if part == 0 else parts[k, slot] + back[k]
                return tuple(totals)

            totals = tuple(tuple(sums[x, k, span, lanes] for k in range(outs)) for span in spans)
            totals = lax.fori_loop(0, limit // unroll, step, totals)
            for span, total in zip(spans, totals):
                for k in range(outs):
                    sums[x, k, span, lanes] = total[k]
        for k in range(outs):
            for lo in range(0, limit, ROWS):
                reaction[k, b, lo : lo + ROWS, :] = sign * sum_rows([parts[k, lo + r] for r in range(ROWS)])
        return carry

    lax.fori_loop(0, blocks, lane_block, 0)


def take_reaction(sums, reaction, col, shift, outs):
    blocks, slots = reaction.shape[1], reaction.shape[2]
    lane = lane_of((slots, LANES))
    for k in range(outs):
        values = [reaction[k, b] for b in range(blocks)]
        if shift == 1:
            turned = [jnp.zeros((slots, LANES), jnp.float32)] + [pltpu.roll(v, 1, 1) for v in values]
            values = [jnp.where(lane == 0, turned[b], turned[b + 1]) for b in range(blocks)]
        elif shift == -1:
            turned = [pltpu.roll(v, LANES - 1, 1) for v in values] + [jnp.zeros((slots, LANES), jnp.float32)]
            values = [jnp.where(lane == LANES - 1, turned[b + 1], turned[b]) for b in range(blocks)]
        for b in range(blocks):
            lanes = slice(b * LANES, (b + 1) * LANES)
            sums[col, k, :, lanes] = sums[col, k, :, lanes] + values[b]


def edge_pairs(kind, motion_ref, pressure_ref, shifted, forms, edges, sums, packed, limit):
    pair, outs = kind[3], kind[4]
    blocks, rows = shifted.shape[2], shifted.shape[3]
    lane = lane_of((ROWS, LANES))
    width = blocks * LANES
    tall = lane_of((limit, LANES))
    for r in range(rows):
        value = jnp.zeros((limit, LANES), jnp.float32)
        for q, (x, col, shift) in enumerate(edges):
            block, turn = (0, q) if shift == -1 else (blocks - 1, q + 1)
            value = jnp.where(tall == q, pltpu.roll(shifted[col, forms.index(shift), block, r, :limit, :], turn, 1), value)
        packed[r] = value
    spans = [slice(lo, lo + ROWS) for lo in range(0, limit, ROWS)]
    group = min(limit // ROWS, 2 if outs == 3 else 4)
    unroll = 8
    for part in range(len(spans) // group):
        mine = []
        for span in spans[part * group : (part + 1) * group]:
            values = None
            for q, (x, col, shift) in enumerate(edges):
                lanes, turn = (slice(0, LANES), q) if shift == -1 else (slice(width - LANES, width), q + 1)
                cell = own_rows(kind, motion_ref, pressure_ref, x, span, lanes)
                cell = [pltpu.roll(v, turn, 1) if turn else v for v in cell]
                cell[0] = cell[0] - float(col - x)
                values = cell if values is None else [jnp.where(lane == q, c, v) for c, v in zip(cell, values)]
            mine.append(values)

        def step(outer, totals):
            totals = list(totals)
            for inner in range(unroll):
                slot = outer * unroll + inner
                their = [jnp.broadcast_to(packed[r, pl.ds(slot, 1), :], (ROWS, LANES)) for r in range(rows)]
                for v in range(group):
                    totals[v] = pair(mine[v], their, totals[v], closeness(displacement(mine[v], their)))
            return tuple(totals)

        zero = jnp.zeros((ROWS, LANES), jnp.float32)
        totals = lax.fori_loop(0, limit // unroll, step, tuple((zero,) * outs for _ in range(group)))
        for v, span in enumerate(spans[part * group : (part + 1) * group]):
            for k in range(outs):
                for q, (x, col, shift) in enumerate(edges):
                    at = 0 if shift == -1 else LANES - 1
                    lanes = slice(0, LANES) if shift == -1 else slice(width - LANES, width)
                    back = pltpu.roll(totals[v][k], (at - q) % LANES, 1) if at != q else totals[v][k]
                    sums[x, k, span, lanes] = sums[x, k, span, lanes] + jnp.where(lane == at, back, 0.0)


def halo_sums(kind, refs, columns, slots, limit, first, last, motion_ref, pressure_ref, shifted, sizes_m, sizes_p, kept_ref):
    spans_m, spans_p = bounds_of(sizes_m), bounds_of(sizes_p)
    for side in range(2):
        m_refs, p_refs = refs[side]
        column = columns - 1 if side == 0 else 0

        def field_of(ref, at, size):
            return ref.at[at : at + size]

        def piece(cells, ends, lo, hi):
            return (cells, ends.at[:, 0:LANES], ends.at[:, LANES : 2 * LANES], lo, hi)

        def motion_pieces(field):
            out = []
            for i, lo, hi in spans_m if field < 6 else [(len(sizes_m) - 1, 0, slots)]:
                size = sizes_m[i]
                ends = field_of(m_refs[i], (4 if i == len(sizes_m) - 1 else 3) * size, size)
                if field < 3 or field == 6:
                    cells = field_of(m_refs[i], min(field, 3) * size, size)
                else:
                    cells = field_of(p_refs[i], 4 * sizes_p[i] + (field - 3) * size, size)
                out.append(piece(cells, ends, lo, hi))
            return out

        def pressure_pieces(field):
            return [
                piece(field_of(p_refs[i], field * sizes_p[i], sizes_p[i]), field_of(p_refs[i], 3 * sizes_p[i], sizes_p[i]), lo, hi)
                for i, lo, hi in spans_p
            ]

        fill_column(shifted, side, kind, motion_pieces, pressure_pieces, lambda f: f * columns + column, SHIFTS)
        x, shift = (0, -1) if side == 0 else (columns - 1, 1)
        add_pairs(
            kind, motion_ref, pressure_ref, shifted, x, [(side, shift)], limit, first, last, kept_ref, side * len(SHIFTS)
        )


def density_rest(motion, partial, messages, sizes, density, entropy, counts, level, limit, slots_sent, keep):
    columns, _, slots, width = motion.shape
    (m_left, m_right) = messages
    first = density is None
    inputs = [motion, partial, entropy, counts] + ([] if first else [density]) + m_left + m_right
    n_in, n_m = len(inputs), len(m_left)
    rows = 4
    kept_shape = jax.ShapeDtypeStruct((2 * len(SHIFTS), width // LANES, slots * limit // ROWS, ROWS, LANES), jnp.float32)

    def kernel(*refs):
        motion_ref, partial_ref, entropy_ref, counts_ref = refs[:4]
        old_ref = None if first else refs[4]
        m_refs = refs[n_in - 2 * n_m : n_in]
        press_ref, left_ref, right_ref, *left = refs[n_in:]
        kept_ref = left[0] if keep else None
        shifted, sums = left[-2:]
        sums[...] = partial_ref[...]

        def start(x, span, lanes):
            return (sums[x, 0, span, lanes],)

        def end(x, span, lanes, total):
            sums[x, 0, span, lanes] = total[0]

        sides = ((m_refs[:n_m], []), (m_refs[n_m:], []))
        halo_sums(DENSITY, sides, columns, slots, limit, start, end, motion_ref, None, shifted, sizes, [], kept_ref)
        for x in range(columns):
            count = counts_ref[level, x : x + 1, :]
            for lo in range(0, slots, ROWS):
                span = slice(lo, lo + ROWS)
                if lo >= limit:
                    if first:
                        value = jnp.ones((ROWS, width), jnp.float32)
                    else:
                        for f in range(3):
                            press_ref[x, f, span, :] = old_ref[x, f, span, :]
                        continue
                else:
                    slot = lax.broadcasted_iota(jnp.int32, (ROWS, width), 0) + lo
                    before = jnp.ones((ROWS, width), jnp.float32) if first else old_ref[x, 2, span, :]
                    value = jnp.where(slot < count, sums[x, 0, span, :], before)
                pressure = entropy_ref[x, span, :] * jnp.exp(jnp.log(value) * (GAMMA - 2.0))
                press_ref[x, 0, span, :] = pressure
                press_ref[x, 1, span, :] = jnp.sqrt(GAMMA * pressure * value)
                press_ref[x, 2, span, :] = value
        pack_ends(lambda f, c, last: end_block(press_ref, c, f, last, slots_sent), PRESSURE, columns, left_ref, right_ref)

    ends = jax.ShapeDtypeStruct((slots_sent, LANES), jnp.float32)
    return pl.pallas_call(
        kernel,
        out_shape=(
            jax.ShapeDtypeStruct((columns, PRESSURE, slots, width), jnp.float32),
            ends,
            ends,
        )
        + ((kept_shape,) if keep else ()),
        in_specs=[VMEM] * n_in,
        out_specs=(VMEM,) * (4 if keep else 3),
        scratch_shapes=[
            pltpu.VMEM((2, 3, width // LANES, rows, slots, LANES), jnp.float32),
            pltpu.VMEM((columns, 1, limit, width), jnp.float32),
        ],
        compiler_params=PARAMS,
        cost_estimate=cost(limit * slots * 6 * width, 30),
    )(*inputs)


def force_rest(motion, pressure, partial, messages_m, messages_p, sizes_m, sizes_p, counts, level, limit, slots_sent, closeness_kept):
    columns, _, slots, width = motion.shape
    n_m, n_p = len(messages_m[0]), len(messages_p[0])
    inputs = [motion, pressure, partial, counts] + messages_m[0] + messages_p[0] + messages_m[1] + messages_p[1]
    inputs += [] if closeness_kept is None else [closeness_kept]
    n_in = len(inputs)
    rows = 10
    ends = jax.ShapeDtypeStruct((slots_sent, LANES), jnp.float32)
    outs = (jax.ShapeDtypeStruct(motion.shape, jnp.float32),) + ((ends, ends) if slots_sent else ())

    def kernel(*refs):
        motion_ref, pressure_ref, partial_ref, counts_ref = refs[:4]
        sides = []
        for side in range(2):
            at = 4 + side * (n_m + n_p)
            sides.append((refs[at : at + n_m], refs[at + n_m : at + n_m + n_p]))
        new_ref = refs[n_in]
        shifted, sums = refs[-2:]
        sums[...] = partial_ref[...]

        def start(x, span, lanes):
            return tuple(sums[x, k, span, lanes] for k in range(3))

        def end(x, span, lanes, total):
            for k in range(3):
                sums[x, k, span, lanes] = total[k]

        halo_sums(
            FORCE, sides, columns, slots, limit, start, end, motion_ref, pressure_ref, shifted, sizes_m, sizes_p,
            None if closeness_kept is None else refs[n_in - 1],
        )
        for x in range(columns):
            count = counts_ref[level, x : x + 1, :]
            new_ref[x, 6, :, :] = motion_ref[x, 6, :, :]
            if limit < slots:
                for f in range(6):
                    new_ref[x, f, limit:, :] = motion_ref[x, f, limit:, :]
            for lo in range(0, limit, ROWS):
                span = slice(lo, lo + ROWS)
                active = lax.broadcasted_iota(jnp.int32, (ROWS, width), 0) + lo < count
                for k in range(3):
                    place, speed = motion_ref[x, k, span, :], motion_ref[x, 3 + k, span, :]
                    faster = speed + TIME_STEP * sums[x, k, span, :]
                    new_ref[x, 3 + k, span, :] = jnp.where(active, faster, speed)
                    new_ref[x, k, span, :] = jnp.where(active, place + TIME_STEP * faster, place)
        if slots_sent:
            left_ref, right_ref = refs[n_in + 1 : n_in + 3]
            pack_ends(lambda f, c, last: end_block(new_ref, c, f, last, slots_sent), 6, columns, left_ref, right_ref)

    made = pl.pallas_call(
        kernel,
        out_shape=outs,
        in_specs=[VMEM] * n_in,
        out_specs=(VMEM,) * len(outs),
        scratch_shapes=[
            pltpu.VMEM((2, 3, width // LANES, rows, slots, LANES), jnp.float32),
            pltpu.VMEM((columns, 3, limit, width), jnp.float32),
        ],
        compiler_params=PARAMS,
        cost_estimate=cost(limit * slots * 6 * width, 60),
    )(*inputs)
    return made if slots_sent else (made[0], None, None)


def ranks(destination, parts):
    rows, width = destination.shape

    def kernel(dest_ref, place_ref, meta_ref):
        dest = dest_ref[...]
        low = lax.broadcasted_iota(jnp.int32, (width, width), 0)
        upto = jnp.where(low <= lane_of((width, width)), 1.0, 0.0).astype(jnp.bfloat16)
        above = lax.broadcasted_iota(jnp.int32, (rows, rows), 0) > lane_of((rows, rows))
        above = jnp.where(above, 1.0, 0.0).astype(jnp.bfloat16)
        lane = lane_of((rows, LANES))
        meta = jnp.zeros((rows, LANES), jnp.float32)
        place = jnp.zeros((rows, width), jnp.float32)
        start = jnp.zeros((rows, 1), jnp.float32)
        for d in range(parts):
            mask = jnp.where(dest == d, 1.0, 0.0)
            inside = jnp.dot(mask.astype(jnp.bfloat16), upto, preferred_element_type=jnp.float32)
            count = inside[:, width - 1 : width]
            wide = jnp.broadcast_to(count, (rows, LANES))
            before = jnp.dot(above, wide.astype(jnp.bfloat16), preferred_element_type=jnp.float32)
            place = place + mask * (inside - 1.0 + start)
            meta = jnp.where(lane == d, before, meta)
            meta = jnp.where(lane == parts + d, jnp.broadcast_to(start, (rows, LANES)), meta)
            meta = jnp.where(lane == 2 * parts + d, before + wide, meta)
            start = start + count
        place_ref[...] = place.astype(jnp.int32)
        meta_ref[...] = meta.astype(jnp.int32)

    return pl.pallas_call(
        kernel,
        out_shape=(jax.ShapeDtypeStruct((rows, width), jnp.int32), jax.ShapeDtypeStruct((rows, LANES), jnp.int32)),
        in_specs=[VMEM],
        out_specs=(VMEM, VMEM),
        compiler_params=PARAMS,
    )(destination)


def compact(motion, pressure, place, meta, here, parts, capacity):
    columns, _, slots, width = motion.shape
    chunks = width // LANES
    total = -(-capacity // LANES)

    def kernel(motion_ref, pressure_ref, place_ref, meta_ref, here_ref, *refs):
        out_refs, (local, lists) = refs[:parts], refs[parts:]
        target = [lax.rem(here_ref[0] + k, parts) for k in range(parts)]
        lane = lane_of((ROWS, LANES))

        def do_group(group, carry):
            span = pl.ds(pl.multiple_of(group * ROWS, ROWS), ROWS)
            fields = [
                [motion_ref[x, f, span, :] for f in range(6)] + [pressure_ref[x, 2, span, :], motion_ref[x, 6, span, :]]
                for x in range(columns)
            ]
            for s in range(ROWS):
                for x in range(columns):
                    state = jnp.concatenate([v[s : s + 1, :] for v in fields[x]], axis=0)
                    high = state.astype(jnp.bfloat16).astype(jnp.float32)
                    rest = state - high
                    middle = rest.astype(jnp.bfloat16).astype(jnp.float32)
                    lowest = rest - middle
                    stacked = jnp.concatenate([high, middle, lowest], axis=0).astype(jnp.bfloat16)
                    row = (group * ROWS + s) * columns + x
                    wanted = place_ref[pl.ds(row, 1), :]
                    hot = jnp.where(lax.broadcasted_iota(jnp.int32, (width, width), 0) == wanted, 1.0, 0.0)
                    moved = lax.dot_general(
                        stacked, hot.astype(jnp.bfloat16), (((1,), (1,)), ((), ())), preferred_element_type=jnp.float32
                    )
                    moved = moved[0:8] + moved[8:16] + moved[16:24]
                    buffer = (s * columns + x) % 4
                    for c in range(chunks):
                        local[buffer, c + 1] = moved[:, c * LANES : (c + 1) * LANES]
                    for d in range(parts):
                        base = meta_ref[row, target[d]]
                        begin = meta_ref[row, parts + target[d]]
                        chunk = lax.shift_right_logical(base, 7)
                        off = lax.bitwise_and(base, LANES - 1)
                        turn = lax.bitwise_and(off - begin, LANES - 1)
                        at = lax.shift_right_logical(begin, 7)
                        at = at + jnp.where(off < lax.bitwise_and(begin, LANES - 1), 1, 0)
                        turned = [pltpu.roll(local[buffer, at + k], turn, 1) for k in range(chunks + 2)]
                        for k in range(chunks + 1):
                            value = jnp.where(lane >= turn, turned[k + 1], turned[k])
                            if k == 0:
                                value = jnp.where(lane >= off, value, lists[d, chunk])
                            lists[d, chunk + k] = value
            return carry

        lax.fori_loop(0, slots // ROWS, do_group, 0)
        for d in range(parts):
            count = meta_ref[slots * columns - 1, 2 * parts + target[d]]
            for c in range(total):
                out_refs[d][:, c * LANES : (c + 1) * LANES] = jnp.where(lane + c * LANES < count, lists[d, c], 0.0)

    return pl.pallas_call(
        kernel,
        out_shape=(jax.ShapeDtypeStruct((8, capacity), jnp.float32),) * parts,
        in_specs=[VMEM, VMEM, VMEM, SMEM, SMEM],
        out_specs=(VMEM,) * parts,
        scratch_shapes=[
            pltpu.VMEM((4, 2 * chunks + 4, ROWS, LANES), jnp.float32),
            pltpu.VMEM((parts, total + chunks + 2, ROWS, LANES), jnp.float32),
        ],
        compiler_params=PARAMS,
    )(motion, pressure, place, meta, here)


def in_order(here, received):
    parts = len(received)
    rows, capacity = received[0].shape

    def kernel(here_ref, *refs):
        out_ref = refs[parts]
        for k in range(parts):

            @pl.when(pl.program_id(0) == k)
            def _():
                out_ref[...] = refs[k][...]

    return pl.pallas_call(
        kernel,
        out_shape=jax.ShapeDtypeStruct((rows, parts * capacity), jnp.float32),
        grid_spec=pltpu.PrefetchScalarGridSpec(
            num_scalar_prefetch=1,
            grid=(parts,),
            in_specs=[VMEM] * parts,
            out_specs=pl.BlockSpec((rows, capacity), lambda k, here_ref: (0, lax.rem(here_ref[0] - k + parts, parts))),
        ),
        compiler_params=PARAMS,
    )(here, *received)


def pass_on(value, axis, step):
    count = lax.axis_size(axis)
    return lax.ppermute(value, axis, [(i, (i + step) % count) for i in range(count)])


def swap_ends(left_ends, right_ends):
    return pass_on(right_ends, "sub", 1), pass_on(left_ends, "sub", -1)


def swap_columns(parts_of):
    first = jnp.concatenate(parts_of(0), axis=0)
    final = jnp.concatenate(parts_of(-1), axis=0)
    return pass_on(final, "tile", 1), pass_on(first, "tile", -1)


def rows_of(fields):
    return fields.reshape(-1, fields.shape[-1])


def beside(ends, width):
    plane = jnp.concatenate(ends, axis=1)
    return jnp.pad(plane, ((0, 0), (0, width - plane.shape[1])))


def shards(offsets, velocity, mass, entropy, active_counts, targets):
    slots, columns, width = mass.shape
    levels = active_counts.shape[0]
    parts = lax.axis_size("sub")
    slot_index = lax.broadcasted_iota(jnp.int32, mass.shape, 0)
    mass_live = jnp.where(slot_index < active_counts[0][None], mass, 0.0)
    motion = jnp.concatenate([offsets, velocity, mass_live[None]], axis=0).transpose(2, 0, 1, 3)
    entropy = entropy.transpose(1, 0, 2)
    limits = (slots, slots // 2, slots // 4)
    pressure = None
    ends_m, ends_p, sizes_m, sizes_p = [], [], [], []
    left_m, right_m, left_p, right_p = [], [], [], []
    made = first_ends(motion)
    place, meta = ranks(targets.reshape(slots * columns, width), parts)
    for level in range(levels):
        limit = limits[level]
        sent = limits[max(level - 1, 0)]
        ends_m.insert(0, swap_ends(*made))
        partial, *inner_kept = own_part(DENSITY, motion, None, ends_m, [], limit, (0,), keep=KEEP[level][0])
        ends_m[0], partial = lax.optimization_barrier((ends_m[0], partial))
        plane = beside(ends_m[0], width)
        masses = (lambda c: [motion[c, 6]]) if level == 0 else (lambda c: [])
        cells = swap_columns(lambda c: [rows_of(motion[c, :3, :sent]), *masses(c), plane])
        sizes_m.insert(0, sent)
        left_m.insert(0, cells[0])
        right_m.insert(0, cells[1])
        partial, *outer_kept = own_part(DENSITY, motion, None, ends_m, [], limit, (-1, 1), partial, keep=KEEP[level][1])
        pressure, *made = density_rest(motion, partial, (left_m, right_m), sizes_m, pressure, entropy, active_counts, level, limit, limit, KEEP[level][2])
        rest_kept = made.pop() if KEEP[level][2] else None
        ends_p.insert(0, swap_ends(*made))
        (partial,) = own_part(FORCE, motion, pressure, ends_m, ends_p, limit, (0,), None, *inner_kept)
        ends_p[0], partial = lax.optimization_barrier((ends_p[0], partial))
        plane = beside(ends_p[0], width)
        cells = swap_columns(lambda c: [rows_of(pressure[c, :, :limit]), plane, rows_of(motion[c, 3:6, :sent])])
        sizes_p.insert(0, limit)
        left_p.insert(0, cells[0])
        right_p.insert(0, cells[1])
        (partial,) = own_part(FORCE, motion, pressure, ends_m, ends_p, limit, (-1, 1), partial, *outer_kept)
        more = limit if level < levels - 1 else 0
        motion, *made = force_rest(
            motion, pressure, partial, (left_m, right_m), (left_p, right_p), sizes_m, sizes_p, active_counts, level, limit, more, rest_kept
        )
    capacity = 3 * slots * columns * width // 8
    here = lax.axis_index("sub").astype(jnp.int32).reshape(1)
    lists = compact(motion, pressure, place, meta[:, : 3 * parts], here, parts, capacity)
    received = {0: lists[0]}
    for k in sorted(range(1, parts), key=lambda k: -min(k, parts - k)):
        received[k] = pass_on(lists[k], "sub", k)
    return in_order(here, [received[k] for k in range(parts)])


def solution(mesh):
    placed = (
        P(None, None, "tile", "sub"),
        P(None, None, "tile", "sub"),
        P(None, "tile", "sub"),
        P(None, "tile", "sub"),
        P(None, "tile", "sub"),
        P(None, "tile", "sub"),
    )
    return jax.shard_map(
        shards, mesh=mesh, in_specs=placed, out_specs=P(None, ("tile", "sub")), check_vma=False
    )
```
